32 devices in a mesh: batch: 4 (over x, core), seq: 8 (over z, y).
Axes of the slice: x: 2, y: 2, z: 4, core: 2. Of those that a mesh axis runs over, the one named last changes fastest.
Arguments:
- tokens: bfloat16 [4, 1024, 1600], P('batch', 'seq'), may hold values from -6 to 6
- ln1_gain: bfloat16 [1600], P('seq'), may hold values from 0.25 to 1.75
- ln1_bias: bfloat16 [1600], P('seq'), may hold values from -3 to 3
- qkv_weight: bfloat16 [1600, 4800], P('seq'), may hold values from -0.15625 to 0.15625
- qv_bias: bfloat16 [3200], P('seq'), may hold values from -3 to 3
- proj_weight: bfloat16 [1600, 1600], P('seq'), may hold values from -0.625 to 0.625
- proj_bias: bfloat16 [1600], P('seq'), may hold values from -3 to 3
- ln2_gain: bfloat16 [1600], P('seq'), may hold values from 0.25 to 1.75
- ln2_bias: bfloat16 [1600], P('seq'), may hold values from -3 to 3
- fc_weight: bfloat16 [1600, 6400], P('seq'), may hold values from -0.15625 to 0.15625
- fc_bias: bfloat16 [6400], P('seq'), may hold values from -3 to 3
- out_weight: bfloat16 [6400, 1600], P('seq'), may hold values from -0.078125 to 0.078125
- out_bias: bfloat16 [1600], P('seq'), may hold values from -3 to 3
- cotangent: bfloat16 [4, 1024, 1600], P('batch', 'seq'), may hold values from -6 to 6
Outputs:
- out: bfloat16 [4, 1024, 1600], P('batch', 'seq')
- input_grad: bfloat16 [4, 1024, 1600], P('batch', 'seq')
- ln1_gain_grad: float32 [1600], P('seq')
- ln1_bias_grad: float32 [1600], P('seq')
- qkv_weight_grad: float32 [1600, 4800], P('seq', 'batch')
- qv_bias_grad: float32 [3200], P('seq')
- proj_weight_grad: float32 [1600, 1600], P('seq', 'batch')
- proj_bias_grad: float32 [1600], P('seq')
- ln2_gain_grad: float32 [1600], P('seq')
- ln2_bias_grad: float32 [1600], P('seq')
- fc_weight_grad: float32 [1600, 6400], P('seq', 'batch')
- fc_bias_grad: float32 [6400], P('seq')
- out_weight_grad: float32 [6400, 1600], P('seq', 'batch')
- out_bias_grad: float32 [1600], P('seq')
The draws below stay inside these ranges and needn't reach their ends.
All inputs are finite; a program needn't handle non-finite values.
Results may differ from the reference program's by a relative error of at most 0.017.
Values may be sent and summed in bfloat16 or wider, within the bound.
No kernel may reach another device: no remote copies, remote signals or barrier semaphores. Data moves between devices by JAX's collectives and lax.ppermute only.
A program may use at most 384 MiB of HBM per device.

```python
import jax
import jax.numpy as jnp
from jax import lax

D = 1600
HEADS = 25
HEAD_DIM = 64
FF = 6400
LENGTH = 1024
SEQS_ALL = 4


def steps_of(rng, extent, shards, least, top_value):
    loudness = 1.0
    for dim, parts in shards:
        draws = jax.random.uniform(jax.random.fold_in(jax.random.fold_in(rng, 6), dim), (parts,), jnp.float32, least / len(shards), top_value / len(shards))
        loudness = loudness * jnp.repeat(jnp.exp(draws), extent[dim] // parts).reshape((-1,) + (1,) * (len(extent) - 1 - dim))
    return loudness


def scatter_about(rng, dims, width, bound, shards=(), kind=jnp.bfloat16):
    drawn = jax.random.normal(rng, dims, jnp.float32) * width
    if len(shards) > 0:
        drawn = steps_of(rng, dims, shards, -0.22, 0.18) * drawn
    return jnp.clip(drawn, min=-bound, max=bound).astype(kind)


def setup_inputs(seed: int = 0) -> dict:
    streams_of = jax.random.split(jax.random.key(seed), 15)
    tokens = scatter_about(streams_of[0], (SEQS_ALL, LENGTH, D), 1.0, 6.0, ((0, 4), (1, 8)))
    ln1_gain = jnp.clip(1.0 + 0.15 * jax.random.normal(streams_of[1], (D,), jnp.float32), 0.25, 1.75).astype(jnp.bfloat16)
    ln1_bias = scatter_about(streams_of[2], (D,), 0.5, 3.0, ((0, 8),))
    qkv_weight = scatter_about(streams_of[3], (D, 3 * D), D ** -0.5, 0.15625, ((0, 8),))
    qv_bias = scatter_about(streams_of[4], (2 * D,), 0.5, 3.0, ((0, 8),))
    proj_weight = scatter_about(streams_of[5], (D, D), (D // 16) ** -0.5, 0.625, ((0, 8),))
    proj_bias = scatter_about(streams_of[6], (D,), 0.5, 3.0, ((0, 8),))
    ln2_gain = jnp.clip(1.0 + 0.15 * jax.random.normal(streams_of[7], (D,), jnp.float32), 0.25, 1.75).astype(jnp.bfloat16)
    ln2_bias = scatter_about(streams_of[8], (D,), 0.5, 3.0, ((0, 8),))
    fc_weight = scatter_about(streams_of[9], (D, FF), D ** -0.5, 0.15625, ((0, 8),))
    fc_bias = scatter_about(streams_of[10], (FF,), 0.5, 3.0, ((0, 8),))
    out_weight = scatter_about(streams_of[11], (FF, D), FF ** -0.5, 0.078125, ((0, 8),))
    out_bias = scatter_about(streams_of[12], (D,), 0.5, 3.0, ((0, 8),))
    cotangent = scatter_about(streams_of[13], (SEQS_ALL, LENGTH, D), 1.0, 6.0, ((0, 4), (1, 8)))
    return {"tokens": tokens, "ln1_gain": ln1_gain, "ln1_bias": ln1_bias, "qkv_weight": qkv_weight, "qv_bias": qv_bias, "proj_weight": proj_weight, "proj_bias": proj_bias, "ln2_gain": ln2_gain, "ln2_bias": ln2_bias, "fc_weight": fc_weight, "fc_bias": fc_bias, "out_weight": out_weight, "out_bias": out_bias, "cotangent": cotangent}


EPSILON = 1e-05
FLOOR_SCORE = -1e+30

@jax.custom_vjp
def low(v):
    return lax.optimization_barrier(v.astype(jnp.bfloat16)).astype(jnp.float32)

@jax.custom_vjp
def low_back(v):
    return v

def low_keep(v):
    return (low(v), None)

def low_pass(kept, grad):
    return (grad,)

def back_keep(v):
    return (v, None)

def back_low(kept, grad):
    return (low(grad),)
low.defvjp(low_keep, low_pass)
low_back.defvjp(back_keep, back_low)

def matmul_high(left_side, right_side):
    return jnp.dot(left_side, right_side, precision=lax.Precision.HIGHEST)

def norm_rows(inputs, gain_full, shift_full):
    mean_rows = lax.optimization_barrier(jnp.mean(inputs, axis=-1, keepdims=True))
    centred = inputs - mean_rows
    variance = lax.optimization_barrier(jnp.mean(centred * centred, axis=-1, keepdims=True))
    return centred * lax.rsqrt(variance + EPSILON) * gain_full + shift_full

def gelu_tanh(inputs):
    return jax.nn.gelu(inputs, approximate=True)

def attend(query_all, key_all, value_all):
    seq_len = query_all.shape[0]
    block_len = min(512, seq_len)
    block_count = seq_len // block_len
    starts = jnp.arange(block_count, dtype=jnp.int32) * block_len
    blocks = query_all.reshape(block_count, block_len, HEADS, HEAD_DIM)
    key_pos = jnp.arange(seq_len, dtype=jnp.int32)
    score_scale = HEAD_DIM ** (-0.5)

    def one_block(block_pair):
        query_block, block_first = block_pair
        raw_scores = jnp.einsum('qhd,khd->hqk', query_block, key_all, precision=lax.Precision.HIGHEST) * score_scale
        raw_scores = low_back(raw_scores)
        query_pos = block_first + jnp.arange(block_len, dtype=jnp.int32)
        allowed = key_pos[None, :] <= query_pos[:, None]
        masked = jnp.where(allowed, raw_scores, FLOOR_SCORE)
        row_top = lax.optimization_barrier(jnp.max(masked, axis=-1, keepdims=True))
        expd = jnp.exp(masked - row_top)
        probs = expd / lax.optimization_barrier(jnp.sum(expd, axis=-1, keepdims=True))
        return jnp.einsum('hqk,khd->qhd', low(probs), value_all, precision=lax.Precision.HIGHEST)
    result = lax.map(jax.checkpoint(one_block), (blocks, starts))
    return result.reshape(seq_len, HEADS * HEAD_DIM)

def block_forward(inputs, params):
    gain_one, shift_one, qkv_weight, qv_bias, proj_weight, proj_bias, gain_two, shift_two, fc_weight, fc_bias, out_weight, out_bias = params
    model_width = inputs.shape[1]
    normed_one = low(norm_rows(inputs, gain_one, shift_one))
    bias_full = jnp.concatenate([qv_bias[:model_width], jnp.zeros((model_width,), jnp.float32), qv_bias[model_width:]])
    projected = low(low_back(matmul_high(normed_one, qkv_weight)) + bias_full)
    query_all = projected[:, :model_width].reshape(-1, HEADS, HEAD_DIM)
    key_all = projected[:, model_width:2 * model_width].reshape(-1, HEADS, HEAD_DIM)
    value_all = projected[:, 2 * model_width:].reshape(-1, HEADS, HEAD_DIM)
    attended = low(low_back(attend(query_all, key_all, value_all)))
    mixed_rows = inputs + low_back(matmul_high(attended, proj_weight)) + proj_bias
    normed_two = low(norm_rows(mixed_rows, gain_two, shift_two))
    hidden = low_back(matmul_high(normed_two, fc_weight)) + fc_bias
    activated = low(gelu_tanh(hidden))
    return mixed_rows + matmul_high(activated, out_weight) + out_bias

def reference(tokens, ln1_gain, ln1_bias, qkv_weight, qv_bias, proj_weight, proj_bias, ln2_gain, ln2_bias, fc_weight, fc_bias, out_weight, out_bias, cotangent):
    params = tuple((weight_item.astype(jnp.float32) for weight_item in (ln1_gain, ln1_bias, qkv_weight, qv_bias, proj_weight, proj_bias, ln2_gain, ln2_bias, fc_weight, fc_bias, out_weight, out_bias)))

    def one_sequence(totals, seq_pair):
        seq_tokens, seq_grad = seq_pair
        result, pull_back = jax.vjp(block_forward, seq_tokens.astype(jnp.float32), params)
        grad_parts = pull_back(seq_grad.astype(jnp.float32))
        totals = jax.tree.map(lambda first_term, second_term: first_term + second_term, totals, grad_parts[1])
        return (totals, (result.astype(jnp.bfloat16), grad_parts[0].astype(jnp.bfloat16)))
    start_totals = tuple((jnp.zeros_like(weight_item) for weight_item in params))
    totals, outputs = lax.scan(one_sequence, start_totals, (tokens, cotangent))
    return (outputs[0], outputs[1], totals[0], totals[1], totals[2], totals[3], totals[4], totals[5], totals[6], totals[7], totals[8], totals[9], totals[10], totals[11])
```

```python
import functools

import jax
import jax.numpy as jnp
from jax import lax
from jax.experimental import pallas as pl
from jax.experimental.pallas import tpu as pltpu
from jax.sharding import PartitionSpec as P

HEAD_DIM = 64
HEAD_COLS = 3 * HEAD_DIM
EPSILON = 1e-05
FLOOR_SCORE = -1e30
SCALE = HEAD_DIM**-0.5
BF = jnp.bfloat16
F32 = jnp.float32


def dot_nn(a, b):
    return lax.dot_general(a, b, (((1,), (0,)), ((), ())), preferred_element_type=F32)


def dot_nt(a, b):
    return lax.dot_general(a, b, (((1,), (1,)), ((), ())), preferred_element_type=F32)


def dot_tn(a, b):
    return lax.dot_general(a, b, (((0,), (0,)), ((), ())), preferred_element_type=F32)


def steps(count, unrolled, body, carry):
    if unrolled:
        for j in range(count):
            carry = body(j, carry)
        return carry
    return lax.fori_loop(0, count, body, carry)


def rows_of(index, size):
    if isinstance(index, int):
        return pl.ds(index * size, size)
    return pl.ds(pl.multiple_of(index * size, size), size)


def causal(tile):
    key_pos = lax.broadcasted_iota(jnp.int32, (tile, tile), 0)
    query_pos = lax.broadcasted_iota(jnp.int32, (tile, tile), 1)
    return key_pos <= query_pos


def forward_kernel(tile, unrolled, x_ref, low_ref, full_ref, log_ref, value_t):
    tiles = x_ref.shape[0] // tile
    for head in range(2):
        base = head * HEAD_COLS
        k_cols = pl.ds(base + HEAD_DIM, HEAD_DIM)
        out_cols = pl.ds(head * HEAD_DIM, HEAD_DIM)

        def turn(j, carry):
            value_t[j] = x_ref[rows_of(j, tile), pl.ds(base + 2 * HEAD_DIM, HEAD_DIM)].T
            return carry

        steps(tiles, unrolled, turn, 0)

        def query_tile(i, carry):
            rows = rows_of(i, tile)
            query = x_ref[rows, pl.ds(base, HEAD_DIM)] * jnp.asarray(SCALE, BF)

            def add(j, state, masked):
                top, total, acc = state
                scores = dot_nt(x_ref[rows_of(j, tile), k_cols], query)
                if masked:
                    scores = jnp.where(causal(tile), scores, FLOOR_SCORE)
                new_top = jnp.maximum(top, jnp.max(scores, axis=0, keepdims=True))
                probs = jnp.exp(scores - new_top)
                fade = jnp.exp(top - new_top)
                total = total * fade + jnp.sum(probs, axis=0, keepdims=True)
                acc = acc * fade + dot_nn(value_t[j], probs.astype(BF))
                return new_top, total, acc

            state = (
                jnp.full((1, tile), FLOOR_SCORE, F32),
                jnp.zeros((1, tile), F32),
                jnp.zeros((HEAD_DIM, tile), F32),
            )
            state = steps(i, unrolled, lambda j, s: add(j, s, False), state)
            top, total, acc = add(i, state, True)
            result = (acc / total).T
            low_ref[rows, out_cols] = result.astype(BF)
            full_ref[rows, out_cols] = result
            log_ref[0, pl.ds(head, 1), rows] = top + jnp.log(total)
            return carry

        steps(tiles, unrolled, query_tile, 0)


def backward_kernel(
    tile, unrolled, x_ref, grad_ref, full_ref, log_ref, dx_ref, sum_ref, key_t, key_acc, value_acc
):
    tiles = x_ref.shape[0] // tile
    for head in range(2):
        base = head * HEAD_COLS
        q_cols = pl.ds(base, HEAD_DIM)
        k_cols = pl.ds(base + HEAD_DIM, HEAD_DIM)
        v_cols = pl.ds(base + 2 * HEAD_DIM, HEAD_DIM)
        out_cols = pl.ds(head * HEAD_DIM, HEAD_DIM)

        def turn(j, carry):
            key_t[j] = x_ref[rows_of(j, tile), k_cols].T
            return carry

        steps(tiles, unrolled, turn, 0)
        key_acc[...] = jnp.zeros_like(key_acc)
        value_acc[...] = jnp.zeros_like(value_acc)

        def query_tile(i, query_sum):
            rows = rows_of(i, tile)
            query = x_ref[rows, q_cols] * jnp.asarray(SCALE, BF)
            grad = grad_ref[rows, out_cols]
            delta = jnp.sum((grad.astype(F32) * full_ref[rows, out_cols]).T, axis=0, keepdims=True)
            log_row = log_ref[0, pl.ds(head, 1), rows]

            def add(j, acc, masked):
                key_rows = rows_of(j, tile)
                scores = dot_nt(x_ref[key_rows, k_cols], query)
                probs = jnp.exp(scores - log_row)
                if masked:
                    probs = jnp.where(causal(tile), probs, 0.0)
                grad_probs = dot_nt(x_ref[key_rows, v_cols], grad)
                grad_scores = (probs * (grad_probs - delta)).astype(BF)
                value_acc[key_rows, :] += dot_nn(probs.astype(BF), grad)
                key_acc[key_rows, :] += dot_nn(grad_scores, query)
                return acc + dot_nn(key_t[j], grad_scores)

            acc = jnp.zeros((HEAD_DIM, tile), F32)
            acc = steps(i, unrolled, lambda j, s: add(j, s, False), acc)
            acc = add(i, acc, True)
            result = acc.T * SCALE
            dx_ref[rows, q_cols] = result.astype(BF)
            return query_sum + jnp.sum(result, axis=0, keepdims=True)

        query_sum = steps(tiles, unrolled, query_tile, jnp.zeros((1, HEAD_DIM), F32))
        dx_ref[:, k_cols] = key_acc[...].astype(BF)
        dx_ref[:, v_cols] = value_acc[...].astype(BF)
        sum_ref[0, :, q_cols] = query_sum
        sum_ref[0, :, k_cols] = jnp.sum(key_acc[...], axis=0, keepdims=True)
        sum_ref[0, :, v_cols] = jnp.sum(value_acc[...], axis=0, keepdims=True)


def attention_tile(length):
    return min(256, length)


def attention_forward(projected, heads):
    length = projected.shape[0]
    tile = attention_tile(length)
    tiles = length // tile
    pairs = heads // 2
    return pl.pallas_call(
        functools.partial(forward_kernel, tile, tiles <= 4),
        grid=(pairs,),
        in_specs=[pl.BlockSpec((length, 2 * HEAD_COLS), lambda g: (0, g))],
        out_specs=[
            pl.BlockSpec((length, 2 * HEAD_DIM), lambda g: (0, g)),
            pl.BlockSpec((length, 2 * HEAD_DIM), lambda g: (0, g)),
            pl.BlockSpec((1, 2, length), lambda g: (g, 0, 0)),
        ],
        out_shape=[
            jax.ShapeDtypeStruct((length, heads * HEAD_DIM), BF),
            jax.ShapeDtypeStruct((length, heads * HEAD_DIM), F32),
            jax.ShapeDtypeStruct((pairs, 2, length), F32),
        ],
        scratch_shapes=[pltpu.VMEM((tiles, HEAD_DIM, tile), BF)],
        compiler_params=pltpu.CompilerParams(vmem_limit_bytes=48 << 20),
        cost_estimate=pl.CostEstimate(
            flops=4 * length * length * heads * HEAD_DIM,
            bytes_accessed=length * heads * HEAD_DIM * 12,
            transcendentals=length * length * heads // 2,
        ),
        name="attention_forward",
    )(projected)


def attention_backward(projected, grad, full, logs, heads):
    length = projected.shape[0]
    tile = attention_tile(length)
    tiles = length // tile
    pairs = heads // 2
    return pl.pallas_call(
        functools.partial(backward_kernel, tile, tiles <= 4),
        grid=(pairs,),
        in_specs=[
            pl.BlockSpec((length, 2 * HEAD_COLS), lambda g: (0, g)),
            pl.BlockSpec((length, 2 * HEAD_DIM), lambda g: (0, g)),
            pl.BlockSpec((length, 2 * HEAD_DIM), lambda g: (0, g)),
            pl.BlockSpec((1, 2, length), lambda g: (g, 0, 0)),
        ],
        out_specs=[
            pl.BlockSpec((length, 2 * HEAD_COLS), lambda g: (0, g)),
            pl.BlockSpec((1, 1, 2 * HEAD_COLS), lambda g: (g, 0, 0)),
        ],
        out_shape=[
            jax.ShapeDtypeStruct((length, heads * HEAD_COLS), BF),
            jax.ShapeDtypeStruct((pairs, 1, 2 * HEAD_COLS), F32),
        ],
        scratch_shapes=[
            pltpu.VMEM((tiles, HEAD_DIM, tile), BF),
            pltpu.VMEM((length, HEAD_DIM), F32),
            pltpu.VMEM((length, HEAD_DIM), F32),
        ],
        compiler_params=pltpu.CompilerParams(vmem_limit_bytes=48 << 20),
        cost_estimate=pl.CostEstimate(
            flops=10 * length * length * heads * HEAD_DIM,
            bytes_accessed=length * heads * HEAD_DIM * 20,
            transcendentals=length * length * heads // 2,
        ),
        name="attention_backward",
    )(projected, grad, full, logs)


def norm_stats(rows):
    mean = jnp.mean(rows, axis=-1, keepdims=True)
    centred = rows - mean
    variance = jnp.mean(centred * centred, axis=-1, keepdims=True)
    inverse = lax.rsqrt(variance + EPSILON)
    return centred * inverse, inverse


def norm_back(grad, xhat, inverse, gain):
    h = grad * gain
    return inverse * (
        h - jnp.mean(h, axis=-1, keepdims=True) - xhat * jnp.mean(h * xhat, axis=-1, keepdims=True)
    )


def gelu_both(hidden):
    activated, pull = jax.vjp(lambda v: jax.nn.gelu(v, approximate=True), hidden)
    return activated, pull(jnp.ones_like(hidden))[0]


def gather(value, axis="seq", dim=0):
    return lax.all_gather(value, axis, axis=dim, tiled=True)


def scatter_sum(value, axis="seq", dim=0):
    return lax.psum_scatter(value, axis, scatter_dimension=dim, tiled=True)


def exchange(value, split, concat, axis="seq"):
    return lax.all_to_all(value, axis, split, concat, tiled=True)


def per_device(
    shards,
    batches,
    tokens,
    ln1_gain,
    ln1_bias,
    qkv_weight,
    qv_bias,
    proj_weight,
    proj_bias,
    ln2_gain,
    ln2_bias,
    fc_weight,
    fc_bias,
    out_weight,
    out_bias,
    cotangent,
):
    _, span, width = tokens.shape
    length = span * shards
    head_count = width // HEAD_DIM
    heads = -(-head_count // shards)
    heads += heads % 2
    padded = heads * shards
    hidden_width = fc_bias.shape[0]
    me = lax.axis_index("seq")

    own_tokens = tokens[0]
    own_cot = cotangent[0]
    all_tokens = gather(own_tokens)

    small = jnp.concatenate(
        [ln1_gain, ln1_bias, qv_bias, proj_bias, ln2_gain, ln2_bias, out_bias]
    )
    part = width // shards
    small_all = gather(small.reshape(1, -1))
    gain_one = small_all[:, :part].reshape(width).astype(F32)
    shift_one = small_all[:, part : 2 * part].reshape(width).astype(F32)
    bias_qv = small_all[:, 2 * part : 4 * part].reshape(2 * width)
    b_proj = small_all[:, 4 * part : 5 * part].reshape(width).astype(F32)
    gain_two = small_all[:, 5 * part : 6 * part].reshape(width).astype(F32)
    shift_two = small_all[:, 6 * part : 7 * part].reshape(width).astype(F32)
    b_out = small_all[:, 7 * part : 8 * part].reshape(width).astype(F32)

    def by_head(rows):
        count = rows.shape[0]
        rows = rows.reshape(count, 3, head_count, HEAD_DIM)
        rows = jnp.pad(rows, ((0, 0), (0, 0), (0, padded - head_count), (0, 0)))
        return jnp.swapaxes(rows, 1, 2).reshape(count, padded * HEAD_COLS)

    w_qkv = exchange(by_head(qkv_weight), 1, 0)
    w_fc = exchange(fc_weight, 1, 0)
    w_proj = gather(proj_weight)
    all_cot = gather(own_cot)
    bias_row = jnp.concatenate([bias_qv[:width], jnp.zeros((width,), BF), bias_qv[width:]])
    slice_cols = heads * HEAD_COLS
    bias_slice = lax.dynamic_slice_in_dim(
        by_head(bias_row.reshape(1, -1)), me * slice_cols, slice_cols, 1
    ).astype(F32)

    xhat_all, _ = norm_stats(all_tokens.astype(F32))
    normed_one = (xhat_all * gain_one + shift_one).astype(BF)
    projected = (dot_nn(normed_one, w_qkv) + bias_slice).astype(BF)
    attended_heads, attended_full, log_total = attention_forward(projected, heads)
    attn_low = exchange(attended_heads, 0, 1)[:, :width]

    inputs = own_tokens.astype(F32)
    mixed = inputs + dot_nn(attn_low, w_proj) + b_proj
    xhat_two, inverse_two = norm_stats(mixed)
    normed_two = gather((xhat_two * gain_two + shift_two).astype(BF))
    hidden = dot_nn(normed_two, w_fc) + fc_bias.astype(F32)
    activated, gelu_slope = gelu_both(hidden)
    activated = activated.astype(BF)
    out_part = scatter_sum(dot_nn(activated, out_weight).astype(BF))
    block_out = (mixed + out_part.astype(F32) + b_out).astype(BF)

    grad_hidden = dot_nt(all_cot, out_weight) * gelu_slope
    fc_bias_grad = jnp.sum(grad_hidden, axis=0)
    hidden_low = grad_hidden.astype(BF)
    g_two = scatter_sum(dot_nt(hidden_low, w_fc).astype(BF)).astype(F32)
    out_grad = dot_tn(activated, all_cot).astype(BF)
    fc_grad = dot_tn(normed_two, hidden_low).astype(BF)
    cot_full = own_cot.astype(F32)
    gain_two_grad = jnp.sum(g_two * xhat_two, axis=0)
    shift_two_grad = jnp.sum(g_two, axis=0)
    grad_mixed = cot_full + norm_back(g_two, xhat_two, inverse_two, gain_two)
    mixed_low = grad_mixed.astype(BF)

    grad_attn = dot_nt(mixed_low, w_proj).astype(BF)
    grad_attn = jnp.pad(grad_attn, ((0, 0), (0, padded * HEAD_DIM - width)))
    grad_heads = exchange(grad_attn, 1, 0)
    proj_grad = dot_tn(attn_low, mixed_low).astype(BF)
    grad_projected, column_sums = attention_backward(
        projected, grad_heads, attended_full, log_total, heads
    )
    g_one = scatter_sum(dot_nt(grad_projected, w_qkv).astype(BF)).astype(F32)
    qkv_grad = dot_tn(normed_one, grad_projected).astype(BF)
    xhat_one, inverse_one = norm_stats(inputs)
    gain_one_grad = jnp.sum(g_one * xhat_one, axis=0)
    shift_one_grad = jnp.sum(g_one, axis=0)
    grad_first = norm_back(g_one, xhat_one, inverse_one, gain_one)
    input_grad = (grad_mixed + grad_first).astype(BF)

    def from_heads(rows):
        count = rows.shape[0]
        rows = rows.reshape(count, padded, 3, HEAD_DIM)[:, :head_count]
        return jnp.swapaxes(rows, 1, 2).reshape(count, 3 * width)

    qkv_share = scatter_sum(from_heads(exchange(qkv_grad, 0, 1)), "batch", 1).astype(F32)
    fc_share = scatter_sum(exchange(fc_grad, 0, 1), "batch", 1).astype(F32)
    out_share = scatter_sum(out_grad, "batch", 1).astype(F32)
    proj_share = scatter_sum(scatter_sum(proj_grad), "batch", 1).astype(F32)

    head_sums = jnp.zeros((padded * HEAD_COLS,), F32)
    head_sums = lax.dynamic_update_slice_in_dim(
        head_sums, column_sums.reshape(-1), me * slice_cols, 0
    )
    qkv_sums = from_heads(head_sums.reshape(1, -1))[0]
    qv_sums = jnp.concatenate([qkv_sums[:width], qkv_sums[2 * width :]])
    vectors = [
        gain_one_grad,
        shift_one_grad,
        qv_sums,
        jnp.sum(grad_mixed, axis=0),
        gain_two_grad,
        shift_two_grad,
        jnp.sum(cot_full, axis=0),
    ]
    table = jnp.concatenate([v.reshape(shards, -1) for v in vectors], axis=1)
    own = scatter_sum(table.reshape(-1))
    sums = lax.psum(jnp.concatenate([own, fc_bias_grad]), "batch")
    return (
        block_out[None],
        input_grad[None],
        sums[:part],
        sums[part : 2 * part],
        qkv_share,
        sums[2 * part : 4 * part],
        proj_share,
        sums[4 * part : 5 * part],
        sums[5 * part : 6 * part],
        sums[6 * part : 7 * part],
        fc_share,
        sums[8 * part : 8 * part + hidden_width],
        out_share,
        sums[7 * part : 8 * part],
    )


def solution(mesh):
    rows = P("batch", "seq", None)
    matrix, vector = P("seq", None), P("seq")
    shared = P("seq", "batch")
    return jax.shard_map(
        functools.partial(per_device, mesh.shape["seq"], mesh.shape["batch"]),
        mesh=mesh,
        in_specs=(
            rows, vector, vector, matrix, vector, matrix, vector,
            vector, vector, matrix, vector, matrix, vector, rows,
        ),
        out_specs=(
            rows, rows, vector, vector, shared, vector, shared,
            vector, vector, vector, shared, vector, shared, vector,
        ),
        check_vma=False,
    )
```

```python
import functools

import jax
import jax.numpy as jnp
from jax import lax
from jax.experimental import pallas as pl
from jax.experimental.pallas import tpu as pltpu
from jax.sharding import PartitionSpec as P

HEAD_DIM = 64
HEAD_COLS = 3 * HEAD_DIM
EPSILON = 1e-05
FLOOR_SCORE = -1e30
SCALE = HEAD_DIM**-0.5
BF = jnp.bfloat16
F32 = jnp.float32
VMEM_LIMIT = 56 << 20
COST = 1.6e8


def dot_nn(a, b):
    return lax.dot_general(a, b, (((1,), (0,)), ((), ())), preferred_element_type=F32)


def dot_nt(a, b):
    return lax.dot_general(a, b, (((1,), (1,)), ((), ())), preferred_element_type=F32)


def dot_tn(a, b):
    return lax.dot_general(a, b, (((0,), (0,)), ((), ())), preferred_element_type=F32)


def shape_of(dims, kind):
    return jax.ShapeDtypeStruct(dims, kind)


def whole(*dims):
    return pl.BlockSpec(dims, lambda *_: (0,) * len(dims))


def call(
    kernel, table, operands, outs, scratch=(), name=None, us=1, in_specs=None, out_specs=None, grid=(1,), wait=()
):
    count, wait = 1 + len(operands), jax.tree.leaves(wait)

    def body(*refs):
        kernel(*refs[:count], *refs[count + len(wait) :])

    return pl.pallas_call(
        body,
        grid_spec=pltpu.PrefetchScalarGridSpec(
            num_scalar_prefetch=1,
            grid=grid,
            in_specs=(in_specs or [whole(*a.shape) for a in operands])
            + [pl.BlockSpec(memory_space=pl.ANY)] * len(wait),
            out_specs=out_specs or [whole(*o.shape) for o in outs],
            scratch_shapes=list(scratch),
        ),
        out_shape=list(outs),
        compiler_params=pltpu.CompilerParams(vmem_limit_bytes=VMEM_LIMIT),
        cost_estimate=pl.CostEstimate(flops=int(us * COST), bytes_accessed=1 << 16, transcendentals=0),
        name=name,
    )(table, *operands, *wait)


def steps(count, unrolled, body, carry):
    if unrolled:
        for j in range(count):
            carry = body(j, carry)
        return carry
    return lax.fori_loop(0, count, body, carry)


def rows_of(index, size):
    if isinstance(index, int):
        return pl.ds(index * size, size)
    return pl.ds(pl.multiple_of(index * size, size), size)


def causal(tile):
    key_pos = lax.broadcasted_iota(jnp.int32, (tile, tile), 0)
    query_pos = lax.broadcasted_iota(jnp.int32, (tile, tile), 1)
    return key_pos <= query_pos


def forward_kernel(tile, unrolled, table, x_ref, low_ref, full_ref, log_ref, value_t):
    tiles = x_ref.shape[0] // tile
    for head in range(2):
        base = head * HEAD_COLS
        k_cols = pl.ds(base + HEAD_DIM, HEAD_DIM)
        out_cols = pl.ds(head * HEAD_DIM, HEAD_DIM)

        def turn(j, carry):
            value_t[j] = x_ref[rows_of(j, tile), pl.ds(base + 2 * HEAD_DIM, HEAD_DIM)].T
            return carry

        steps(tiles, unrolled, turn, 0)

        def query_tile(i, carry):
            rows = rows_of(i, tile)
            query = x_ref[rows, pl.ds(base, HEAD_DIM)] * jnp.asarray(SCALE, BF)

            def add(j, state, masked):
                top, total, acc = state
                scores = dot_nt(x_ref[rows_of(j, tile), k_cols], query)
                if masked:
                    scores = jnp.where(causal(tile), scores, FLOOR_SCORE)
                new_top = jnp.maximum(top, jnp.max(scores, axis=0, keepdims=True))
                probs = jnp.exp(scores - new_top)
                fade = jnp.exp(top - new_top)
                total = total * fade + jnp.sum(probs, axis=0, keepdims=True)
                acc = acc * fade + dot_nn(value_t[j], probs.astype(BF))
                return new_top, total, acc

            state = (
                jnp.full((1, tile), FLOOR_SCORE, F32),
                jnp.zeros((1, tile), F32),
                jnp.zeros((HEAD_DIM, tile), F32),
            )
            state = steps(i, unrolled, lambda j, s: add(j, s, False), state)
            top, total, acc = add(i, state, True)
            result = (acc / total).T
            low_ref[rows, out_cols] = result.astype(BF)
            full_ref[rows, out_cols] = result
            log_ref[0, pl.ds(head, 1), rows] = top + jnp.log(total)
            return carry

        steps(tiles, unrolled, query_tile, 0)


def backward_kernel(
    tile, unrolled, table, x_ref, grad_ref, full_ref, log_ref, dx_ref, sum_ref, key_t, key_acc, value_acc
):
    tiles = x_ref.shape[0] // tile
    for head in range(2):
        base = head * HEAD_COLS
        q_cols = pl.ds(base, HEAD_DIM)
        k_cols = pl.ds(base + HEAD_DIM, HEAD_DIM)
        v_cols = pl.ds(base + 2 * HEAD_DIM, HEAD_DIM)
        out_cols = pl.ds(head * HEAD_DIM, HEAD_DIM)

        def turn(j, carry):
            key_t[j] = x_ref[rows_of(j, tile), k_cols].T
            return carry

        steps(tiles, unrolled, turn, 0)
        key_acc[...] = jnp.zeros_like(key_acc)
        value_acc[...] = jnp.zeros_like(value_acc)

        def query_tile(i, query_sum):
            rows = rows_of(i, tile)
            query = x_ref[rows, q_cols] * jnp.asarray(SCALE, BF)
            grad = grad_ref[rows, out_cols]
            delta = jnp.sum((grad.astype(F32) * full_ref[rows, out_cols]).T, axis=0, keepdims=True)
            log_row = log_ref[0, pl.ds(head, 1), rows]

            def add(j, acc, masked):
                key_rows = rows_of(j, tile)
                scores = dot_nt(x_ref[key_rows, k_cols], query)
                probs = jnp.exp(scores - log_row)
                if masked:
                    probs = jnp.where(causal(tile), probs, 0.0)
                grad_probs = dot_nt(x_ref[key_rows, v_cols], grad)
                grad_scores = (probs * (grad_probs - delta)).astype(BF)
                value_acc[key_rows, :] += dot_nn(probs.astype(BF), grad)
                key_acc[key_rows, :] += dot_nn(grad_scores, query)
                return acc + dot_nn(key_t[j], grad_scores)

            acc = jnp.zeros((HEAD_DIM, tile), F32)
            acc = steps(i, unrolled, lambda j, s: add(j, s, False), acc)
            acc = add(i, acc, True)
            result = acc.T * SCALE
            dx_ref[rows, q_cols] = result.astype(BF)
            return query_sum + jnp.sum(result, axis=0, keepdims=True)

        query_sum = steps(tiles, unrolled, query_tile, jnp.zeros((1, HEAD_DIM), F32))
        dx_ref[:, k_cols] = key_acc[...].astype(BF)
        dx_ref[:, v_cols] = value_acc[...].astype(BF)
        sum_ref[0, :, q_cols] = query_sum
        sum_ref[0, :, k_cols] = jnp.sum(key_acc[...], axis=0, keepdims=True)
        sum_ref[0, :, v_cols] = jnp.sum(value_acc[...], axis=0, keepdims=True)


def attention_forward(projected, table, heads):
    length = projected.shape[0]
    tile = min(256, length)
    tiles, pairs = length // tile, heads // 2
    wide, narrow = 2 * HEAD_COLS, 2 * HEAD_DIM
    columns = lambda g, t: (0, g)
    return call(
        functools.partial(forward_kernel, tile, tiles <= 4),
        table,
        [projected],
        [
            shape_of((length, heads * HEAD_DIM), BF),
            shape_of((length, heads * HEAD_DIM), F32),
            shape_of((pairs, 2, length), F32),
        ],
        grid=(pairs,),
        in_specs=[pl.BlockSpec((length, wide), columns)],
        out_specs=[
            pl.BlockSpec((length, narrow), columns),
            pl.BlockSpec((length, narrow), columns),
            pl.BlockSpec((1, 2, length), lambda g, t: (g, 0, 0)),
        ],
        scratch=[pltpu.VMEM((tiles, HEAD_DIM, tile), BF)],
        us=15,
        name="attention_forward",
    )


def attention_backward(projected, grads, full, logs, table, heads, wait):
    length = projected.shape[0]
    tile = min(256, length)
    tiles, pairs = length // tile, heads // 2
    wide, narrow = 2 * HEAD_COLS, 2 * HEAD_DIM
    columns = lambda g, t: (0, g)
    return call(
        functools.partial(backward_kernel, tile, tiles <= 4),
        table,
        [projected, grads, full, logs],
        [shape_of((length, heads * HEAD_COLS), BF), shape_of((pairs, 1, wide), F32)],
        grid=(pairs,),
        in_specs=[
            pl.BlockSpec((length, wide), columns),
            pl.BlockSpec((length, narrow), columns),
            pl.BlockSpec((length, narrow), columns),
            pl.BlockSpec((1, 2, length), lambda g, t: (g, 0, 0)),
        ],
        out_specs=[
            pl.BlockSpec((length, wide), columns),
            pl.BlockSpec((1, 1, wide), lambda g, t: (g, 0, 0)),
        ],
        scratch=[
            pltpu.VMEM((tiles, HEAD_DIM, tile), BF),
            pltpu.VMEM((length, HEAD_DIM), F32),
            pltpu.VMEM((length, HEAD_DIM), F32),
        ],
        us=14,
        wait=wait,
        name="attention_backward",
    )


def norm_stats(rows):
    mean = jnp.mean(rows, axis=-1, keepdims=True)
    centred = rows - mean
    variance = jnp.mean(centred * centred, axis=-1, keepdims=True)
    inverse = lax.rsqrt(variance + EPSILON)
    return centred * inverse, inverse


def norm_back(grad, xhat, inverse, gain):
    h = grad * gain
    return inverse * (
        h - jnp.mean(h, axis=-1, keepdims=True) - xhat * jnp.mean(h * xhat, axis=-1, keepdims=True)
    )


ROOT = 0.7978845608028654
CUBE = 0.044715


def gelu_both(hidden):
    square = hidden * hidden
    bent = jnp.tanh(ROOT * hidden * (1.0 + CUBE * square))
    half = 0.5 * (1.0 + bent)
    slope = half + 0.5 * hidden * (1.0 - bent * bent) * ROOT * (1.0 + 3.0 * CUBE * square)
    return hidden * half, slope


def project_kernel(table, gain, shift, bias, weight, tokens, normed, projected, kept):
    length = tokens.shape[0]
    chunk = min(256, length)
    for first in range(0, length, chunk):
        rows = slice(first, first + chunk)
        xhat, _ = norm_stats(tokens[rows, :].astype(F32))
        kept[rows, :] = xhat.astype(BF)
        normed[rows, :] = (xhat * gain[...] + shift[...]).astype(BF)
        projected[rows, :] = (dot_nn(normed[rows, :], weight[...]) + bias[...]).astype(BF)


def unproject_kernel(shards, table, grad, weight, xhat, *refs):
    others, blocks, (sums, rows) = refs[:shards], refs[shards : 2 * shards], refs[2 * shards :]
    length = rows.shape[0]
    span, chunk = length // shards, min(256, length)
    sums[...] = jnp.zeros_like(sums)
    for first in range(0, length, chunk):
        share = dot_nt(grad[first : first + chunk, :], weight[...])
        rows[first : first + chunk, :] = share.astype(BF)
        sums[0:1, :] += jnp.sum(share * xhat[first : first + chunk, :].astype(F32), axis=0, keepdims=True)
        sums[1:2, :] += jnp.sum(share, axis=0, keepdims=True)
    for r in range(shards):
        blocks[r][:span, :] = rows[rows_of(table[r], span), :]
        blocks[r][span:, :] = others[r][...]


def mix_kernel(shards, table, tokens, weight, bias, gain, shift, heads, attended, mixed, normed, spread):
    cols, width = heads.shape[2], attended.shape[1]
    for s in range(shards):
        spread[:, s * cols : (s + 1) * cols] = heads[s]
    attended[...] = spread[:, :width]
    mixed[...] = tokens[...].astype(F32) + dot_nn(attended[...], weight[...]) + bias[...]
    xhat, _ = norm_stats(mixed[...])
    normed[...] = (xhat * gain[...] + shift[...]).astype(BF)


def unmix_kernel(shards, table, first, second, third, mixed, cotangent, weight, gain, *refs):
    grad_mixed, low, sums, pieces, spread = refs
    cols, (span, width) = pieces.shape[2], low.shape
    grad = first[...].astype(F32) + second[...].astype(F32) + third[...].astype(F32)
    xhat, inverse = norm_stats(mixed[...])
    full = cotangent[...].astype(F32) + norm_back(grad, xhat, inverse, gain[...])
    grad_mixed[...] = full
    low[...] = full.astype(BF)
    sums[0:1, :] = jnp.sum(grad * xhat, axis=0, keepdims=True)
    sums[1:2, :] = jnp.sum(grad, axis=0, keepdims=True)
    sums[2:3, :] = jnp.sum(full, axis=0, keepdims=True)
    spread[:, width:] = jnp.zeros_like(spread[:, width:])
    spread[:, :width] = dot_nt(low[...], weight[...]).astype(BF)
    for s in range(shards):
        pieces[s] = spread[:, s * cols : (s + 1) * cols]


def mlp_kernel(shards, group, table, fc, bias, out, *refs):
    blocks, cotangents, refs = refs[:shards], refs[shards : shards + group], refs[shards + group :]
    act, low, cots, sums, shares, results, normed = refs
    step = pl.program_id(0)
    span = blocks[0].shape[0]
    for first in range(0, shards, group):

        @pl.when(step == first // group)
        def _(first=first):
            for i in range(group):
                normed[i * span : (i + 1) * span, :] = blocks[first + i][...]

    for i in range(group):
        cots[i * span : (i + 1) * span, :] = cotangents[i][0]
    hidden = dot_nn(normed[...], fc[...]) + bias[...]
    activated, slope = gelu_both(hidden)
    act[...] = activated.astype(BF)
    grad = dot_nt(cots[...], out[...]) * slope
    total = jnp.sum(grad, axis=0, keepdims=True)

    @pl.when(step == 0)
    def _():
        sums[...] = total

    @pl.when(step > 0)
    def _():
        sums[...] += total

    low[...] = grad.astype(BF)
    share = dot_nt(low[...], fc[...]).astype(BF)
    result = dot_nn(act[...], out[...]).astype(BF)
    for i in range(group):
        shares[i] = share[i * span : (i + 1) * span, :]
        results[i] = result[i * span : (i + 1) * span, :]


def mlp_part(blocks, cotangent, fc, bias, out, table):
    shards = len(blocks)
    span, width = blocks[0].shape
    rows, units = shards * span, fc.shape[1]
    group = min(shards, max(1, 512 // span))
    cotangent = cotangent.reshape(shards, span, width)
    own = lambda i: pl.BlockSpec((1, span, width), lambda g, t: (t[g * group + i], 0, 0))
    rows_at = lambda cols: pl.BlockSpec((group * span, cols), lambda g, t: (g, 0))
    return call(
        functools.partial(mlp_kernel, shards, group),
        table,
        [fc, bias, out, *blocks] + [cotangent] * group,
        [shape_of((rows, units), BF)] * 2
        + [
            shape_of((rows, width), BF),
            shape_of((1, units), F32),
            shape_of((shards, span, width), BF),
            shape_of((shards, span, width), BF),
        ],
        grid=(shards // group,),
        in_specs=[whole(*a.shape) for a in (fc, bias, out, *blocks)] + [own(i) for i in range(group)],
        out_specs=[
            rows_at(units),
            rows_at(units),
            rows_at(width),
            whole(1, units),
            pl.BlockSpec((group, span, width), lambda g, t: (g, 0, 0)),
            pl.BlockSpec((group, span, width), lambda g, t: (g, 0, 0)),
        ],
        scratch=[pltpu.VMEM((group * span, width), BF)],
        us=15,
        name="mlp",
    )


def weight_kernel(shards, batches, row_blocks, count, table, *refs):
    lefts, rights, refs = refs[:count], refs[count:-batches], refs[-batches:]
    left = jnp.concatenate([v[...] for v in lefts])
    right = jnp.concatenate([v[...] for v in rights])
    product = dot_tn(left, right).astype(BF)
    cols = product.shape[1] // batches
    size = product.shape[0] // row_blocks
    for member in range(batches):

        @pl.when(table[shards] == member)
        def _(member=member):
            for apart in range(batches):
                first = (member ^ apart) * cols
                for s in range(row_blocks):
                    refs[apart][s] = product[s * size : (s + 1) * size, first : first + cols]


def weight_shares(lefts, rights, table, shards, batches, row_blocks, name, wait=()):
    rows, cols = lefts[0].shape[1], rights[0].shape[1]
    length = sum(v.shape[0] for v in lefts)
    dims = (row_blocks, rows // row_blocks, cols // batches)
    return call(
        functools.partial(weight_kernel, shards, batches, row_blocks, len(lefts)),
        table,
        [*lefts, *rights],
        [shape_of(dims, BF)] * batches,
        us=9,
        wait=wait,
        name=name,
    )


def pack_kernel(shards, batches, ranges, table, weight, *refs):
    out, rows = refs[-1], weight.shape[0]
    for extra in refs[:-1]:
        count = (out.shape[1] - rows) // extra.shape[0]
        size = extra.shape[1] // count
        for shard in range(shards):
            for i in range(extra.shape[0]):
                for j in range(count):
                    at = rows + i * count + j
                    out[shard, at : at + 1, :size] = extra[i : i + 1, j * size : (j + 1) * size]
    for member in range(batches):

        @pl.when(table[shards] == member)
        def _(member=member):
            for shard in range(shards):
                at = 0
                for first, size in ranges(shard, member):
                    if first is None:
                        out[shard, :rows, at : at + size] = jnp.zeros((rows, size), BF)
                    else:
                        out[shard, :rows, at : at + size] = weight[:, first : first + size]
                    at += size


def pack(weight, table, shards, batches, cols, ranges, extra=(), wait=()):
    rows = weight.shape[0] + sum(v.shape[0] * -(-v.shape[1] // cols) for v in extra)
    return call(
        functools.partial(pack_kernel, shards, batches, ranges),
        table,
        [weight, *extra],
        [shape_of((shards, rows, cols), BF)],
        us=3.5,
        wait=wait,
        name="pack",
    )[0]


def assemble_kernel(shards, batches, rows, table, *refs):
    parts, out = refs[:batches], refs[batches]
    blocks, _, cols = parts[0].shape
    for member in range(batches):

        @pl.when(table[shards] == member)
        def _(member=member):
            for apart in range(batches):
                at = (member ^ apart) * cols
                for block in range(blocks):
                    out[block * rows : (block + 1) * rows, at : at + cols] = parts[apart][block, :rows, :]


def assemble(parts, table, shards, rows, wait=()):
    blocks, _, cols = parts[0].shape
    return call(
        functools.partial(assemble_kernel, shards, len(parts), rows),
        table,
        parts,
        [shape_of((blocks * rows, len(parts) * cols), BF)],
        us=5,
        wait=wait,
        name="assemble",
    )[0]


def join_kernel(table, source, out):
    out[...] = source[...]


def join(source, table, wait):
    shards, rows, cols = source.shape
    return call(
        join_kernel,
        table,
        [source],
        [shape_of(source.shape, BF)],
        grid=(shards,),
        in_specs=[pl.BlockSpec((1, rows, cols), lambda g, t: (g, 0, 0))],
        out_specs=[pl.BlockSpec((1, rows, cols), lambda g, t: (t[g], 0, 0))],
        us=4,
        wait=wait,
        name="join",
    )[0]


def proj_grad_kernel(shards, batches, table, *refs):
    lefts, rights, refs = refs[:batches], refs[batches : 2 * batches], refs[2 * batches :]
    blocks, quarter, product = refs[:-2], refs[-2], refs[-1]
    span, cols = rights[0].shape[0], quarter.shape[1]
    for member in range(batches):

        @pl.when(table[shards] == member)
        def _(member=member):
            for i in range(batches):
                quarter[i * span : (i + 1) * span, :] = rights[i][:, member * cols : (member + 1) * cols]

    left = jnp.concatenate([v[...] for v in lefts])
    result = dot_tn(left, quarter[...]).astype(BF)
    rows = result.shape[0] // shards
    piece = -(-rows // batches)
    product[...] = jnp.zeros_like(product)
    for s in range(shards):
        for i in range(batches):
            size = min(piece, rows - i * piece)
            first = s * rows + i * piece
            product[s, :size, i * cols : (i + 1) * cols] = result[first : first + size, :]
    for r in range(shards):
        blocks[r][...] = product[table[r]]


def proj_grad(lefts, rights, table, shards, span):
    batches, rows = len(lefts), lefts[0].shape[1]
    width = rights[0].shape[1]
    piece = -(-(rows // shards) // batches)
    dims = (piece + -(span + piece) % 8, width)
    return call(
        functools.partial(proj_grad_kernel, shards, batches),
        table,
        [*lefts, *rights],
        [shape_of(dims, BF)] * shards,
        scratch=[
            pltpu.VMEM((batches * lefts[0].shape[0], width // batches), BF),
            pltpu.VMEM((shards, *dims), BF),
        ],
        us=6,
        name="proj_grad",
    )


def copy_kernel(shards, batches, copies, table, source, out):
    for member in range(batches):

        @pl.when(table[shards] == member)
        def _(member=member):
            for block, first, to_block, to, size in copies(member):
                piece = source[block, :, first : first + size].astype(out.dtype)
                out[to_block, :, to : to + size] = piece


def copy_columns(source, table, shards, batches, dims, kind, copies):
    return call(
        functools.partial(copy_kernel, shards, batches, copies),
        table,
        [source],
        [shape_of(dims, kind)],
        us=4,
        name="copy_columns",
    )[0]


def cut(value):
    rows = value.shape[-2]
    if rows % 8:
        return value
    groups = max(g for g in range(1, 33) if rows // 8 % g == 0)
    return value.reshape(*value.shape[:-2], rows // 8 // groups, groups, 8, value.shape[-1])


def permute(value, axis, pairs):
    return lax.ppermute(cut(value), axis, pairs).reshape(value.shape)


def gate_kernel(count, total, *refs):
    outs = refs[-total:]
    for i in range(count):
        outs[i][...] = (refs[i][...].astype(F32) + refs[total + i][...].astype(F32)).astype(BF)


def gate(values, *others, parts=()):
    values, others, parts = list(values), jax.tree.leaves(others), list(parts)
    if not values:
        return []
    count, total = len(parts), len(values)
    anywhere = pl.BlockSpec(memory_space=pl.ANY)
    blocks = [pl.BlockSpec(memory_space=pltpu.VMEM)] * count
    return pl.pallas_call(
        functools.partial(gate_kernel, count, total),
        in_specs=blocks + [anywhere] * (total - count) + blocks + [anywhere] * len(others),
        out_specs=blocks + [anywhere] * (total - count),
        out_shape=[shape_of(v.shape, v.dtype) for v in values],
        input_output_aliases={i: i for i in range(count, total)},
        name="gate",
    )(*values, *parts, *others)


def after(value, *others):
    return gate([value], *others)[0]


class Rounds:
    def __init__(self):
        self.chains, self.mark = [], None

    def add(self, chain):
        self.chains.append([chain, None])

    def end(self, start, parts=()):
        pending, alive = [], []
        for chain, gated in self.chains:
            try:
                pending.append(list(chain.send(gated)))
                alive.append(chain)
            except StopIteration:
                pass
        values = list(start())
        out = gate(values + [v for p in pending for v in p], parts=parts)
        at, self.chains = len(values), []
        for chain, p in zip(alive, pending):
            self.chains.append([chain, out[at : at + len(p)]])
            at += len(p)
        if out:
            self.mark = out[0]
        return out[: len(values)]

    def finish(self):
        while self.chains:
            self.end(lambda: [])


class Ring:
    def __init__(self, size, rounds):
        self.size, self.rounds = size, rounds
        self.order = list(range(0, size, 2)) + list(range(size - 1, 0, -2))

    def shift(self, value, by):
        pairs = [(self.order[i], self.order[(i + by) % self.size]) for i in range(self.size)]
        return permute(value, "seq", pairs)

    def both(self, right, left):
        return [self.shift(v, 1) for v in right] + [self.shift(v, -1) for v in left]

    def gather(self, value):
        got = [value] * self.size
        right = left = value
        for far in range(1, self.size // 2 + 1):
            left = left if far < self.size - far else []
            came = self.rounds.end(lambda: self.both(right, left))
            right, left = came[: len(value)], came[len(value) :]
            got[self.size - far] = right
            if left:
                got[far] = left
        return got

    def scatter_sum(self, parts):
        size = self.size
        right, left = [parts[size // 2]], []
        for far in range(size // 2 - 1, -1, -1):
            adds = [] if not far else [parts[far]] + [parts[size - far]] * len(left)
            right, *left = self.rounds.end(lambda: self.both(right, left), adds)
            right = [right]
            if far and not left:
                left = [parts[size - far]]
        return right[0], left[0], parts[0]


def add(a, b):
    return (a.astype(F32) + b.astype(F32)).astype(BF)


def swap_blocks(value, axis="seq"):
    return lax.all_to_all(cut(value), axis, 0, 0, tiled=True).reshape(value.shape)


def over_batch(value, batches, apart):
    return permute(value, "batch", [(b, b ^ apart) for b in range(batches)])


def batch_gather_steps(value, batches):
    parts, bit = {0: value}, batches // 2
    while bit:
        came = {apart ^ bit: over_batch(part, batches, bit) for apart, part in parts.items()}
        parts.update(zip(came, (yield list(came.values()))))
        bit //= 2
    return [parts[apart] for apart in range(batches)]


def vector_kernel(shards, table, *refs):
    *rows, last, out = refs
    at = 0
    for ref in rows:
        size = ref.shape[1] // shards
        for i in range(ref.shape[0]):
            for s in range(shards):
                out[s, :, at : at + size] = ref[i : i + 1, s * size : (s + 1) * size]
            at += size
    for i in range(last.shape[0]):
        for s in range(shards):
            out[s, :, at : at + last.shape[2]] = last[i]
        at += last.shape[2]


def cut_vectors(rows, last, table, shards):
    cols = sum(v.size for v in rows) // shards + last.size
    return call(
        functools.partial(vector_kernel, shards),
        table,
        [*rows, last],
        [shape_of((shards, 1, cols), F32)],
        us=3,
        name="vectors",
    )[0]


def per_device(
    shards,
    batches,
    tokens,
    ln1_gain,
    ln1_bias,
    qkv_weight,
    qv_bias,
    proj_weight,
    proj_bias,
    ln2_gain,
    ln2_bias,
    fc_weight,
    fc_bias,
    out_weight,
    out_bias,
    cotangent,
):
    _, span, width = tokens.shape
    head_count = width // HEAD_DIM
    heads = -(-head_count // shards)
    heads += heads % 2
    padded = heads * shards
    length = span * shards
    units = fc_bias.shape[0]
    part = width // shards
    me, member = lax.axis_index("seq"), lax.axis_index("batch")
    rounds = Rounds()
    ring = Ring(shards, rounds)
    place = jnp.where(me % 2 == 0, me // 2, shards - 1 - me // 2)
    place = (place + jnp.arange(shards, dtype=jnp.int32)) % shards
    order = jnp.where(place < shards // 2, 2 * place, 2 * shards - 2 * place - 1)
    table = jnp.concatenate([order, member[None]]).astype(jnp.int32)
    row = lambda v: v.reshape(1, -1).astype(F32)

    slice_cols = heads * HEAD_COLS
    quarter = slice_cols // batches
    fc_quarter = units // batches

    def head_ranges(shard, b):
        found = []
        for col in range(shard * slice_cols + b * quarter, shard * slice_cols + (b + 1) * quarter):
            head, kind, at = col // HEAD_COLS, col % HEAD_COLS // HEAD_DIM, col % HEAD_DIM
            first = kind * width + head * HEAD_DIM + at if head < head_count else None
            if found and first is not None and found[-1][0] is not None and first == sum(found[-1]):
                found[-1] = (found[-1][0], found[-1][1] + 1)
            elif found and first is None and found[-1][0] is None:
                found[-1] = (None, found[-1][1] + 1)
            else:
                found.append((first, 1))
        return found

    def fc_ranges(shard, b):
        return [(shard * units + b * fc_quarter, fc_quarter)]

    own_tokens, own_cot = tokens[0], cotangent[0]
    far = shards // 2
    out_cols = width // batches
    out_cols = width // batches
    proj_part = lax.dynamic_slice_in_dim(proj_weight, member * out_cols, out_cols, 1)
    small = jnp.stack(
        [ln1_gain, ln1_bias, qv_bias[:part], qv_bias[part:], proj_bias, ln2_gain, ln2_bias, out_bias]
    )
    packed = pack(qkv_weight, table, shards, batches, quarter, head_ranges, [small])
    held = {}

    def first_weights():
        (got,) = yield [swap_blocks(packed)]
        held["small"] = got[:, part:, : part // ((got.shape[1] - part) // 8)]
        parts = yield from batch_gather_steps(got, batches)
        held["qkv"] = assemble(parts, table, shards, part)
        held["qkv"] = (yield [held["qkv"]])[0]

    def fc_weights():
        yield []
        got = pack(fc_weight, table, shards, batches, fc_quarter, fc_ranges, wait=[rounds.mark])
        (got,) = yield [got]
        while "qkv" not in held:
            yield []
        got = swap_blocks(after(got, rounds.mark))
        yield []
        (got,) = yield [got]
        while "normed_two" not in held:
            yield []
        came = over_batch(after(got, rounds.mark), batches, batches // 2)
        yield []
        parts = {0: got, batches // 2: (yield [came])[0]}
        bit = batches // 4
        while bit:
            came = {apart ^ bit: over_batch(p, batches, bit) for apart, p in parts.items()}
            parts.update(zip(came, (yield list(came.values()))))
            bit //= 2
        parts = [parts[apart] for apart in range(batches)]
        held["fc"] = (yield [assemble(parts, table, shards, part)])[0]

    rounds.add(first_weights())
    rounds.add(fc_weights())
    all_tokens = lax.all_gather(cut(own_tokens), "seq", axis=0, tiled=True).reshape(length, width)
    while "qkv" not in held:
        rounds.end(lambda: [])
    w_qkv = held["qkv"]
    proj_rows = after(proj_part, all_tokens, rounds.mark)
    proj_rows = lax.all_gather(cut(proj_rows), "seq", axis=0, tiled=True).reshape(shards, part, out_cols)
    small = held["small"].reshape(shards, -1)
    gain_one = row(small[:, :part])
    shift_one = row(small[:, part : 2 * part])
    bias_qv = small[:, 2 * part : 4 * part].reshape(2 * width)
    b_proj = row(small[:, 4 * part : 5 * part])
    gain_two = row(small[:, 5 * part : 6 * part])
    shift_two = row(small[:, 6 * part : 7 * part])
    b_out = row(small[:, 7 * part : 8 * part])
    bias_row = jnp.concatenate([bias_qv[:width], jnp.zeros((width,), BF), bias_qv[width:]])
    bias_heads = jnp.pad(
        bias_row.reshape(3, head_count, HEAD_DIM), ((0, 0), (0, padded - head_count), (0, 0))
    )
    bias_heads = jnp.swapaxes(bias_heads, 0, 1).reshape(1, padded * HEAD_COLS)
    bias_slice = lax.dynamic_slice_in_dim(bias_heads, me * slice_cols, slice_cols, 1).astype(F32)
    def project():
        return call(
            project_kernel,
            table,
            [gain_one, shift_one, bias_slice, w_qkv, all_tokens],
            [
                shape_of((length, width), BF),
                shape_of((length, slice_cols), BF),
                shape_of((length, width), BF),
            ],
            us=11,
            name="project",
        )

    def proj_weights():
        yield []
        yield []
        got = proj_rows
        came = over_batch(after(got, rounds.mark), batches, batches // 2)
        (came,) = yield [came]
        parts = {0: got, batches // 2: came}
        bit = batches // 4
        while bit:
            came = {apart ^ bit: over_batch(p, batches, bit) for apart, p in parts.items()}
            parts.update(zip(came, (yield list(came.values()))))
            bit //= 2
        parts = [parts[apart] for apart in range(batches)]
        held["w_proj"] = (yield [assemble(parts, table, shards, part)])[0]

    rounds.add(proj_weights())
    normed_one, projected, xhat_one = rounds.end(project)
    attended_heads, attended_full, log_total = rounds.end(lambda: attention_forward(projected, table, heads))
    all_cot = lax.all_gather(cut(after(own_cot, proj_rows, rounds.mark)), "seq", axis=0, tiled=True)
    all_cot = all_cot.reshape(length, width)
    (attended_heads,) = rounds.end(
        lambda: [swap_blocks(attended_heads.reshape(shards, span, heads * HEAD_DIM))]
    )
    while "w_proj" not in held:
        rounds.end(lambda: [])
    w_proj = held["w_proj"]
    attended, mixed, normed_two = call(
        functools.partial(mix_kernel, shards),
        table,
        [own_tokens, w_proj, b_proj, gain_two, shift_two, attended_heads],
        [shape_of((span, width), BF), shape_of((span, width), F32), shape_of((span, width), BF)],
        scratch=[pltpu.VMEM((span, padded * HEAD_DIM), BF)],
        us=6,
        name="mix",
    )

    held["normed_two"] = normed_two
    gathered = {}

    def batch_rows(value, name, flag):
        while flag not in held:
            yield []
        value = after(value, rounds.mark)
        gathered[name] = yield from batch_gather_steps(value, batches)

    rounds.add(batch_rows(attended, "attended", "mlp"))
    normed_blocks = [block for (block,) in ring.gather([normed_two])]
    while "fc" not in held:
        rounds.end(lambda: [])
    w_fc = held["fc"]
    activated, hidden_low, cot_rows, fc_sums, g_two, out_rows = mlp_part(
        normed_blocks, all_cot, w_fc, row(fc_bias), out_weight, table
    )

    shares = functools.partial(weight_shares, table=table, shards=shards, batches=batches)

    def near_sums(found):
        came = yield [over_batch(found[apart ^ 1], batches, 1) for apart in range(0, batches, 2)]
        return [add(found[2 * i], c) for i, c in enumerate(came)]

    def far_sum(kept):
        came = yield [over_batch(kept[1], batches, 2)]
        return add(kept[0], came[0])

    def fc_gradient():
        yield []
        yield []
        found = yield shares(
            normed_blocks, [hidden_low], row_blocks=shards, name="fc_grad", wait=[rounds.mark]
        )
        kept = yield from near_sums(found)
        came = over_batch(after(kept[1], rounds.mark), batches, 2)
        yield []
        share = add(kept[0], *(yield [came]))
        share = swap_blocks(share)
        yield []
        (share,) = yield [share]
        held["fc_grad"] = (yield [swap_blocks(share, "batch")])[0]

    def out_gradient():
        yield []
        yield []
        yield []
        found = yield shares([activated], [cot_rows], row_blocks=1, name="out_grad", wait=[rounds.mark])
        yield []
        kept = yield from near_sums(found)
        came = over_batch(after(kept[1], rounds.mark), batches, 2)
        yield []
        held["out_grad"] = add(kept[0], *(yield [came]))

    def out_result():
        yield []
        (total,) = yield [join(out_rows, table, [rounds.mark])]
        held["out"] = lax.psum_scatter(cut(total), "seq", scatter_dimension=0, tiled=True)

    held["mlp"] = True
    rounds.add(out_result())
    rounds.add(fc_gradient())
    rounds.add(out_gradient())
    g_two = ring.scatter_sum([g_two[r] for r in range(shards)])

    def unmix():
        return call(
            functools.partial(unmix_kernel, shards),
            table,
            [*g_two, mixed, own_cot, w_proj, gain_two],
            [
                shape_of((span, width), F32),
                shape_of((span, width), BF),
                shape_of((3, width), F32),
                shape_of((shards, span, heads * HEAD_DIM), BF),
            ],
            scratch=[pltpu.VMEM((span, padded * HEAD_DIM), BF)],
            us=7,
            name="unmix",
        )

    grad_mixed, mixed_low, norm_sums, grad_messages = rounds.end(unmix)

    rounds.add(batch_rows(mixed_low, "mixed_low", "mlp"))
    (grad_heads,) = rounds.end(lambda: [swap_blocks(grad_messages)])
    held["grad_heads"] = grad_heads
    grad_projected, column_sums = rounds.end(
        lambda: attention_backward(
            projected, grad_heads.reshape(length, -1), attended_full, log_total, table, heads, []
        )
    )
    qkv_kept = rounds.end(
        lambda: shares([normed_one], [grad_projected], row_blocks=shards, name="qkv_grad")
    )
    proj_blocks = proj_grad(gathered["attended"], gathered["mixed_low"], table, shards, span)
    share_cols = 3 * width // batches

    def overlaps(source, target):
        found = []
        for shard in range(shards):
            at = 0
            for first, size in head_ranges(shard, source):
                if first is not None:
                    low = max(first, target * share_cols)
                    high = min(first + size, (target + 1) * share_cols)
                    if low < high:
                        found.append((shard, at + low - first, low - target * share_cols, high - low))
                at += size
        return found

    most = max(sum(o[3] for o in overlaps(q, b)) for q in range(batches) for b in range(batches))
    most = -(-most // 128) * 128

    def outgoing(b):
        copies = []
        for target in range(batches):
            at = 0
            for shard, first, _, size in overlaps(b, target):
                copies.append((shard, first, target, at, size))
                at += size
        return copies

    def incoming(b):
        copies = []
        for source in range(batches):
            at = 0
            for _, _, to, size in overlaps(source, b):
                copies.append((source, at, 0, to, size))
                at += size
        return copies

    def qkv_gradient():
        kept = yield from near_sums(qkv_kept)
        share = yield from far_sum(kept)
        (share,) = yield [swap_blocks(share)]
        share = copy_columns(share, table, shards, batches, (batches, part, most), BF, outgoing)
        (share,) = yield [swap_blocks(share, "batch")]
        held["qkv_grad"] = copy_columns(share, table, shards, batches, (1, part, share_cols), F32, incoming)[0]

    def vector_gradients():
        yield []
        cot_sums = jnp.sum(own_cot.astype(F32), axis=0, keepdims=True)
        rows = cut_vectors([held["norm_one"], norm_sums, cot_sums], column_sums, table, shards)
        (rows,) = yield [lax.all_to_all(rows, "seq", 0, 0, tiled=True)]
        part_sums = jnp.sum(rows[:, :, : 6 * part], axis=0)
        head_sums = rows[:, 0, 6 * part :].reshape(padded, 3, HEAD_DIM)[:head_count]
        qv_sums = jnp.concatenate([head_sums[:, 0], head_sums[:, 2]]).reshape(1, 2 * width)
        qv_sums = lax.dynamic_slice_in_dim(qv_sums, me * 2 * part, 2 * part, 1)
        sums = jnp.concatenate([part_sums, qv_sums, fc_sums], axis=1)
        bit = 1
        while bit < batches:
            (came,) = yield [lax.ppermute(sums, "batch", [(b, b ^ bit) for b in range(batches)])]
            sums = sums + came
            bit *= 2
        held["sums"] = sums[0]

    rounds.add(qkv_gradient())
    rounds.add(vector_gradients())

    def unproject():
        return call(
            functools.partial(unproject_kernel, shards),
            table,
            [grad_projected, w_qkv, xhat_one, *proj_blocks],
            [shape_of((span + proj_blocks[0].shape[0], width), BF)] * shards + [shape_of((2, width), F32)],
            scratch=[pltpu.VMEM((length, width), BF)],
            us=9,
            name="unproject",
        )

    *g_one, held["norm_one"] = rounds.end(unproject)
    total = sum(term.astype(F32) for term in ring.scatter_sum(g_one))
    g_one, pieces = total[:span], -(-part // batches)
    proj_share = [total[span : span + pieces, b * out_cols : (b + 1) * out_cols] for b in range(batches)]
    proj_share = jnp.concatenate(proj_share)[:part]
    xhat, inverse = norm_stats(own_tokens.astype(F32))
    block_out = (mixed + b_out + held["out"].reshape(span, width).astype(F32)).astype(BF)
    input_grad = (grad_mixed + norm_back(g_one, xhat, inverse, gain_one)).astype(BF)
    rounds.finish()

    runs = shards // batches

    def fc_copies(b):
        return [
            (q * runs + run, 0, 0, (run * batches + q) * fc_quarter, fc_quarter)
            for q in range(batches)
            for run in range(runs)
        ]

    fc_share = held["fc_grad"]
    fc_share = copy_columns(fc_share, table, shards, batches, (1, part, runs * units), F32, fc_copies)[0]
    sums = held["sums"]
    vectors = [sums[i * part : (i + 1) * part] for i in range(6)]
    return (
        block_out[None],
        input_grad[None],
        vectors[0],
        vectors[1],
        held["qkv_grad"],
        sums[6 * part : 8 * part],
        proj_share,
        vectors[4],
        vectors[2],
        vectors[3],
        fc_share,
        sums[8 * part : 8 * part + units],
        held["out_grad"][0].astype(F32),
        vectors[5],
    )


def solution(mesh):
    rows = P("batch", "seq", None)
    matrix, vector = P("seq", None), P("seq")
    shared = P("seq", "batch")
    return jax.shard_map(
        functools.partial(per_device, mesh.shape["seq"], mesh.shape["batch"]),
        mesh=mesh,
        in_specs=(
            rows, vector, vector, matrix, vector, matrix, vector,
            vector, vector, matrix, vector, matrix, vector, rows,
        ),
        out_specs=(
            rows, rows, vector, vector, shared, vector, shared,
            vector, vector, vector, shared, vector, shared, vector,
        ),
        check_vma=False,
    )
```

```python
import functools

import jax
import jax.numpy as jnp
from jax import lax
from jax.experimental import pallas as pl
from jax.experimental.pallas import tpu as pltpu
from jax.sharding import PartitionSpec as P

HEAD_DIM = 64
HEAD_COLS = 3 * HEAD_DIM
EPSILON = 1e-05
FLOOR_SCORE = -1e30
SCALE = HEAD_DIM**-0.5
BF = jnp.bfloat16
F32 = jnp.float32
VMEM_LIMIT = 56 << 20
MOST_ROWS = 1024
COST = 1.6e8


def dot_nn(a, b):
    return lax.dot_general(a, b, (((1,), (0,)), ((), ())), preferred_element_type=F32)


def dot_nt(a, b):
    return lax.dot_general(a, b, (((1,), (1,)), ((), ())), preferred_element_type=F32)


def dot_tn(a, b):
    return lax.dot_general(a, b, (((0,), (0,)), ((), ())), preferred_element_type=F32)


def shape_of(dims, kind):
    return jax.ShapeDtypeStruct(dims, kind)


def whole(*dims):
    return pl.BlockSpec(dims, lambda *_: (0,) * len(dims), pipeline_mode=pl.Buffered(1))


def call(
    kernel, table, operands, outs, scratch=(), name=None, us=1, in_specs=None, out_specs=None, grid=(1,), wait=()
):
    count, wait = 1 + len(operands), jax.tree.leaves(wait)

    def body(*refs):
        kernel(*refs[:count], *refs[count + len(wait) :])

    return pl.pallas_call(
        body,
        grid_spec=pltpu.PrefetchScalarGridSpec(
            num_scalar_prefetch=1,
            grid=grid,
            in_specs=(in_specs or [whole(*a.shape) for a in operands])
            + [pl.BlockSpec(memory_space=pl.ANY)] * len(wait),
            out_specs=out_specs or [whole(*o.shape) for o in outs],
            scratch_shapes=list(scratch),
        ),
        out_shape=list(outs),
        compiler_params=pltpu.CompilerParams(vmem_limit_bytes=VMEM_LIMIT),
        cost_estimate=pl.CostEstimate(flops=int(us * COST), bytes_accessed=1 << 16, transcendentals=0),
        name=name,
    )(table, *operands, *wait)


def steps(count, unrolled, body, carry):
    if unrolled:
        for j in range(count):
            carry = body(j, carry)
        return carry
    return lax.fori_loop(0, count, body, carry)


def rows_of(index, size):
    if isinstance(index, int):
        return pl.ds(index * size, size)
    return pl.ds(pl.multiple_of(index * size, size), size)


def causal(tile):
    key_pos = lax.broadcasted_iota(jnp.int32, (tile, tile), 0)
    query_pos = lax.broadcasted_iota(jnp.int32, (tile, tile), 1)
    return key_pos <= query_pos


def forward_kernel(tile, unrolled, table, x_ref, low_ref, full_ref, log_ref, value_t):
    tiles = x_ref.shape[0] // tile
    for head in range(2):
        base = head * HEAD_COLS
        k_cols = pl.ds(base + HEAD_DIM, HEAD_DIM)
        out_cols = pl.ds(head * HEAD_DIM, HEAD_DIM)

        def turn(j, carry):
            value_t[j] = x_ref[rows_of(j, tile), pl.ds(base + 2 * HEAD_DIM, HEAD_DIM)].T
            return carry

        steps(tiles, unrolled, turn, 0)

        def query_tile(i, carry):
            rows = rows_of(i, tile)
            query = x_ref[rows, pl.ds(base, HEAD_DIM)] * jnp.asarray(SCALE, BF)

            def add(j, state, masked):
                top, total, acc = state
                scores = dot_nt(x_ref[rows_of(j, tile), k_cols], query)
                if masked:
                    scores = jnp.where(causal(tile), scores, FLOOR_SCORE)
                new_top = jnp.maximum(top, jnp.max(scores, axis=0, keepdims=True))
                probs = jnp.exp(scores - new_top)
                fade = jnp.exp(top - new_top)
                total = total * fade + jnp.sum(probs, axis=0, keepdims=True)
                acc = acc * fade + dot_nn(value_t[j], probs.astype(BF))
                return new_top, total, acc

            state = (
                jnp.full((1, tile), FLOOR_SCORE, F32),
                jnp.zeros((1, tile), F32),
                jnp.zeros((HEAD_DIM, tile), F32),
            )
            state = steps(i, unrolled, lambda j, s: add(j, s, False), state)
            top, total, acc = add(i, state, True)
            result = (acc / total).T
            low_ref[rows, out_cols] = result.astype(BF)
            full_ref[rows, out_cols] = result
            log_ref[0, pl.ds(head, 1), rows] = top + jnp.log(total)
            return carry

        steps(tiles, unrolled, query_tile, 0)


def backward_kernel(
    tile, unrolled, table, x_ref, grad_ref, full_ref, log_ref, dx_ref, sum_ref, key_t, key_acc, value_acc
):
    tiles = x_ref.shape[0] // tile
    for head in range(2):
        base = head * HEAD_COLS
        q_cols = pl.ds(base, HEAD_DIM)
        k_cols = pl.ds(base + HEAD_DIM, HEAD_DIM)
        v_cols = pl.ds(base + 2 * HEAD_DIM, HEAD_DIM)
        out_cols = pl.ds(head * HEAD_DIM, HEAD_DIM)

        def turn(j, carry):
            key_t[j] = x_ref[rows_of(j, tile), k_cols].T
            return carry

        steps(tiles, unrolled, turn, 0)
        key_acc[...] = jnp.zeros_like(key_acc)
        value_acc[...] = jnp.zeros_like(value_acc)

        def query_tile(i, query_sum):
            rows = rows_of(i, tile)
            query = x_ref[rows, q_cols] * jnp.asarray(SCALE, BF)
            grad = grad_ref[rows, out_cols]
            delta = jnp.sum((grad.astype(F32) * full_ref[rows, out_cols]).T, axis=0, keepdims=True)
            log_row = log_ref[0, pl.ds(head, 1), rows]

            def add(j, acc, masked):
                key_rows = rows_of(j, tile)
                scores = dot_nt(x_ref[key_rows, k_cols], query)
                probs = jnp.exp(scores - log_row)
                if masked:
                    probs = jnp.where(causal(tile), probs, 0.0)
                grad_probs = dot_nt(x_ref[key_rows, v_cols], grad)
                grad_scores = (probs * (grad_probs - delta)).astype(BF)
                value_acc[key_rows, :] += dot_nn(probs.astype(BF), grad)
                key_acc[key_rows, :] += dot_nn(grad_scores, query)
                return acc + dot_nn(key_t[j], grad_scores)

            acc = jnp.zeros((HEAD_DIM, tile), F32)
            acc = steps(i, unrolled, lambda j, s: add(j, s, False), acc)
            acc = add(i, acc, True)
            result = acc.T * SCALE
            dx_ref[rows, q_cols] = result.astype(BF)
            return query_sum + jnp.sum(result, axis=0, keepdims=True)

        query_sum = steps(tiles, unrolled, query_tile, jnp.zeros((1, HEAD_DIM), F32))
        dx_ref[:, k_cols] = key_acc[...].astype(BF)
        dx_ref[:, v_cols] = value_acc[...].astype(BF)
        sum_ref[0, :, q_cols] = query_sum
        sum_ref[0, :, k_cols] = jnp.sum(key_acc[...], axis=0, keepdims=True)
        sum_ref[0, :, v_cols] = jnp.sum(value_acc[...], axis=0, keepdims=True)


def attention_forward(projected, table, heads):
    length = projected.shape[0]
    tile = min(256, length)
    tiles, pairs = length // tile, heads // 2
    wide, narrow = 2 * HEAD_COLS, 2 * HEAD_DIM
    columns = lambda g, t: (0, g)
    return call(
        functools.partial(forward_kernel, tile, tiles <= 4),
        table,
        [projected],
        [
            shape_of((length, heads * HEAD_DIM), BF),
            shape_of((length, heads * HEAD_DIM), F32),
            shape_of((pairs, 2, length), F32),
        ],
        grid=(pairs,),
        in_specs=[pl.BlockSpec((length, wide), columns)],
        out_specs=[
            pl.BlockSpec((length, narrow), columns),
            pl.BlockSpec((length, narrow), columns),
            pl.BlockSpec((1, 2, length), lambda g, t: (g, 0, 0)),
        ],
        scratch=[pltpu.VMEM((tiles, HEAD_DIM, tile), BF)],
        us=15,
        name="attention_forward",
    )


def attention_backward(projected, grads, full, logs, table, heads, wait):
    length = projected.shape[0]
    tile = min(256, length)
    tiles, pairs = length // tile, heads // 2
    wide, narrow = 2 * HEAD_COLS, 2 * HEAD_DIM
    columns = lambda g, t: (0, g)
    return call(
        functools.partial(backward_kernel, tile, tiles <= 4),
        table,
        [projected, grads, full, logs],
        [shape_of((length, heads * HEAD_COLS), BF), shape_of((pairs, 1, wide), F32)],
        grid=(pairs,),
        in_specs=[
            pl.BlockSpec((length, wide), columns),
            pl.BlockSpec((length, narrow), columns),
            pl.BlockSpec((length, narrow), columns),
            pl.BlockSpec((1, 2, length), lambda g, t: (g, 0, 0)),
        ],
        out_specs=[
            pl.BlockSpec((length, wide), columns),
            pl.BlockSpec((1, 1, wide), lambda g, t: (g, 0, 0)),
        ],
        scratch=[
            pltpu.VMEM((tiles, HEAD_DIM, tile), BF),
            pltpu.VMEM((length, HEAD_DIM), F32),
            pltpu.VMEM((length, HEAD_DIM), F32),
        ],
        us=14,
        wait=wait,
        name="attention_backward",
    )


def norm_stats(rows):
    mean = jnp.mean(rows, axis=-1, keepdims=True)
    centred = rows - mean
    variance = jnp.mean(centred * centred, axis=-1, keepdims=True)
    inverse = lax.rsqrt(variance + EPSILON)
    return centred * inverse, inverse


def norm_back(grad, xhat, inverse, gain):
    h = grad * gain
    return inverse * (
        h - jnp.mean(h, axis=-1, keepdims=True) - xhat * jnp.mean(h * xhat, axis=-1, keepdims=True)
    )


ROOT = 0.7978845608028654
CUBE = 0.044715


def gelu_both(hidden):
    square = hidden * hidden
    bent = jnp.tanh(ROOT * hidden * (1.0 + CUBE * square))
    half = 0.5 * (1.0 + bent)
    slope = half + 0.5 * hidden * (1.0 - bent * bent) * ROOT * (1.0 + 3.0 * CUBE * square)
    return hidden * half, slope


def project_kernel(shards, table, gain, shift, bias, weight, *refs):
    blocks, (normed, projected, kept) = refs[:shards], refs[shards:]
    span = blocks[0].shape[0]
    for r in range(shards):
        normed[rows_of(table[r], span), :] = blocks[r][...]
    length = span * shards
    chunk = min(256, length)

    def some_rows(i, carry):
        rows = rows_of(i, chunk)
        xhat, _ = norm_stats(normed[rows, :].astype(F32))
        kept[rows, :] = xhat.astype(BF)
        normed[rows, :] = (xhat * gain[...] + shift[...]).astype(BF)
        projected[rows, :] = (dot_nn(normed[rows, :], weight[...]) + bias[...]).astype(BF)
        return carry

    lax.fori_loop(0, length // chunk, some_rows, 0)


def unproject_kernel(shards, batches, heads, table, grad, weight, xhat, norms, cots, head_sums, *refs):
    others, blocks, (sums, rows, vectors) = refs[:shards], refs[shards : 2 * shards], refs[2 * shards :]
    length = rows.shape[0]
    span, chunk = length // shards, min(256, length)
    sums[...] = jnp.zeros_like(sums)

    def some_rows(i, carry):
        at = rows_of(i, chunk)
        share = dot_nt(grad[at, :], weight[...])
        rows[at, :] = share.astype(BF)
        sums[0:1, :] += jnp.sum(share * xhat[at, :].astype(F32), axis=0, keepdims=True)
        sums[1:2, :] += jnp.sum(share, axis=0, keepdims=True)
        return carry

    lax.fori_loop(0, length // chunk, some_rows, 0)
    width = sums.shape[1]
    part = width // shards
    for s in range(shards):
        for i, source in enumerate([sums[0:1], sums[1:2], norms[0:1], norms[1:2], norms[2:3], cots[...]]):
            vectors[s, :, i * part : (i + 1) * part] = source[:, s * part : (s + 1) * part]
        vectors[s, :, 6 * part :] = jnp.zeros((1, width - 6 * part), F32)
    for s in range(shards):

        @pl.when(table[0] == s)
        def _(s=s):
            for first, shard, to, size in head_copies(s, shards, heads, width):
                pair, at = first
                vectors[shard, :, 6 * part + to : 6 * part + to + size] = head_sums[pair, :, at : at + size]

    last = others[0].shape[0] - 1
    for r in range(shards):
        blocks[r][:span, :] = rows[rows_of(table[r], span), :]
        blocks[r][span : span + last, :] = others[r][:last, :]
        blocks[r][span + last :, :] = vectors[table[r]].astype(BF)


def head_copies(shard, shards, heads, width):
    found, piece = [], 2 * width // shards
    for head in range(heads):
        number = shard * heads + head
        if (number + 1) * HEAD_DIM > width:
            continue
        for kind, base in ((0, 0), (2, width)):
            at, end = base + number * HEAD_DIM, base + (number + 1) * HEAD_DIM
            first = head % 2 * HEAD_COLS + kind * HEAD_DIM
            while at < end:
                size = min(end, (at // piece + 1) * piece) - at
                found.append(((head // 2, first), at // piece, at % piece, size))
                at, first = at + size, first + size
    return found


def mix_kernel(shards, table, tokens, weight, bias, gain, shift, heads, attended, mixed, normed, spread):
    cols, width = heads.shape[2], attended.shape[1]
    for s in range(shards):
        spread[:, s * cols : (s + 1) * cols] = heads[s]
    attended[...] = spread[:, :width]
    mixed[...] = tokens[...].astype(F32) + dot_nn(attended[...], weight[...]) + bias[...]
    xhat, _ = norm_stats(mixed[...])
    normed[...] = (xhat * gain[...] + shift[...]).astype(BF)


def unmix_kernel(shards, table, first, second, third, mixed, cotangent, weight, gain, *refs):
    grad_mixed, low, sums, pieces, spread = refs
    cols, (span, width) = pieces.shape[2], low.shape
    grad = first[...].astype(F32) + second[...].astype(F32) + third[...].astype(F32)
    xhat, inverse = norm_stats(mixed[...])
    full = cotangent[...].astype(F32) + norm_back(grad, xhat, inverse, gain[...])
    grad_mixed[...] = full
    low[...] = full.astype(BF)
    sums[0:1, :] = jnp.sum(grad * xhat, axis=0, keepdims=True)
    sums[1:2, :] = jnp.sum(grad, axis=0, keepdims=True)
    sums[2:3, :] = jnp.sum(full, axis=0, keepdims=True)
    spread[:, width:] = jnp.zeros_like(spread[:, width:])
    spread[:, :width] = dot_nt(low[...], weight[...]).astype(BF)
    for s in range(shards):
        pieces[s] = spread[:, s * cols : (s + 1) * cols]


def mlp_kernel(shards, group, table, fc, bias, out, *refs):
    blocks, cotangents, refs = refs[:shards], refs[shards : 2 * shards], refs[2 * shards :]
    act, low, sums, results = refs[:4]
    shares, (normed, cots) = refs[4 : 4 + shards], refs[4 + shards :]
    step = pl.program_id(0)
    span = blocks[0].shape[0]
    for first in range(0, shards, group):

        @pl.when(step == first // group)
        def _(first=first):
            for i in range(group):
                normed[i * span : (i + 1) * span, :] = blocks[first + i][...]
                cots[i * span : (i + 1) * span, :] = cotangents[first + i][...]

    hidden = dot_nn(normed[...], fc[...]) + bias[...]
    activated, slope = gelu_both(hidden)
    act[...] = activated.astype(BF)
    grad = dot_nt(cots[...], out[...]) * slope
    total = jnp.sum(grad, axis=0, keepdims=True)

    @pl.when(step == 0)
    def _():
        sums[...] = total

    @pl.when(step > 0)
    def _():
        sums[...] += total

    low[...] = grad.astype(BF)
    share = dot_nt(low[...], fc[...]).astype(BF)
    result = dot_nn(act[...], out[...]).astype(BF)
    for i in range(group):
        results[i] = result[i * span : (i + 1) * span, :]
    for first in range(0, shards, group):

        @pl.when(step == first // group)
        def _(first=first):
            for i in range(group):
                shares[first + i][...] = share[i * span : (i + 1) * span, :]


def mlp_part(blocks, cotangents, fc, bias, out, table):
    shards = len(blocks)
    span, width = blocks[0].shape
    rows, units = shards * span, fc.shape[1]
    if rows > MOST_ROWS:
        half = shards // 2
        halves = [mlp_part(blocks[i:][:half], cotangents[i:][:half], fc, bias, out, table) for i in (0, half)]
        first, second = halves
        results = jnp.concatenate([first[3], second[3]])
        return first[0] + second[0], first[1] + second[1], first[2] + second[2], results, first[4] + second[4]
    group = min(shards, max(1, 512 // span))
    rows_at = lambda cols: pl.BlockSpec((group * span, cols), lambda g, t: (g, 0))
    got = call(
        functools.partial(mlp_kernel, shards, group),
        table,
        [fc, bias, out, *blocks, *cotangents],
        [shape_of((rows, units), BF)] * 2
        + [
            shape_of((1, units), F32),
            shape_of((shards, span, width), BF),
        ]
        + [shape_of((span, width), BF)] * shards,
        grid=(shards // group,),
        out_specs=[
            rows_at(units),
            rows_at(units),
            whole(1, units),
            pl.BlockSpec((group, span, width), lambda g, t: (g, 0, 0)),
        ]
        + [whole(span, width)] * shards,
        scratch=[pltpu.VMEM((group * span, width), BF)] * 2,
        us=15,
        name="mlp",
    )
    return got[:1], got[1:2], got[2], got[3], got[4:]


def take_rows(pieces):
    found = []
    while pieces and sum(v.shape[0] for v in found) < MOST_ROWS:
        found.append(pieces.pop(0))
    return found


def weight_kernel(shards, batches, row_blocks, count, table, *refs):
    lefts, rights, refs = refs[:count], refs[count:-batches], refs[-batches:]
    left = jnp.concatenate([v[...] for v in lefts])
    right = jnp.concatenate([v[...] for v in rights])
    product = dot_tn(left, right).astype(BF)
    cols = product.shape[1] // batches
    size = product.shape[0] // row_blocks
    for member in range(batches):

        @pl.when(table[shards] == member)
        def _(member=member):
            for apart in range(batches):
                first = (member ^ apart) * cols
                for s in range(row_blocks):
                    refs[apart][s] = product[s * size : (s + 1) * size, first : first + cols]


def weight_shares(lefts, rights, table, shards, batches, row_blocks, name, wait=()):
    rows, cols = lefts[0].shape[1], rights[0].shape[1]
    dims = (row_blocks, rows // row_blocks, cols // batches)
    if sum(v.shape[0] for v in lefts) > MOST_ROWS:
        cut_rows = lambda vs: [v[i : i + MOST_ROWS] for v in vs for i in range(0, v.shape[0], MOST_ROWS)]
        total, lefts, rights = None, cut_rows(lefts), cut_rows(rights)
        while lefts:
            some = [take_rows(lefts), take_rows(rights)]
            found = weight_shares(*some, table, shards, batches, row_blocks, name, wait)
            total = found if total is None else [add(a, b) for a, b in zip(total, found)]
        return total
    return call(
        functools.partial(weight_kernel, shards, batches, row_blocks, len(lefts)),
        table,
        [*lefts, *rights],
        [shape_of(dims, BF)] * batches,
        us=9,
        wait=wait,
        name=name,
    )


def pack_kernel(shards, batches, ranges, table, weight, *refs):
    out, rows = refs[-1], weight.shape[0]
    for extra in refs[:-1]:
        count = (out.shape[1] - rows) // extra.shape[0]
        size = extra.shape[1] // count
        for shard in range(shards):
            for i in range(extra.shape[0]):
                for j in range(count):
                    at = rows + i * count + j
                    out[shard, at : at + 1, :size] = extra[i : i + 1, j * size : (j + 1) * size]
    for member in range(batches):

        @pl.when(table[shards] == member)
        def _(member=member):
            for shard in range(shards):
                at = 0
                for first, size in ranges(shard, member):
                    if first is None:
                        out[shard, :rows, at : at + size] = jnp.zeros((rows, size), BF)
                    else:
                        out[shard, :rows, at : at + size] = weight[:, first : first + size]
                    at += size


def pack(weight, table, shards, batches, cols, ranges, extra=(), wait=()):
    rows = weight.shape[0] + sum(v.shape[0] * -(-v.shape[1] // cols) for v in extra)
    return call(
        functools.partial(pack_kernel, shards, batches, ranges),
        table,
        [weight, *extra],
        [shape_of((shards, rows, cols), BF)],
        us=3.5,
        wait=wait,
        name="pack",
    )[0]


def assemble_kernel(shards, batches, rows, pieces, table, *refs):
    out = refs[-1]
    blocks, _, cols = refs[0].shape
    for member in range(batches):

        @pl.when(table[shards] == member)
        def _(member=member):
            for apart in range(batches):
                at = (member ^ apart) * cols
                for i in range(pieces * blocks):
                    source = refs[apart * pieces + i // blocks][i % blocks, :rows, :]
                    out[i * rows : (i + 1) * rows, at : at + cols] = source


def assemble(parts, table, shards, rows, pieces=1, wait=()):
    blocks, _, cols = parts[0].shape
    batches = len(parts) // pieces
    return call(
        functools.partial(assemble_kernel, shards, batches, rows, pieces),
        table,
        parts,
        [shape_of((pieces * blocks * rows, batches * cols), BF)],
        us=5,
        wait=wait,
        name="assemble",
    )[0]


def join_kernel(table, source, out):
    out[...] = source[...]


def join(source, table, wait):
    shards, rows, cols = source.shape
    return call(
        join_kernel,
        table,
        [source],
        [shape_of(source.shape, BF)],
        grid=(shards,),
        in_specs=[pl.BlockSpec((1, rows, cols), lambda g, t: (g, 0, 0))],
        out_specs=[pl.BlockSpec((1, rows, cols), lambda g, t: (t[g], 0, 0))],
        us=4,
        wait=wait,
        name="join",
    )[0]


def proj_grad_kernel(shards, batches, table, *refs):
    lefts, rights, refs = refs[:batches], refs[batches : 2 * batches], refs[2 * batches :]
    blocks, quarter, product = refs[:-2], refs[-2], refs[-1]
    span, cols = rights[0].shape[0], quarter.shape[1]
    for member in range(batches):

        @pl.when(table[shards] == member)
        def _(member=member):
            for i in range(batches):
                quarter[i * span : (i + 1) * span, :] = rights[i][:, member * cols : (member + 1) * cols]

    left = jnp.concatenate([v[...] for v in lefts])
    result = dot_tn(left, quarter[...]).astype(BF)
    rows = result.shape[0] // shards
    piece = -(-rows // batches)
    product[...] = jnp.zeros_like(product)
    for s in range(shards):
        for i in range(batches):
            size = min(piece, rows - i * piece)
            first = s * rows + i * piece
            product[s, :size, i * cols : (i + 1) * cols] = result[first : first + size, :]
    for r in range(shards):
        blocks[r][...] = product[table[r]]


def proj_grad(lefts, rights, table, shards, span):
    batches, rows = len(lefts), lefts[0].shape[1]
    width = rights[0].shape[1]
    piece = -(-(rows // shards) // batches)
    dims = (piece + 1 + -(span + piece + 1) % 8, width)
    return call(
        functools.partial(proj_grad_kernel, shards, batches),
        table,
        [*lefts, *rights],
        [shape_of(dims, BF)] * shards,
        scratch=[
            pltpu.VMEM((batches * lefts[0].shape[0], width // batches), BF),
            pltpu.VMEM((shards, *dims), BF),
        ],
        us=6,
        name="proj_grad",
    )


def copy_kernel(shards, batches, copies, table, source, out):
    for member in range(batches):

        @pl.when(table[shards] == member)
        def _(member=member):
            for block, first, to_block, to, size in copies(member):
                piece = source[block, :, first : first + size].astype(out.dtype)
                out[to_block, :, to : to + size] = piece


def copy_columns(source, table, shards, batches, dims, kind, copies):
    return call(
        functools.partial(copy_kernel, shards, batches, copies),
        table,
        [source],
        [shape_of(dims, kind)],
        us=4,
        name="copy_columns",
    )[0]


def cut(value):
    rows = value.shape[-2]
    if rows % 8:
        return value
    groups = max(g for g in range(1, 33) if rows // 8 % g == 0)
    return value.reshape(*value.shape[:-2], rows // 8 // groups, groups, 8, value.shape[-1])


def permute(value, axis, pairs):
    return lax.ppermute(cut(value), axis, pairs).reshape(value.shape)


def gate_kernel(count, total, *refs):
    outs = refs[-total:]
    for i in range(count):
        outs[i][...] = (refs[i][...].astype(F32) + refs[total + i][...].astype(F32)).astype(BF)


def gate(values, *others, parts=()):
    values, others, parts = list(values), jax.tree.leaves(others), list(parts)
    if not values:
        return []
    count, total = len(parts), len(values)
    anywhere = pl.BlockSpec(memory_space=pl.ANY)
    blocks = [pl.BlockSpec(memory_space=pltpu.VMEM)] * count
    return pl.pallas_call(
        functools.partial(gate_kernel, count, total),
        in_specs=blocks + [anywhere] * (total - count) + blocks + [anywhere] * len(others),
        out_specs=blocks + [anywhere] * (total - count),
        out_shape=[shape_of(v.shape, v.dtype) for v in values],
        input_output_aliases={i: i for i in range(count, total)},
        name="gate",
    )(*values, *parts, *others)


def after(value, *others):
    return gate([value], *others)[0]


class Rounds:
    def __init__(self):
        self.chains, self.mark, self.waits = [], None, []

    def add(self, chain):
        self.chains.append([chain, None])

    def end(self, start, parts=()):
        pending, alive = [], []
        for chain, gated in self.chains:
            try:
                pending.append(list(chain.send(gated)))
                alive.append(chain)
            except StopIteration:
                pass
        values = list(start())
        out = gate(values + [v for p in pending for v in p], self.waits, parts=parts)
        self.waits = []
        at, self.chains = len(values), []
        for chain, p in zip(alive, pending):
            self.chains.append([chain, out[at : at + len(p)]])
            at += len(p)
        if out:
            self.mark = out[0]
        return out[: len(values)]

    def finish(self):
        while self.chains:
            self.end(lambda: [])


class Ring:
    def __init__(self, size, rounds):
        self.size, self.rounds = size, rounds
        self.order = list(range(0, size, 2)) + list(range(size - 1, 0, -2))

    def shift(self, value, by):
        pairs = [(self.order[i], self.order[(i + by) % self.size]) for i in range(self.size)]
        return permute(value, "seq", pairs)

    def both(self, right, left):
        return [self.shift(v, 1) for v in right] + [self.shift(v, -1) for v in left]

    def gather(self, value):
        got = [value] * self.size
        right = left = value
        for far in range(1, self.size // 2 + 1):
            left = left if far < self.size - far else []
            came = self.rounds.end(lambda: self.both(right, left))
            right, left = came[: len(value)], came[len(value) :]
            got[self.size - far] = right
            if left:
                got[far] = left
        return got

    def scatter_sum(self, parts):
        size = self.size
        right, left = [parts[size // 2]], []
        for far in range(size // 2 - 1, -1, -1):
            adds = [] if not far else [parts[far]] + [parts[size - far]] * len(left)
            right, *left = self.rounds.end(lambda: self.both(right, left), adds)
            right = [right]
            if far and not left:
                left = [parts[size - far]]
        return right[0], left[0], parts[0]


def add(a, b):
    return (a.astype(F32) + b.astype(F32)).astype(BF)


def swap_blocks(value, axis="seq"):
    return lax.all_to_all(cut(value), axis, 0, 0, tiled=True).reshape(value.shape)


def over_batch(value, batches, apart):
    return permute(value, "batch", [(b, b ^ apart) for b in range(batches)])


def batch_gather_steps(value, batches):
    parts, bit = {0: value}, batches // 2
    while bit:
        came = {apart ^ bit: over_batch(part, batches, bit) for apart, part in parts.items()}
        parts.update(zip(came, (yield list(came.values()))))
        bit //= 2
    return [parts[apart] for apart in range(batches)]


def per_device(
    shards,
    batches,
    tokens,
    ln1_gain,
    ln1_bias,
    qkv_weight,
    qv_bias,
    proj_weight,
    proj_bias,
    ln2_gain,
    ln2_bias,
    fc_weight,
    fc_bias,
    out_weight,
    out_bias,
    cotangent,
):
    _, span, width = tokens.shape
    head_count = width // HEAD_DIM
    heads = -(-head_count // shards)
    heads += heads % 2
    padded = heads * shards
    length = span * shards
    units = fc_bias.shape[0]
    part = width // shards
    me, member = lax.axis_index("seq"), lax.axis_index("batch")
    rounds = Rounds()
    ring = Ring(shards, rounds)
    place = jnp.where(me % 2 == 0, me // 2, shards - 1 - me // 2)
    place = (place + jnp.arange(shards, dtype=jnp.int32)) % shards
    order = jnp.where(place < shards // 2, 2 * place, 2 * shards - 2 * place - 1)
    table = jnp.concatenate([order, member[None]]).astype(jnp.int32)
    row = lambda v: v.reshape(1, -1).astype(F32)

    slice_cols = heads * HEAD_COLS
    quarter = slice_cols // batches
    fc_quarter = units // batches

    def head_ranges(shard, b):
        found = []
        for col in range(shard * slice_cols + b * quarter, shard * slice_cols + (b + 1) * quarter):
            head, kind, at = col // HEAD_COLS, col % HEAD_COLS // HEAD_DIM, col % HEAD_DIM
            first = kind * width + head * HEAD_DIM + at if head < head_count else None
            if found and first is not None and found[-1][0] is not None and first == sum(found[-1]):
                found[-1] = (found[-1][0], found[-1][1] + 1)
            elif found and first is None and found[-1][0] is None:
                found[-1] = (None, found[-1][1] + 1)
            else:
                found.append((first, 1))
        return found

    def fc_ranges(shard, b):
        return [(shard * units + b * fc_quarter, fc_quarter)]

    own_tokens, own_cot = tokens[0], cotangent[0]
    far = shards // 2
    out_cols = width // batches
    out_cols = width // batches
    proj_part = lax.dynamic_slice_in_dim(proj_weight, member * out_cols, out_cols, 1)
    small = jnp.stack(
        [ln1_gain, ln1_bias, qv_bias[:part], qv_bias[part:], proj_bias, ln2_gain, ln2_bias, out_bias]
    )
    packed = pack(qkv_weight, table, shards, batches, quarter, head_ranges, [small])
    held = {}

    def first_weights():
        (got,) = yield [swap_blocks(packed)]
        held["small"] = got[:, part:, : part // ((got.shape[1] - part) // 8)]
        parts = yield from batch_gather_steps(got, batches)
        held["qkv"] = assemble(parts, table, shards, part)
        rounds.waits.append(held["qkv"])

    far = shards // 2

    def fc_weights():
        yield []
        got = pack(fc_weight, table, shards, batches, fc_quarter, fc_ranges, wait=[rounds.mark])
        (got,) = yield [got]
        for _ in range(far - 2):
            yield []
        (got,) = yield [swap_blocks(after(got, rounds.mark))]
        while "normed_two" not in held:
            yield []
        got = after(got, rounds.mark)
        came = over_batch(got, batches, batches // 2)
        yield []
        parts = {0: got, batches // 2: (yield [came])[0]}
        bit = batches // 4
        while bit:
            came = {apart ^ bit: over_batch(p, batches, bit) for apart, p in parts.items()}
            parts.update(zip(came, (yield list(came.values()))))
            bit //= 2
        parts = [parts[apart] for apart in range(batches)]
        held["fc"] = (yield [assemble(parts, table, shards, part)])[0]

    def proj_weights():
        got = lax.all_gather(cut(proj_part), "seq", axis=0, tiled=True)
        for _ in range(far):
            yield []
        got = after(got.reshape(shards, part, out_cols), rounds.mark)
        got = [got[:far], got[far:]]
        came = [over_batch(v, batches, batches // 2) for v in got]
        came[0] = (yield came[:1])[0]
        came[1] = (yield came[1:])[0]
        parts = {0: got, batches // 2: came}
        bit = batches // 4
        while bit:
            parts.update(
                {apart ^ bit: [over_batch(v, batches, bit) for v in p] for apart, p in parts.items()}
            )
            bit //= 2
        parts = [v for apart in range(batches) for v in parts[apart]]
        held["w_proj"] = (yield [assemble(parts, table, shards, part, 2)])[0]

    rounds.add(first_weights())
    rounds.add(fc_weights())
    rounds.add(proj_weights())
    token_blocks = [block for (block,) in ring.gather([own_tokens])]
    while "qkv" not in held:
        rounds.end(lambda: [])
    w_qkv = held["qkv"]
    small = held["small"].reshape(shards, -1)
    gain_one = row(small[:, :part])
    shift_one = row(small[:, part : 2 * part])
    bias_qv = small[:, 2 * part : 4 * part].reshape(2 * width)
    b_proj = row(small[:, 4 * part : 5 * part])
    gain_two = row(small[:, 5 * part : 6 * part])
    shift_two = row(small[:, 6 * part : 7 * part])
    b_out = row(small[:, 7 * part : 8 * part])
    bias_row = jnp.concatenate([bias_qv[:width], jnp.zeros((width,), BF), bias_qv[width:]])
    bias_heads = jnp.pad(
        bias_row.reshape(3, head_count, HEAD_DIM), ((0, 0), (0, padded - head_count), (0, 0))
    )
    bias_heads = jnp.swapaxes(bias_heads, 0, 1).reshape(1, padded * HEAD_COLS)
    bias_slice = lax.dynamic_slice_in_dim(bias_heads, me * slice_cols, slice_cols, 1).astype(F32)
    cot_blocks = [own_cot] * shards

    def cotangents():
        right = left = after(own_cot, rounds.mark)
        for step in range(1, far + 1):
            came = yield ring.both([right], [left] if step < shards - step else [])
            right = cot_blocks[shards - step] = came[0]
            if step < shards - step:
                left = cot_blocks[step] = came[1]

    rounds.add(cotangents())

    def project():
        return call(
            functools.partial(project_kernel, shards),
            table,
            [gain_one, shift_one, bias_slice, w_qkv, *token_blocks],
            [
                shape_of((length, width), BF),
                shape_of((length, slice_cols), BF),
                shape_of((length, width), BF),
            ],
            us=11,
            name="project",
        )

    normed_one, projected, xhat_one = rounds.end(project)
    attended_heads, attended_full, log_total = rounds.end(lambda: attention_forward(projected, table, heads))
    (attended_heads,) = rounds.end(
        lambda: [
            swap_blocks(
                attended_heads.reshape(shards, span, heads * HEAD_DIM)
            )
        ]
    )
    while "w_proj" not in held:
        rounds.end(lambda: [])
    w_proj = held["w_proj"]
    attended, mixed, normed_two = call(
        functools.partial(mix_kernel, shards),
        table,
        [own_tokens, w_proj, b_proj, gain_two, shift_two, attended_heads],
        [shape_of((span, width), BF), shape_of((span, width), F32), shape_of((span, width), BF)],
        scratch=[pltpu.VMEM((span, padded * HEAD_DIM), BF)],
        us=6,
        name="mix",
    )

    held["normed_two"] = normed_two
    gathered = {}

    def batch_rows(value, name, flag):
        while flag not in held:
            yield []
        value = after(value, rounds.mark)
        gathered[name] = yield from batch_gather_steps(value, batches)

    rounds.add(batch_rows(attended, "attended", "mlp"))
    normed_blocks = [block for (block,) in ring.gather([normed_two])]
    while "fc" not in held:
        rounds.end(lambda: [])
    w_fc = held["fc"]
    activated, hidden_low, fc_sums, out_rows, g_two = mlp_part(
        normed_blocks, cot_blocks, w_fc, row(fc_bias), out_weight, table
    )

    shares = functools.partial(weight_shares, table=table, shards=shards, batches=batches)

    def near_sums(found):
        came = yield [over_batch(found[apart ^ 1], batches, 1) for apart in range(0, batches, 2)]
        return [add(found[2 * i], c) for i, c in enumerate(came)]

    def far_sum(kept):
        came = yield [over_batch(kept[1], batches, 2)]
        return add(kept[0], came[0])

    def fc_gradient():
        yield []
        yield []
        found = yield shares(
            normed_blocks, hidden_low, row_blocks=shards, name="fc_grad", wait=[rounds.mark]
        )
        kept = yield from near_sums(found)
        yield []
        yield []
        came = over_batch(after(kept[1], rounds.mark), batches, 2)
        share = add(kept[0], *(yield [came]))
        share = swap_blocks(share)
        yield []
        (share,) = yield [share]
        for _ in range(far - 1):
            yield []
        held["fc_grad"] = (yield [swap_blocks(after(share, rounds.mark), "batch")])[0]

    def out_gradient():
        yield []
        yield []
        yield []
        found = yield shares(activated, cot_blocks, row_blocks=1, name="out_grad", wait=[rounds.mark])
        yield []
        kept = yield from near_sums(found)
        while "unproject" not in held:
            yield []
        came = over_batch(after(kept[1], rounds.mark), batches, 2)
        yield []
        held["out_grad"] = add(kept[0], *(yield [came]))

    def out_result():
        yield []
        (total,) = yield [join(out_rows, table, [rounds.mark])]
        for _ in range(far - 2):
            yield []
        total = cut(after(total, rounds.mark))
        held["out"] = lax.psum_scatter(total, "seq", scatter_dimension=0, tiled=True)

    held["mlp"] = True
    rounds.add(out_result())
    rounds.add(fc_gradient())
    rounds.add(out_gradient())
    g_two = ring.scatter_sum(g_two)

    def unmix():
        return call(
            functools.partial(unmix_kernel, shards),
            table,
            [*g_two, mixed, own_cot, w_proj, gain_two],
            [
                shape_of((span, width), F32),
                shape_of((span, width), BF),
                shape_of((3, width), F32),
                shape_of((shards, span, heads * HEAD_DIM), BF),
            ],
            scratch=[pltpu.VMEM((span, padded * HEAD_DIM), BF)],
            us=7,
            name="unmix",
        )

    grad_mixed, mixed_low, norm_sums, grad_messages = rounds.end(unmix)

    rounds.add(batch_rows(mixed_low, "mixed_low", "mlp"))
    (grad_heads,) = rounds.end(lambda: [swap_blocks(grad_messages)])
    held["grad_heads"] = grad_heads
    grad_projected, column_sums = rounds.end(
        lambda: attention_backward(
            projected, grad_heads.reshape(length, -1), attended_full, log_total, table, heads, []
        )
    )
    held["qkv_found"] = shares([normed_one], [grad_projected], row_blocks=shards, name="qkv_grad")
    qkv_near = rounds.end(
        lambda: [over_batch(held["qkv_found"][apart ^ 1], batches, 1) for apart in range(0, batches, 2)]
    )
    proj_blocks = proj_grad(gathered["attended"], gathered["mixed_low"], table, shards, span)
    share_cols = 3 * width // batches

    def overlaps(source, target):
        found = []
        for shard in range(shards):
            at = 0
            for first, size in head_ranges(shard, source):
                if first is not None:
                    low = max(first, target * share_cols)
                    high = min(first + size, (target + 1) * share_cols)
                    if low < high:
                        found.append((shard, at + low - first, low - target * share_cols, high - low))
                at += size
        return found

    most = max(sum(o[3] for o in overlaps(q, b)) for q in range(batches) for b in range(batches))
    most = -(-most // 128) * 128

    def outgoing(b):
        copies = []
        for target in range(batches):
            at = 0
            for shard, first, _, size in overlaps(b, target):
                copies.append((shard, first, target, at, size))
                at += size
        return copies

    def incoming(b):
        copies = []
        for source in range(batches):
            at = 0
            for _, _, to, size in overlaps(source, b):
                copies.append((source, at, 0, to, size))
                at += size
        return copies

    def qkv_gradient():
        kept = [add(held["qkv_found"][2 * i], c) for i, c in enumerate(qkv_near)]
        share = yield from far_sum(kept)
        share = swap_blocks(share)
        yield []
        (share,) = yield [share]
        share = copy_columns(share, table, shards, batches, (batches, part, most), BF, outgoing)
        (share,) = yield [swap_blocks(share, "batch")]
        held["qkv_grad"] = copy_columns(share, table, shards, batches, (1, part, share_cols), F32, incoming)[0]

    rounds.add(qkv_gradient())

    cot_sums = jnp.sum(own_cot.astype(F32), axis=0, keepdims=True)

    def unproject():
        return call(
            functools.partial(unproject_kernel, shards, batches, heads),
            table,
            [grad_projected, w_qkv, xhat_one, norm_sums, cot_sums, column_sums, *proj_blocks],
            [shape_of((span + proj_blocks[0].shape[0], width), BF)] * shards,
            scratch=[
                pltpu.VMEM((2, width), F32),
                pltpu.VMEM((length, width), BF),
                pltpu.VMEM((shards, 1, width), F32),
            ],
            us=9,
            name="unproject",
        )

    g_one = rounds.end(unproject)
    held["unproject"] = True
    rounds.waits.append(held["out"])
    total = sum(term.astype(F32) for term in ring.scatter_sum(g_one))
    g_one, pieces = total[:span], -(-part // batches)
    proj_share = [total[span : span + pieces, b * out_cols : (b + 1) * out_cols] for b in range(batches)]
    proj_share = jnp.concatenate(proj_share)[:part]
    xhat, inverse = norm_stats(own_tokens.astype(F32))
    block_out = (mixed + b_out + held["out"].reshape(span, width).astype(F32)).astype(BF)
    input_grad = (grad_mixed + norm_back(g_one, xhat, inverse, gain_one)).astype(BF)

    def vector_gradients():
        sums = jnp.concatenate([total[-1:, : 8 * part], fc_sums], axis=1)
        bit = 1
        while bit < batches:
            (came,) = yield [lax.ppermute(sums, "batch", [(b, b ^ bit) for b in range(batches)])]
            sums = sums + came
            bit *= 2
        held["sums"] = sums[0]

    rounds.add(vector_gradients())
    rounds.finish()

    runs = shards // batches

    def fc_copies(b):
        return [
            (q * runs + run, 0, 0, (run * batches + q) * fc_quarter, fc_quarter)
            for q in range(batches)
            for run in range(runs)
        ]

    fc_share = held["fc_grad"]
    fc_share = copy_columns(fc_share, table, shards, batches, (1, part, runs * units), F32, fc_copies)[0]
    sums = held["sums"]
    vectors = [sums[i * part : (i + 1) * part] for i in range(6)]
    return (
        block_out[None],
        input_grad[None],
        vectors[0],
        vectors[1],
        held["qkv_grad"],
        sums[6 * part : 8 * part],
        proj_share,
        vectors[4],
        vectors[2],
        vectors[3],
        fc_share,
        sums[8 * part : 8 * part + units],
        held["out_grad"][0].astype(F32),
        vectors[5],
    )


def solution(mesh):
    rows = P("batch", "seq", None)
    matrix, vector = P("seq", None), P("seq")
    shared = P("seq", "batch")
    return jax.shard_map(
        functools.partial(per_device, mesh.shape["seq"], mesh.shape["batch"]),
        mesh=mesh,
        in_specs=(
            rows, vector, vector, matrix, vector, matrix, vector,
            vector, vector, matrix, vector, matrix, vector, rows,
        ),
        out_specs=(
            rows, rows, vector, vector, shared, vector, shared,
            vector, vector, vector, shared, vector, shared, vector,
        ),
        check_vma=False,
    )
```

```python
import functools

import jax
import jax.numpy as jnp
from jax import lax
from jax.experimental import pallas as pl
from jax.experimental.pallas import tpu as pltpu
from jax.sharding import PartitionSpec as P

HEAD_DIM = 64
HEAD_COLS = 3 * HEAD_DIM
EPSILON = 1e-05
FLOOR_SCORE = -1e30
SCALE = HEAD_DIM**-0.5
BF = jnp.bfloat16
F32 = jnp.float32
VMEM_LIMIT = 56 << 20
MOST_ROWS = 1024
COST = 1.6e8


def dot_nn(a, b):
    return lax.dot_general(a, b, (((1,), (0,)), ((), ())), preferred_element_type=F32)


def dot_nt(a, b):
    return lax.dot_general(a, b, (((1,), (1,)), ((), ())), preferred_element_type=F32)


def dot_tn(a, b):
    return lax.dot_general(a, b, (((0,), (0,)), ((), ())), preferred_element_type=F32)


def shape_of(dims, kind):
    return jax.ShapeDtypeStruct(dims, kind)


def whole(*dims):
    return pl.BlockSpec(dims, lambda *_: (0,) * len(dims), pipeline_mode=pl.Buffered(1))


def call(
    kernel, table, operands, outs, scratch=(), name=None, us=1, in_specs=None, out_specs=None, grid=(1,), wait=()
):
    count, wait = 1 + len(operands), jax.tree.leaves(wait)

    def body(*refs):
        kernel(*refs[:count], *refs[count + len(wait) :])

    return pl.pallas_call(
        body,
        grid_spec=pltpu.PrefetchScalarGridSpec(
            num_scalar_prefetch=1,
            grid=grid,
            in_specs=(in_specs or [whole(*a.shape) for a in operands])
            + [pl.BlockSpec(memory_space=pl.ANY)] * len(wait),
            out_specs=out_specs or [whole(*o.shape) for o in outs],
            scratch_shapes=list(scratch),
        ),
        out_shape=list(outs),
        compiler_params=pltpu.CompilerParams(vmem_limit_bytes=VMEM_LIMIT),
        cost_estimate=pl.CostEstimate(flops=int(us * COST), bytes_accessed=1 << 16, transcendentals=0),
        name=name,
    )(table, *operands, *wait)


def steps(count, unrolled, body, carry):
    if unrolled:
        for j in range(count):
            carry = body(j, carry)
        return carry
    return lax.fori_loop(0, count, body, carry)


def rows_of(index, size):
    if isinstance(index, int):
        return pl.ds(index * size, size)
    return pl.ds(pl.multiple_of(index * size, size), size)


def causal(tile):
    key_pos = lax.broadcasted_iota(jnp.int32, (tile, tile), 0)
    query_pos = lax.broadcasted_iota(jnp.int32, (tile, tile), 1)
    return key_pos <= query_pos


def forward_kernel(tile, unrolled, table, x_ref, low_ref, full_ref, log_ref, value_t):
    tiles = x_ref.shape[0] // tile
    heads = range(2)
    cols = lambda head, kind: pl.ds(head * HEAD_COLS + kind * HEAD_DIM, HEAD_DIM)

    def turn(j, carry):
        for head in heads:
            value_t[head, j] = x_ref[rows_of(j, tile), cols(head, 2)].T
        return carry

    steps(tiles, unrolled, turn, 0)

    def query_tile(i, carry):
        rows = rows_of(i, tile)
        queries = [x_ref[rows, cols(head, 0)] * jnp.asarray(SCALE, BF) for head in heads]

        def add(j, states, masked):
            key_rows = rows_of(j, tile)
            scores = [dot_nt(x_ref[key_rows, cols(head, 1)], queries[head]) for head in heads]
            found = []
            for head in heads:
                (top, total, acc), score = states[head], scores[head]
                if masked:
                    score = jnp.where(causal(tile), score, FLOOR_SCORE)
                new_top = jnp.maximum(top, jnp.max(score, axis=0, keepdims=True))
                probs = jnp.exp(score - new_top)
                fade = jnp.exp(top - new_top)
                total = total * fade + jnp.sum(probs, axis=0, keepdims=True)
                acc = acc * fade + dot_nn(value_t[head, j], probs.astype(BF))
                found.append((new_top, total, acc))
            return tuple(found)

        state = (
            jnp.full((1, tile), FLOOR_SCORE, F32),
            jnp.zeros((1, tile), F32),
            jnp.zeros((HEAD_DIM, tile), F32),
        )
        states = steps(i, unrolled, lambda j, s: add(j, s, False), (state, state))
        for head, (top, total, acc) in enumerate(add(i, states, True)):
            result = (acc / total).T
            out_cols = pl.ds(head * HEAD_DIM, HEAD_DIM)
            low_ref[rows, out_cols] = result.astype(BF)
            full_ref[rows, out_cols] = result
            log_ref[0, pl.ds(head, 1), rows] = top + jnp.log(total)
        return carry

    steps(tiles, unrolled, query_tile, 0)


def backward_kernel(
    tile, unrolled, table, x_ref, grad_ref, full_ref, log_ref, dx_ref, sum_ref, key_t, key_acc, value_acc
):
    tiles = x_ref.shape[0] // tile
    heads = range(2)
    cols = lambda head, kind: pl.ds(head * HEAD_COLS + kind * HEAD_DIM, HEAD_DIM)

    def turn(j, carry):
        for head in heads:
            key_t[head, j] = x_ref[rows_of(j, tile), cols(head, 1)].T
        return carry

    steps(tiles, unrolled, turn, 0)
    key_acc[...] = jnp.zeros_like(key_acc)
    value_acc[...] = jnp.zeros_like(value_acc)

    def query_tile(i, query_sums):
        rows = rows_of(i, tile)
        queries, grads, deltas, logs = [], [], [], []
        for head in heads:
            out_cols = pl.ds(head * HEAD_DIM, HEAD_DIM)
            queries.append(x_ref[rows, cols(head, 0)] * jnp.asarray(SCALE, BF))
            grads.append(grad_ref[rows, out_cols])
            product = grads[head].astype(F32) * full_ref[rows, out_cols]
            deltas.append(jnp.sum(product.T, axis=0, keepdims=True))
            logs.append(log_ref[0, pl.ds(head, 1), rows])

        def add(j, accs, masked):
            key_rows = rows_of(j, tile)
            scores = [dot_nt(x_ref[key_rows, cols(head, 1)], queries[head]) for head in heads]
            grad_probs = [dot_nt(x_ref[key_rows, cols(head, 2)], grads[head]) for head in heads]
            found = []
            for head in heads:
                probs = jnp.exp(scores[head] - logs[head])
                if masked:
                    probs = jnp.where(causal(tile), probs, 0.0)
                grad_scores = (probs * (grad_probs[head] - deltas[head])).astype(BF)
                value_acc[head, key_rows, :] += dot_nn(probs.astype(BF), grads[head])
                key_acc[head, key_rows, :] += dot_nn(grad_scores, queries[head])
                found.append(accs[head] + dot_nn(key_t[head, j], grad_scores))
            return tuple(found)

        acc = jnp.zeros((HEAD_DIM, tile), F32)
        accs = steps(i, unrolled, lambda j, s: add(j, s, False), (acc, acc))
        sums = []
        for head, acc in enumerate(add(i, accs, True)):
            result = acc.T * SCALE
            dx_ref[rows, cols(head, 0)] = result.astype(BF)
            sums.append(query_sums[head] + jnp.sum(result, axis=0, keepdims=True))
        return tuple(sums)

    query_sums = steps(tiles, unrolled, query_tile, (jnp.zeros((1, HEAD_DIM), F32),) * 2)
    for head in heads:
        dx_ref[:, cols(head, 1)] = key_acc[head].astype(BF)
        dx_ref[:, cols(head, 2)] = value_acc[head].astype(BF)
        sum_ref[0, :, cols(head, 0)] = query_sums[head]
        sum_ref[0, :, cols(head, 1)] = jnp.sum(key_acc[head], axis=0, keepdims=True)
        sum_ref[0, :, cols(head, 2)] = jnp.sum(value_acc[head], axis=0, keepdims=True)


def attention_forward(projected, table, heads):
    length = projected.shape[0]
    tile = min(256, length)
    tiles, pairs = length // tile, heads // 2
    wide, narrow = 2 * HEAD_COLS, 2 * HEAD_DIM
    columns = lambda g, t: (0, g)
    return call(
        functools.partial(forward_kernel, tile, tiles <= 4),
        table,
        [projected],
        [
            shape_of((length, heads * HEAD_DIM), BF),
            shape_of((length, heads * HEAD_DIM), F32),
            shape_of((pairs, 2, length), F32),
        ],
        grid=(pairs,),
        in_specs=[pl.BlockSpec((length, wide), columns)],
        out_specs=[
            pl.BlockSpec((length, narrow), columns),
            pl.BlockSpec((length, narrow), columns),
            pl.BlockSpec((1, 2, length), lambda g, t: (g, 0, 0)),
        ],
        scratch=[pltpu.VMEM((2, tiles, HEAD_DIM, tile), BF)],
        us=15,
        name="attention_forward",
    )


def attention_backward(projected, grads, full, logs, table, heads, wait):
    length = projected.shape[0]
    tile = min(256, length)
    tiles, pairs = length // tile, heads // 2
    wide, narrow = 2 * HEAD_COLS, 2 * HEAD_DIM
    columns = lambda g, t: (0, g)
    return call(
        functools.partial(backward_kernel, tile, tiles <= 4),
        table,
        [projected, grads, full, logs],
        [shape_of((length, heads * HEAD_COLS), BF), shape_of((pairs, 1, wide), F32)],
        grid=(pairs,),
        in_specs=[
            pl.BlockSpec((length, wide), columns),
            pl.BlockSpec((length, narrow), columns),
            pl.BlockSpec((length, narrow), columns),
            pl.BlockSpec((1, 2, length), lambda g, t: (g, 0, 0)),
        ],
        out_specs=[
            pl.BlockSpec((length, wide), columns),
            pl.BlockSpec((1, 1, wide), lambda g, t: (g, 0, 0)),
        ],
        scratch=[
            pltpu.VMEM((2, tiles, HEAD_DIM, tile), BF),
            pltpu.VMEM((2, length, HEAD_DIM), F32),
            pltpu.VMEM((2, length, HEAD_DIM), F32),
        ],
        us=14,
        wait=wait,
        name="attention_backward",
    )


def norm_stats(rows):
    mean = jnp.mean(rows, axis=-1, keepdims=True)
    centred = rows - mean
    variance = jnp.mean(centred * centred, axis=-1, keepdims=True)
    inverse = lax.rsqrt(variance + EPSILON)
    return centred * inverse, inverse


def norm_back(grad, xhat, inverse, gain):
    h = grad * gain
    return inverse * (
        h - jnp.mean(h, axis=-1, keepdims=True) - xhat * jnp.mean(h * xhat, axis=-1, keepdims=True)
    )


ROOT = 0.7978845608028654
CUBE = 0.044715


def gelu_both(hidden):
    square = hidden * hidden
    bent = jnp.tanh(ROOT * hidden * (1.0 + CUBE * square))
    half = 0.5 * (1.0 + bent)
    slope = half + 0.5 * hidden * (1.0 - bent * bent) * ROOT * (1.0 + 3.0 * CUBE * square)
    return hidden * half, slope


def project_kernel(shards, table, gain, shift, bias, weight, *refs):
    blocks, (normed, projected, kept) = refs[:shards], refs[shards:]
    span = blocks[0].shape[0]
    for r in range(shards):
        normed[rows_of(table[r], span), :] = blocks[r][...]
    length = span * shards
    chunk = min(256, length)

    def some_rows(i, carry):
        rows = rows_of(i, chunk)
        xhat, _ = norm_stats(normed[rows, :].astype(F32))
        kept[rows, :] = xhat.astype(BF)
        normed[rows, :] = (xhat * gain[...] + shift[...]).astype(BF)
        projected[rows, :] = (dot_nn(normed[rows, :], weight[...]) + bias[...]).astype(BF)
        return carry

    lax.fori_loop(0, length // chunk, some_rows, 0)


def unproject_kernel(shards, batches, heads, table, grad, weight, xhat, norms, cots, head_sums, *refs):
    others, blocks, (sums, rows, vectors) = refs[:shards], refs[shards : 2 * shards], refs[2 * shards :]
    length = rows.shape[0]
    span, chunk = length // shards, min(256, length)
    sums[...] = jnp.zeros_like(sums)

    def some_rows(i, carry):
        at = rows_of(i, chunk)
        share = dot_nt(grad[at, :], weight[...])
        rows[at, :] = share.astype(BF)
        sums[0:1, :] += jnp.sum(share * xhat[at, :].astype(F32), axis=0, keepdims=True)
        sums[1:2, :] += jnp.sum(share, axis=0, keepdims=True)
        return carry

    lax.fori_loop(0, length // chunk, some_rows, 0)
    width = sums.shape[1]
    part = width // shards
    for s in range(shards):
        for i, source in enumerate([sums[0:1], sums[1:2], norms[0:1], norms[1:2], norms[2:3], cots[...]]):
            vectors[s, :, i * part : (i + 1) * part] = source[:, s * part : (s + 1) * part]
        vectors[s, :, 6 * part :] = jnp.zeros((1, width - 6 * part), F32)
    for s in range(shards):

        @pl.when(table[0] == s)
        def _(s=s):
            for first, shard, to, size in head_copies(s, shards, heads, width):
                pair, at = first
                vectors[shard, :, 6 * part + to : 6 * part + to + size] = head_sums[pair, :, at : at + size]

    last = others[0].shape[0] - 1
    for r in range(shards):
        blocks[r][:span, :] = rows[rows_of(table[r], span), :]
        blocks[r][span : span + last, :] = others[r][:last, :]
        blocks[r][span + last :, :] = vectors[table[r]].astype(BF)


def head_copies(shard, shards, heads, width):
    found, piece = [], 2 * width // shards
    for head in range(heads):
        number = shard * heads + head
        if (number + 1) * HEAD_DIM > width:
            continue
        for kind, base in ((0, 0), (2, width)):
            at, end = base + number * HEAD_DIM, base + (number + 1) * HEAD_DIM
            first = head % 2 * HEAD_COLS + kind * HEAD_DIM
            while at < end:
                size = min(end, (at // piece + 1) * piece) - at
                found.append(((head // 2, first), at // piece, at % piece, size))
                at, first = at + size, first + size
    return found


def mix_kernel(shards, table, tokens, weight, bias, gain, shift, heads, attended, mixed, normed, spread):
    cols, width = heads.shape[2], attended.shape[1]
    for s in range(shards):
        spread[:, s * cols : (s + 1) * cols] = heads[s]
    attended[...] = spread[:, :width]
    mixed[...] = tokens[...].astype(F32) + dot_nn(attended[...], weight[...]) + bias[...]
    xhat, _ = norm_stats(mixed[...])
    normed[...] = (xhat * gain[...] + shift[...]).astype(BF)


def unmix_kernel(shards, table, first, second, third, mixed, cotangent, weight, gain, *refs):
    grad_mixed, low, sums, pieces, spread = refs
    cols, (span, width) = pieces.shape[2], low.shape
    grad = first[...].astype(F32) + second[...].astype(F32) + third[...].astype(F32)
    xhat, inverse = norm_stats(mixed[...])
    full = cotangent[...].astype(F32) + norm_back(grad, xhat, inverse, gain[...])
    grad_mixed[...] = full
    low[...] = full.astype(BF)
    sums[0:1, :] = jnp.sum(grad * xhat, axis=0, keepdims=True)
    sums[1:2, :] = jnp.sum(grad, axis=0, keepdims=True)
    sums[2:3, :] = jnp.sum(full, axis=0, keepdims=True)
    spread[:, width:] = jnp.zeros_like(spread[:, width:])
    spread[:, :width] = dot_nt(low[...], weight[...]).astype(BF)
    for s in range(shards):
        pieces[s] = spread[:, s * cols : (s + 1) * cols]


def mlp_kernel(shards, group, table, fc, bias, out, *refs):
    blocks, cotangents, refs = refs[:shards], refs[shards : 2 * shards], refs[2 * shards :]
    act, low, sums, results = refs[:4]
    shares, refs = refs[4 : 4 + shards], refs[4 + shards :]
    fc_in, out_in, normed, cots, act_here, low_here, results_here, shares_here, came, left = refs
    span = blocks[0].shape[0]
    pairs = [(fc, fc_in), (out, out_in)]
    for r in range(shards):
        pairs += [(blocks[r], normed.at[r]), (cotangents[r], cots.at[r])]
    copies = [pltpu.make_async_copy(a, b, came.at[i]) for i, (a, b) in enumerate(pairs)]
    for i in [0, *range(2, 2 + 2 * group), 1, *range(2 + 2 * group, len(copies))]:
        copies[i].start()
    copies[0].wait()
    sums[...] = jnp.zeros_like(sums)
    sent = []

    def send(source, target):
        copy = pltpu.make_async_copy(source, target, left.at[len(sent)])
        copy.start()
        sent.append(copy)

    for first in range(0, shards, group):
        places = range(first, first + group)
        rows = pl.ds(first * span, group * span)
        some = pl.ds(first, group)
        for r in places:
            copies[2 + 2 * r].wait()
            copies[3 + 2 * r].wait()
        flat = lambda ref: ref[some].reshape(group * span, ref.shape[2])
        hidden = dot_nn(flat(normed), fc_in[...]) + bias[...]
        activated, slope = gelu_both(hidden)
        act_here[rows, :] = activated.astype(BF)
        if not first:
            copies[1].wait()
        grad = dot_nt(flat(cots), out_in[...]) * slope
        sums[...] += jnp.sum(grad, axis=0, keepdims=True)
        low_here[rows, :] = grad.astype(BF)
        share = dot_nt(low_here[rows, :], fc_in[...]).astype(BF)
        shares_here[some] = share.reshape(group, span, share.shape[1])
        for r in places:
            send(shares_here.at[r], shares[r])
        send(act_here.at[rows, :], act.at[rows, :])
        send(low_here.at[rows, :], low.at[rows, :])
        result = dot_nn(act_here[rows, :], out_in[...]).astype(BF)
        results_here[some] = result.reshape(group, span, result.shape[1])
        send(results_here.at[some], results.at[some])
    for copy in sent:
        copy.wait()


def mlp_part(blocks, cotangents, fc, bias, out, table):
    shards = len(blocks)
    span, width = blocks[0].shape
    rows, units = shards * span, fc.shape[1]
    if rows > MOST_ROWS:
        half = shards // 2
        halves = [mlp_part(blocks[i:][:half], cotangents[i:][:half], fc, bias, out, table) for i in (0, half)]
        first, second = halves
        results = jnp.concatenate([first[3], second[3]])
        return first[0] + second[0], first[1] + second[1], first[2] + second[2], results, first[4] + second[4]
    group = min(shards, max(1, 256 // span))
    rows_at = lambda cols: pl.BlockSpec((group * span, cols), lambda g, t: (g, 0))
    anywhere = pl.BlockSpec(memory_space=pl.ANY)
    stack = pltpu.VMEM((shards, span, width), BF)
    got = call(
        functools.partial(mlp_kernel, shards, group),
        table,
        [fc, bias, out, *blocks, *cotangents],
        [shape_of((rows, units), BF)] * 2
        + [shape_of((1, units), F32), shape_of((shards, span, width), BF)]
        + [shape_of((span, width), BF)] * shards,
        grid=(1,),
        in_specs=[anywhere, whole(1, units)] + [anywhere] * (1 + 2 * shards),
        out_specs=[anywhere, anywhere, whole(1, units)] + [anywhere] * (1 + shards),
        scratch=[
            pltpu.VMEM(fc.shape, BF),
            pltpu.VMEM(out.shape, BF),
            stack,
            stack,
            pltpu.VMEM((rows, units), BF),
            pltpu.VMEM((rows, units), BF),
            stack,
            stack,
            pltpu.SemaphoreType.DMA((2 + 2 * shards,)),
            pltpu.SemaphoreType.DMA((shards + 3 * (shards // group),)),
        ],
        us=18,
        name="mlp",
    )
    return got[:1], got[1:2], got[2], got[3], got[4:]


def take_rows(pieces):
    found = []
    while pieces and sum(v.shape[0] for v in found) < MOST_ROWS:
        found.append(pieces.pop(0))
    return found


def weight_kernel(shards, batches, row_blocks, count, table, *refs):
    lefts, rights, refs = refs[:count], refs[count:-batches], refs[-batches:]
    left = jnp.concatenate([v[...] for v in lefts])
    right = jnp.concatenate([v[...] for v in rights])
    product = dot_tn(left, right).astype(BF)
    cols = product.shape[1] // batches
    size = product.shape[0] // row_blocks
    for member in range(batches):

        @pl.when(table[shards] == member)
        def _(member=member):
            for apart in range(batches):
                first = (member ^ apart) * cols
                for s in range(row_blocks):
                    refs[apart][s] = product[s * size : (s + 1) * size, first : first + cols]


def weight_shares(lefts, rights, table, shards, batches, row_blocks, name, wait=()):
    rows, cols = lefts[0].shape[1], rights[0].shape[1]
    dims = (row_blocks, rows // row_blocks, cols // batches)
    if sum(v.shape[0] for v in lefts) > MOST_ROWS:
        cut_rows = lambda vs: [v[i : i + MOST_ROWS] for v in vs for i in range(0, v.shape[0], MOST_ROWS)]
        total, lefts, rights = None, cut_rows(lefts), cut_rows(rights)
        while lefts:
            some = [take_rows(lefts), take_rows(rights)]
            found = weight_shares(*some, table, shards, batches, row_blocks, name, wait)
            total = found if total is None else [add(a, b) for a, b in zip(total, found)]
        return total
    return call(
        functools.partial(weight_kernel, shards, batches, row_blocks, len(lefts)),
        table,
        [*lefts, *rights],
        [shape_of(dims, BF)] * batches,
        us=9,
        wait=wait,
        name=name,
    )


def pack_kernel(shards, batches, ranges, table, weight, *refs):
    out, rows = refs[-1], weight.shape[0]
    for extra in refs[:-1]:
        count = (out.shape[1] - rows) // extra.shape[0]
        size = extra.shape[1] // count
        for shard in range(shards):
            for i in range(extra.shape[0]):
                for j in range(count):
                    at = rows + i * count + j
                    out[shard, at : at + 1, :size] = extra[i : i + 1, j * size : (j + 1) * size]
    for member in range(batches):

        @pl.when(table[shards] == member)
        def _(member=member):
            for shard in range(shards):
                at = 0
                for first, size in ranges(shard, member):
                    if first is None:
                        out[shard, :rows, at : at + size] = jnp.zeros((rows, size), BF)
                    else:
                        out[shard, :rows, at : at + size] = weight[:, first : first + size]
                    at += size


def pack(weight, table, shards, batches, cols, ranges, extra=(), wait=()):
    rows = weight.shape[0] + sum(v.shape[0] * -(-v.shape[1] // cols) for v in extra)
    return call(
        functools.partial(pack_kernel, shards, batches, ranges),
        table,
        [weight, *extra],
        [shape_of((shards, rows, cols), BF)],
        us=3.5,
        wait=wait,
        name="pack",
    )[0]


def assemble_kernel(shards, batches, rows, pieces, table, *refs):
    out = refs[-1]
    blocks, _, cols = refs[0].shape
    for member in range(batches):

        @pl.when(table[shards] == member)
        def _(member=member):
            for apart in range(batches):
                at = (member ^ apart) * cols
                for i in range(pieces * blocks):
                    source = refs[apart * pieces + i // blocks][i % blocks, :rows, :]
                    out[i * rows : (i + 1) * rows, at : at + cols] = source


def assemble(parts, table, shards, rows, pieces=1, wait=()):
    blocks, _, cols = parts[0].shape
    batches = len(parts) // pieces
    return call(
        functools.partial(assemble_kernel, shards, batches, rows, pieces),
        table,
        parts,
        [shape_of((pieces * blocks * rows, batches * cols), BF)],
        us=5,
        wait=wait,
        name="assemble",
    )[0]


def join_kernel(table, source, out):
    out[...] = source[...]


def join(source, table, wait):
    shards, rows, cols = source.shape
    return call(
        join_kernel,
        table,
        [source],
        [shape_of(source.shape, BF)],
        grid=(shards,),
        in_specs=[pl.BlockSpec((1, rows, cols), lambda g, t: (g, 0, 0))],
        out_specs=[pl.BlockSpec((1, rows, cols), lambda g, t: (t[g], 0, 0))],
        us=4,
        wait=wait,
        name="join",
    )[0]


def proj_grad_kernel(shards, batches, table, *refs):
    lefts, rights, refs = refs[:batches], refs[batches : 2 * batches], refs[2 * batches :]
    blocks, quarter, product = refs[:-2], refs[-2], refs[-1]
    span, cols = rights[0].shape[0], quarter.shape[1]
    for member in range(batches):

        @pl.when(table[shards] == member)
        def _(member=member):
            for i in range(batches):
                quarter[i * span : (i + 1) * span, :] = rights[i][:, member * cols : (member + 1) * cols]

    left = jnp.concatenate([v[...] for v in lefts])
    result = dot_tn(left, quarter[...]).astype(BF)
    rows = result.shape[0] // shards
    piece = -(-rows // batches)
    product[...] = jnp.zeros_like(product)
    for s in range(shards):
        for i in range(batches):
            size = min(piece, rows - i * piece)
            first = s * rows + i * piece
            product[s, :size, i * cols : (i + 1) * cols] = result[first : first + size, :]
    for r in range(shards):
        blocks[r][...] = product[table[r]]


def proj_grad(lefts, rights, table, shards, span):
    batches, rows = len(lefts), lefts[0].shape[1]
    width = rights[0].shape[1]
    piece = -(-(rows // shards) // batches)
    dims = (piece + 1 + -(span + piece + 1) % 8, width)
    return call(
        functools.partial(proj_grad_kernel, shards, batches),
        table,
        [*lefts, *rights],
        [shape_of(dims, BF)] * shards,
        scratch=[
            pltpu.VMEM((batches * lefts[0].shape[0], width // batches), BF),
            pltpu.VMEM((shards, *dims), BF),
        ],
        us=6,
        name="proj_grad",
    )


def copy_kernel(shards, batches, copies, table, source, out):
    for member in range(batches):

        @pl.when(table[shards] == member)
        def _(member=member):
            for block, first, to_block, to, size in copies(member):
                piece = source[block, :, first : first + size].astype(out.dtype)
                out[to_block, :, to : to + size] = piece


def copy_columns(source, table, shards, batches, dims, kind, copies):
    return call(
        functools.partial(copy_kernel, shards, batches, copies),
        table,
        [source],
        [shape_of(dims, kind)],
        us=4,
        name="copy_columns",
    )[0]


def cut(value):
    rows = value.shape[-2]
    if rows % 8:
        return value
    groups = max(g for g in range(1, 33) if rows // 8 % g == 0)
    return value.reshape(*value.shape[:-2], rows // 8 // groups, groups, 8, value.shape[-1])


def permute(value, axis, pairs):
    return lax.ppermute(cut(value), axis, pairs).reshape(value.shape)


def gate_kernel(count, total, *refs):
    outs = refs[-total:]
    for i in range(count):
        outs[i][...] = (refs[i][...].astype(F32) + refs[total + i][...].astype(F32)).astype(BF)


def gate(values, *others, parts=()):
    values, others, parts = list(values), jax.tree.leaves(others), list(parts)
    if not values:
        return []
    count, total = len(parts), len(values)
    anywhere = pl.BlockSpec(memory_space=pl.ANY)
    blocks = [pl.BlockSpec(memory_space=pltpu.VMEM)] * count
    return pl.pallas_call(
        functools.partial(gate_kernel, count, total),
        in_specs=blocks + [anywhere] * (total - count) + blocks + [anywhere] * len(others),
        out_specs=blocks + [anywhere] * (total - count),
        out_shape=[shape_of(v.shape, v.dtype) for v in values],
        input_output_aliases={i: i for i in range(count, total)},
        name="gate",
    )(*values, *parts, *others)


def after(value, *others):
    return gate([value], *others)[0]


class Rounds:
    def __init__(self):
        self.chains, self.mark, self.waits = [], None, []

    def add(self, chain):
        self.chains.append([chain, None])

    def end(self, start, parts=()):
        pending, alive = [], []
        for chain, gated in self.chains:
            try:
                pending.append(list(chain.send(gated)))
                alive.append(chain)
            except StopIteration:
                pass
        values = list(start())
        out = gate(values + [v for p in pending for v in p], self.waits, parts=parts)
        self.waits = []
        at, self.chains = len(values), []
        for chain, p in zip(alive, pending):
            self.chains.append([chain, out[at : at + len(p)]])
            at += len(p)
        if out:
            self.mark = out[0]
        return out[: len(values)]

    def finish(self):
        while self.chains:
            self.end(lambda: [])


class Ring:
    def __init__(self, size, rounds):
        self.size, self.rounds = size, rounds
        self.order = list(range(0, size, 2)) + list(range(size - 1, 0, -2))

    def shift(self, value, by):
        pairs = [(self.order[i], self.order[(i + by) % self.size]) for i in range(self.size)]
        return permute(value, "seq", pairs)

    def both(self, right, left):
        return [self.shift(v, 1) for v in right] + [self.shift(v, -1) for v in left]

    def gather(self, value):
        got = [value] * self.size
        right = left = value
        for far in range(1, self.size // 2 + 1):
            left = left if far < self.size - far else []
            came = self.rounds.end(lambda: self.both(right, left))
            right, left = came[: len(value)], came[len(value) :]
            got[self.size - far] = right
            if left:
                got[far] = left
        return got

    def scatter_sum(self, parts):
        size = self.size
        right, left = [parts[size // 2]], []
        for far in range(size // 2 - 1, -1, -1):
            adds = [] if not far else [parts[far]] + [parts[size - far]] * len(left)
            right, *left = self.rounds.end(lambda: self.both(right, left), adds)
            right = [right]
            if far and not left:
                left = [parts[size - far]]
        return right[0], left[0], parts[0]


def add(a, b):
    return (a.astype(F32) + b.astype(F32)).astype(BF)


def swap_blocks(value, axis="seq"):
    return lax.all_to_all(cut(value), axis, 0, 0, tiled=True).reshape(value.shape)


def over_batch(value, batches, apart):
    return permute(value, "batch", [(b, b ^ apart) for b in range(batches)])


def batch_gather_steps(value, batches):
    parts, bit = {0: value}, batches // 2
    while bit:
        came = {apart ^ bit: over_batch(part, batches, bit) for apart, part in parts.items()}
        parts.update(zip(came, (yield list(came.values()))))
        bit //= 2
    return [parts[apart] for apart in range(batches)]


def per_device(
    shards,
    batches,
    tokens,
    ln1_gain,
    ln1_bias,
    qkv_weight,
    qv_bias,
    proj_weight,
    proj_bias,
    ln2_gain,
    ln2_bias,
    fc_weight,
    fc_bias,
    out_weight,
    out_bias,
    cotangent,
):
    _, span, width = tokens.shape
    head_count = width // HEAD_DIM
    heads = -(-head_count // shards)
    heads += heads % 2
    padded = heads * shards
    length = span * shards
    units = fc_bias.shape[0]
    part = width // shards
    me, member = lax.axis_index("seq"), lax.axis_index("batch")
    rounds = Rounds()
    ring = Ring(shards, rounds)
    place = jnp.where(me % 2 == 0, me // 2, shards - 1 - me // 2)
    place = (place + jnp.arange(shards, dtype=jnp.int32)) % shards
    order = jnp.where(place < shards // 2, 2 * place, 2 * shards - 2 * place - 1)
    table = jnp.concatenate([order, member[None]]).astype(jnp.int32)
    row = lambda v: v.reshape(1, -1).astype(F32)

    slice_cols = heads * HEAD_COLS
    quarter = slice_cols // batches
    fc_quarter = units // batches

    def head_ranges(shard, b):
        found = []
        for col in range(shard * slice_cols + b * quarter, shard * slice_cols + (b + 1) * quarter):
            head, kind, at = col // HEAD_COLS, col % HEAD_COLS // HEAD_DIM, col % HEAD_DIM
            first = kind * width + head * HEAD_DIM + at if head < head_count else None
            if found and first is not None and found[-1][0] is not None and first == sum(found[-1]):
                found[-1] = (found[-1][0], found[-1][1] + 1)
            elif found and first is None and found[-1][0] is None:
                found[-1] = (None, found[-1][1] + 1)
            else:
                found.append((first, 1))
        return found

    def fc_ranges(shard, b):
        return [(shard * units + b * fc_quarter, fc_quarter)]

    own_tokens, own_cot = tokens[0], cotangent[0]
    far = shards // 2
    out_cols = width // batches
    out_cols = width // batches
    proj_part = lax.dynamic_slice_in_dim(proj_weight, member * out_cols, out_cols, 1)
    small = jnp.stack(
        [ln1_gain, ln1_bias, qv_bias[:part], qv_bias[part:], proj_bias, ln2_gain, ln2_bias, out_bias]
    )
    packed = pack(qkv_weight, table, shards, batches, quarter, head_ranges, [small])
    held = {}

    def first_weights():
        (got,) = yield [swap_blocks(packed)]
        held["small"] = got[:, part:, : part // ((got.shape[1] - part) // 8)]
        parts = yield from batch_gather_steps(got, batches)
        held["qkv"] = assemble(parts, table, shards, part)
        rounds.waits.append(held["qkv"])

    far = shards // 2

    def fc_weights():
        yield []
        got = pack(fc_weight, table, shards, batches, fc_quarter, fc_ranges, wait=[rounds.mark])
        (got,) = yield [got]
        for _ in range(far - 2):
            yield []
        (got,) = yield [swap_blocks(after(got, rounds.mark))]
        while "normed_two" not in held:
            yield []
        got = after(got, rounds.mark)
        came = over_batch(got, batches, batches // 2)
        yield []
        parts = {0: got, batches // 2: (yield [came])[0]}
        bit = batches // 4
        while bit:
            came = {apart ^ bit: over_batch(p, batches, bit) for apart, p in parts.items()}
            parts.update(zip(came, (yield list(came.values()))))
            bit //= 2
        parts = [parts[apart] for apart in range(batches)]
        held["fc"] = (yield [assemble(parts, table, shards, part)])[0]

    def proj_weights():
        got = lax.all_gather(cut(proj_part), "seq", axis=0, tiled=True)
        for _ in range(far):
            yield []
        got = after(got.reshape(shards, part, out_cols), rounds.mark)
        got = [got[:far], got[far:]]
        came = [over_batch(v, batches, batches // 2) for v in got]
        came[0] = (yield came[:1])[0]
        came[1] = (yield came[1:])[0]
        parts = {0: got, batches // 2: came}
        bit = batches // 4
        while bit:
            parts.update(
                {apart ^ bit: [over_batch(v, batches, bit) for v in p] for apart, p in parts.items()}
            )
            bit //= 2
        parts = [v for apart in range(batches) for v in parts[apart]]
        held["w_proj"] = (yield [assemble(parts, table, shards, part, 2)])[0]

    rounds.add(first_weights())
    rounds.add(fc_weights())
    rounds.add(proj_weights())
    token_blocks = [block for (block,) in ring.gather([own_tokens])]
    while "qkv" not in held:
        rounds.end(lambda: [])
    w_qkv = held["qkv"]
    small = held["small"].reshape(shards, -1)
    gain_one = row(small[:, :part])
    shift_one = row(small[:, part : 2 * part])
    bias_qv = small[:, 2 * part : 4 * part].reshape(2 * width)
    b_proj = row(small[:, 4 * part : 5 * part])
    gain_two = row(small[:, 5 * part : 6 * part])
    shift_two = row(small[:, 6 * part : 7 * part])
    b_out = row(small[:, 7 * part : 8 * part])
    bias_row = jnp.concatenate([bias_qv[:width], jnp.zeros((width,), BF), bias_qv[width:]])
    bias_heads = jnp.pad(
        bias_row.reshape(3, head_count, HEAD_DIM), ((0, 0), (0, padded - head_count), (0, 0))
    )
    bias_heads = jnp.swapaxes(bias_heads, 0, 1).reshape(1, padded * HEAD_COLS)
    bias_slice = lax.dynamic_slice_in_dim(bias_heads, me * slice_cols, slice_cols, 1).astype(F32)
    cot_blocks = [own_cot] * shards

    def cotangents():
        right = left = after(own_cot, rounds.mark)
        for step in range(1, far + 1):
            came = yield ring.both([right], [left] if step < shards - step else [])
            right = cot_blocks[shards - step] = came[0]
            if step < shards - step:
                left = cot_blocks[step] = came[1]

    rounds.add(cotangents())

    def project():
        return call(
            functools.partial(project_kernel, shards),
            table,
            [gain_one, shift_one, bias_slice, w_qkv, *token_blocks],
            [
                shape_of((length, width), BF),
                shape_of((length, slice_cols), BF),
                shape_of((length, width), BF),
            ],
            us=11,
            name="project",
        )

    normed_one, projected, xhat_one = rounds.end(project)
    attended_heads, attended_full, log_total = rounds.end(lambda: attention_forward(projected, table, heads))
    (attended_heads,) = rounds.end(
        lambda: [
            swap_blocks(
                attended_heads.reshape(shards, span, heads * HEAD_DIM)
            )
        ]
    )
    while "w_proj" not in held:
        rounds.end(lambda: [])
    w_proj = held["w_proj"]
    attended, mixed, normed_two = call(
        functools.partial(mix_kernel, shards),
        table,
        [own_tokens, w_proj, b_proj, gain_two, shift_two, attended_heads],
        [shape_of((span, width), BF), shape_of((span, width), F32), shape_of((span, width), BF)],
        scratch=[pltpu.VMEM((span, padded * HEAD_DIM), BF)],
        us=6,
        name="mix",
    )

    held["normed_two"] = normed_two
    gathered = {}

    def batch_rows(value, name, flag):
        while flag not in held:
            yield []
        value = after(value, rounds.mark)
        gathered[name] = yield from batch_gather_steps(value, batches)

    rounds.add(batch_rows(attended, "attended", "mlp"))
    normed_blocks = [block for (block,) in ring.gather([normed_two])]
    while "fc" not in held:
        rounds.end(lambda: [])
    w_fc = held["fc"]
    activated, hidden_low, fc_sums, out_rows, g_two = mlp_part(
        normed_blocks, cot_blocks, w_fc, row(fc_bias), out_weight, table
    )

    shares = functools.partial(weight_shares, table=table, shards=shards, batches=batches)

    def near_sums(found):
        came = yield [over_batch(found[apart ^ 1], batches, 1) for apart in range(0, batches, 2)]
        return [add(found[2 * i], c) for i, c in enumerate(came)]

    def far_sum(kept):
        came = yield [over_batch(kept[1], batches, 2)]
        return add(kept[0], came[0])

    def fc_gradient():
        yield []
        yield []
        found = yield shares(
            normed_blocks, hidden_low, row_blocks=shards, name="fc_grad", wait=[rounds.mark]
        )
        kept = yield from near_sums(found)
        yield []
        yield []
        came = over_batch(after(kept[1], rounds.mark), batches, 2)
        share = add(kept[0], *(yield [came]))
        share = swap_blocks(share)
        yield []
        (share,) = yield [share]
        for _ in range(far - 1):
            yield []
        held["fc_grad"] = (yield [swap_blocks(after(share, rounds.mark), "batch")])[0]

    def out_gradient():
        yield []
        yield []
        yield []
        found = yield shares(activated, cot_blocks, row_blocks=1, name="out_grad", wait=[rounds.mark])
        yield []
        kept = yield from near_sums(found)
        while "unproject" not in held:
            yield []
        came = over_batch(after(kept[1], rounds.mark), batches, 2)
        yield []
        held["out_grad"] = add(kept[0], *(yield [came]))

    def out_result():
        yield []
        (total,) = yield [join(out_rows, table, [rounds.mark])]
        for _ in range(far - 2):
            yield []
        total = cut(after(total, rounds.mark))
        held["out"] = lax.psum_scatter(total, "seq", scatter_dimension=0, tiled=True)

    held["mlp"] = True
    rounds.add(out_result())
    rounds.add(fc_gradient())
    rounds.add(out_gradient())
    g_two = ring.scatter_sum(g_two)

    def unmix():
        return call(
            functools.partial(unmix_kernel, shards),
            table,
            [*g_two, mixed, own_cot, w_proj, gain_two],
            [
                shape_of((span, width), F32),
                shape_of((span, width), BF),
                shape_of((3, width), F32),
                shape_of((shards, span, heads * HEAD_DIM), BF),
            ],
            scratch=[pltpu.VMEM((span, padded * HEAD_DIM), BF)],
            us=7,
            name="unmix",
        )

    grad_mixed, mixed_low, norm_sums, grad_messages = rounds.end(unmix)

    rounds.add(batch_rows(mixed_low, "mixed_low", "mlp"))
    (grad_heads,) = rounds.end(lambda: [swap_blocks(grad_messages)])
    held["grad_heads"] = grad_heads
    grad_projected, column_sums = rounds.end(
        lambda: attention_backward(
            projected, grad_heads.reshape(length, -1), attended_full, log_total, table, heads, []
        )
    )
    held["qkv_found"] = shares([normed_one], [grad_projected], row_blocks=shards, name="qkv_grad")
    qkv_near = rounds.end(
        lambda: [over_batch(held["qkv_found"][apart ^ 1], batches, 1) for apart in range(0, batches, 2)]
    )
    proj_blocks = proj_grad(gathered["attended"], gathered["mixed_low"], table, shards, span)
    share_cols = 3 * width // batches

    def overlaps(source, target):
        found = []
        for shard in range(shards):
            at = 0
            for first, size in head_ranges(shard, source):
                if first is not None:
                    low = max(first, target * share_cols)
                    high = min(first + size, (target + 1) * share_cols)
                    if low < high:
                        found.append((shard, at + low - first, low - target * share_cols, high - low))
                at += size
        return found

    most = max(sum(o[3] for o in overlaps(q, b)) for q in range(batches) for b in range(batches))
    most = -(-most // 128) * 128

    def outgoing(b):
        copies = []
        for target in range(batches):
            at = 0
            for shard, first, _, size in overlaps(b, target):
                copies.append((shard, first, target, at, size))
                at += size
        return copies

    def incoming(b):
        copies = []
        for source in range(batches):
            at = 0
            for _, _, to, size in overlaps(source, b):
                copies.append((source, at, 0, to, size))
                at += size
        return copies

    def qkv_gradient():
        kept = [add(held["qkv_found"][2 * i], c) for i, c in enumerate(qkv_near)]
        share = yield from far_sum(kept)
        share = swap_blocks(share)
        yield []
        (share,) = yield [share]
        share = copy_columns(share, table, shards, batches, (batches, part, most), BF, outgoing)
        (share,) = yield [swap_blocks(share, "batch")]
        held["qkv_grad"] = copy_columns(share, table, shards, batches, (1, part, share_cols), F32, incoming)[0]

    rounds.add(qkv_gradient())

    cot_sums = jnp.sum(own_cot.astype(F32), axis=0, keepdims=True)

    def unproject():
        return call(
            functools.partial(unproject_kernel, shards, batches, heads),
            table,
            [grad_projected, w_qkv, xhat_one, norm_sums, cot_sums, column_sums, *proj_blocks],
            [shape_of((span + proj_blocks[0].shape[0], width), BF)] * shards,
            scratch=[
                pltpu.VMEM((2, width), F32),
                pltpu.VMEM((length, width), BF),
                pltpu.VMEM((shards, 1, width), F32),
            ],
            us=9,
            name="unproject",
        )

    g_one = rounds.end(unproject)
    held["unproject"] = True
    rounds.waits.append(held["out"])
    total = sum(term.astype(F32) for term in ring.scatter_sum(g_one))
    g_one, pieces = total[:span], -(-part // batches)
    proj_share = [total[span : span + pieces, b * out_cols : (b + 1) * out_cols] for b in range(batches)]
    proj_share = jnp.concatenate(proj_share)[:part]
    xhat, inverse = norm_stats(own_tokens.astype(F32))
    block_out = (mixed + b_out + held["out"].reshape(span, width).astype(F32)).astype(BF)
    input_grad = (grad_mixed + norm_back(g_one, xhat, inverse, gain_one)).astype(BF)

    def vector_gradients():
        sums = jnp.concatenate([total[-1:, : 8 * part], fc_sums], axis=1)
        came = yield [
            lax.ppermute(sums, "batch", [(b, b ^ apart) for b in range(batches)])
            for apart in range(1, batches)
        ]
        sums = sums + sum(came)
        held["sums"] = sums[0]

    rounds.add(vector_gradients())
    rounds.finish()

    runs = shards // batches

    def fc_copies(b):
        return [
            (q * runs + run, 0, 0, (run * batches + q) * fc_quarter, fc_quarter)
            for q in range(batches)
            for run in range(runs)
        ]

    fc_share = held["fc_grad"]
    fc_share = copy_columns(fc_share, table, shards, batches, (1, part, runs * units), F32, fc_copies)[0]
    sums = held["sums"]
    vectors = [sums[i * part : (i + 1) * part] for i in range(6)]
    return (
        block_out[None],
        input_grad[None],
        vectors[0],
        vectors[1],
        held["qkv_grad"],
        sums[6 * part : 8 * part],
        proj_share,
        vectors[4],
        vectors[2],
        vectors[3],
        fc_share,
        sums[8 * part : 8 * part + units],
        held["out_grad"][0].astype(F32),
        vectors[5],
    )


def solution(mesh):
    rows = P("batch", "seq", None)
    matrix, vector = P("seq", None), P("seq")
    shared = P("seq", "batch")
    return jax.shard_map(
        functools.partial(per_device, mesh.shape["seq"], mesh.shape["batch"]),
        mesh=mesh,
        in_specs=(
            rows, vector, vector, matrix, vector, matrix, vector,
            vector, vector, matrix, vector, matrix, vector, rows,
        ),
        out_specs=(
            rows, rows, vector, vector, shared, vector, shared,
            vector, vector, vector, shared, vector, shared, vector,
        ),
        check_vma=False,
    )
```

```python
import functools

import jax
import jax.numpy as jnp
from jax import lax
from jax.experimental import pallas as pl
from jax.experimental.pallas import tpu as pltpu
from jax.sharding import PartitionSpec as P

HEAD_DIM = 64
HEAD_COLS = 3 * HEAD_DIM
EPSILON = 1e-05
FLOOR_SCORE = -1e30
SCALE = HEAD_DIM**-0.5
BF = jnp.bfloat16
F32 = jnp.float32
VMEM_LIMIT = 56 << 20
MOST_ROWS = 1024
COST = 1.6e8


def dot_nn(a, b):
    return lax.dot_general(a, b, (((1,), (0,)), ((), ())), preferred_element_type=F32)


def dot_nt(a, b):
    return lax.dot_general(a, b, (((1,), (1,)), ((), ())), preferred_element_type=F32)


def dot_tn(a, b):
    return lax.dot_general(a, b, (((0,), (0,)), ((), ())), preferred_element_type=F32)


def shape_of(dims, kind):
    return jax.ShapeDtypeStruct(dims, kind)


def whole(*dims):
    return pl.BlockSpec(dims, lambda *_: (0,) * len(dims), pipeline_mode=pl.Buffered(1))


def call(
    kernel, table, operands, outs, scratch=(), name=None, us=1, in_specs=None, out_specs=None, grid=(1,), wait=()
):
    count, wait = 1 + len(operands), jax.tree.leaves(wait)

    def body(*refs):
        kernel(*refs[:count], *refs[count + len(wait) :])

    return pl.pallas_call(
        body,
        grid_spec=pltpu.PrefetchScalarGridSpec(
            num_scalar_prefetch=1,
            grid=grid,
            in_specs=(in_specs or [whole(*a.shape) for a in operands])
            + [pl.BlockSpec(memory_space=pl.ANY)] * len(wait),
            out_specs=out_specs or [whole(*o.shape) for o in outs],
            scratch_shapes=list(scratch),
        ),
        out_shape=list(outs),
        compiler_params=pltpu.CompilerParams(vmem_limit_bytes=VMEM_LIMIT),
        cost_estimate=pl.CostEstimate(flops=int(us * COST), bytes_accessed=1 << 16, transcendentals=0),
        name=name,
    )(table, *operands, *wait)


def steps(count, unrolled, body, carry):
    if unrolled:
        for j in range(count):
            carry = body(j, carry)
        return carry
    return lax.fori_loop(0, count, body, carry)


def rows_of(index, size):
    if isinstance(index, int):
        return pl.ds(index * size, size)
    return pl.ds(pl.multiple_of(index * size, size), size)


def causal(tile):
    key_pos = lax.broadcasted_iota(jnp.int32, (tile, tile), 0)
    query_pos = lax.broadcasted_iota(jnp.int32, (tile, tile), 1)
    return key_pos <= query_pos


def forward_kernel(tile, unrolled, table, x_ref, low_ref, full_ref, log_ref, value_t):
    tiles = x_ref.shape[0] // tile
    heads = range(2)
    cols = lambda head, kind: pl.ds(head * HEAD_COLS + kind * HEAD_DIM, HEAD_DIM)

    def turn(j, carry):
        for head in heads:
            value_t[head, j] = x_ref[rows_of(j, tile), cols(head, 2)].T
        return carry

    steps(tiles, unrolled, turn, 0)

    def query_tile(i, carry):
        rows = rows_of(i, tile)
        queries = [x_ref[rows, cols(head, 0)] * jnp.asarray(SCALE, BF) for head in heads]

        def add(j, states, masked):
            key_rows = rows_of(j, tile)
            scores = [dot_nt(x_ref[key_rows, cols(head, 1)], queries[head]) for head in heads]
            found = []
            for head in heads:
                (top, total, acc), score = states[head], scores[head]
                if masked:
                    score = jnp.where(causal(tile), score, FLOOR_SCORE)
                new_top = jnp.maximum(top, jnp.max(score, axis=0, keepdims=True))
                probs = jnp.exp(score - new_top)
                fade = jnp.exp(top - new_top)
                total = total * fade + jnp.sum(probs, axis=0, keepdims=True)
                acc = acc * fade + dot_nn(value_t[head, j], probs.astype(BF))
                found.append((new_top, total, acc))
            return tuple(found)

        state = (
            jnp.full((1, tile), FLOOR_SCORE, F32),
            jnp.zeros((1, tile), F32),
            jnp.zeros((HEAD_DIM, tile), F32),
        )
        states = steps(i, unrolled, lambda j, s: add(j, s, False), (state, state))
        for head, (top, total, acc) in enumerate(add(i, states, True)):
            result = (acc / total).T
            out_cols = pl.ds(head * HEAD_DIM, HEAD_DIM)
            low_ref[rows, out_cols] = result.astype(BF)
            full_ref[rows, out_cols] = result
            log_ref[0, pl.ds(head, 1), rows] = top + jnp.log(total)
        return carry

    steps(tiles, unrolled, query_tile, 0)


def backward_kernel(
    tile, unrolled, table, x_ref, grad_ref, full_ref, log_ref, dx_ref, sum_ref, key_t, key_acc, value_acc
):
    tiles = x_ref.shape[0] // tile
    heads = range(2)
    cols = lambda head, kind: pl.ds(head * HEAD_COLS + kind * HEAD_DIM, HEAD_DIM)

    def turn(j, carry):
        for head in heads:
            key_t[head, j] = x_ref[rows_of(j, tile), cols(head, 1)].T
        return carry

    steps(tiles, unrolled, turn, 0)
    key_acc[...] = jnp.zeros_like(key_acc)
    value_acc[...] = jnp.zeros_like(value_acc)

    def query_tile(i, query_sums):
        rows = rows_of(i, tile)
        queries, grads, deltas, logs = [], [], [], []
        for head in heads:
            out_cols = pl.ds(head * HEAD_DIM, HEAD_DIM)
            queries.append(x_ref[rows, cols(head, 0)] * jnp.asarray(SCALE, BF))
            grads.append(grad_ref[rows, out_cols])
            product = grads[head].astype(F32) * full_ref[rows, out_cols]
            deltas.append(jnp.sum(product.T, axis=0, keepdims=True))
            logs.append(log_ref[0, pl.ds(head, 1), rows])

        def add(j, accs, masked):
            key_rows = rows_of(j, tile)
            scores = [dot_nt(x_ref[key_rows, cols(head, 1)], queries[head]) for head in heads]
            grad_probs = [dot_nt(x_ref[key_rows, cols(head, 2)], grads[head]) for head in heads]
            found = []
            for head in heads:
                probs = jnp.exp(scores[head] - logs[head])
                if masked:
                    probs = jnp.where(causal(tile), probs, 0.0)
                grad_scores = (probs * (grad_probs[head] - deltas[head])).astype(BF)
                value_acc[head, key_rows, :] += dot_nn(probs.astype(BF), grads[head])
                key_acc[head, key_rows, :] += dot_nn(grad_scores, queries[head])
                found.append(accs[head] + dot_nn(key_t[head, j], grad_scores))
            return tuple(found)

        acc = jnp.zeros((HEAD_DIM, tile), F32)
        accs = steps(i, unrolled, lambda j, s: add(j, s, False), (acc, acc))
        sums = []
        for head, acc in enumerate(add(i, accs, True)):
            result = acc.T * SCALE
            dx_ref[rows, cols(head, 0)] = result.astype(BF)
            sums.append(query_sums[head] + jnp.sum(result, axis=0, keepdims=True))
        return tuple(sums)

    query_sums = steps(tiles, unrolled, query_tile, (jnp.zeros((1, HEAD_DIM), F32),) * 2)
    for head in heads:
        dx_ref[:, cols(head, 1)] = key_acc[head].astype(BF)
        dx_ref[:, cols(head, 2)] = value_acc[head].astype(BF)
        sum_ref[0, :, cols(head, 0)] = query_sums[head]
        sum_ref[0, :, cols(head, 1)] = jnp.sum(key_acc[head], axis=0, keepdims=True)
        sum_ref[0, :, cols(head, 2)] = jnp.sum(value_acc[head], axis=0, keepdims=True)


def attention_forward(projected, table, heads):
    length = projected.shape[0]
    tile = min(256, length)
    tiles, pairs = length // tile, heads // 2
    wide, narrow = 2 * HEAD_COLS, 2 * HEAD_DIM
    columns = lambda g, t: (0, g)
    return call(
        functools.partial(forward_kernel, tile, tiles <= 4),
        table,
        [projected],
        [
            shape_of((length, heads * HEAD_DIM), BF),
            shape_of((length, heads * HEAD_DIM), F32),
            shape_of((pairs, 2, length), F32),
        ],
        grid=(pairs,),
        in_specs=[pl.BlockSpec((length, wide), columns)],
        out_specs=[
            pl.BlockSpec((length, narrow), columns),
            pl.BlockSpec((length, narrow), columns),
            pl.BlockSpec((1, 2, length), lambda g, t: (g, 0, 0)),
        ],
        scratch=[pltpu.VMEM((2, tiles, HEAD_DIM, tile), BF)],
        us=15,
        name="attention_forward",
    )


def attention_backward(projected, grads, full, logs, table, heads, wait):
    length = projected.shape[0]
    tile = min(256, length)
    tiles, pairs = length // tile, heads // 2
    wide, narrow = 2 * HEAD_COLS, 2 * HEAD_DIM
    columns = lambda g, t: (0, g)
    return call(
        functools.partial(backward_kernel, tile, tiles <= 4),
        table,
        [projected, grads, full, logs],
        [shape_of((length, heads * HEAD_COLS), BF), shape_of((pairs, 1, wide), F32)],
        grid=(pairs,),
        in_specs=[
            pl.BlockSpec((length, wide), columns),
            pl.BlockSpec((length, narrow), columns),
            pl.BlockSpec((length, narrow), columns),
            pl.BlockSpec((1, 2, length), lambda g, t: (g, 0, 0)),
        ],
        out_specs=[
            pl.BlockSpec((length, wide), columns),
            pl.BlockSpec((1, 1, wide), lambda g, t: (g, 0, 0)),
        ],
        scratch=[
            pltpu.VMEM((2, tiles, HEAD_DIM, tile), BF),
            pltpu.VMEM((2, length, HEAD_DIM), F32),
            pltpu.VMEM((2, length, HEAD_DIM), F32),
        ],
        us=14,
        wait=wait,
        name="attention_backward",
    )


def norm_stats(rows):
    mean = jnp.mean(rows, axis=-1, keepdims=True)
    centred = rows - mean
    variance = jnp.mean(centred * centred, axis=-1, keepdims=True)
    inverse = lax.rsqrt(variance + EPSILON)
    return centred * inverse, inverse


def norm_back(grad, xhat, inverse, gain):
    h = grad * gain
    return inverse * (
        h - jnp.mean(h, axis=-1, keepdims=True) - xhat * jnp.mean(h * xhat, axis=-1, keepdims=True)
    )


ROOT = 0.7978845608028654
CUBE = 0.044715


def gelu_both(hidden):
    square = hidden * hidden
    bent = jnp.tanh(ROOT * hidden * (1.0 + CUBE * square))
    half = 0.5 * (1.0 + bent)
    slope = half + 0.5 * hidden * (1.0 - bent * bent) * ROOT * (1.0 + 3.0 * CUBE * square)
    return hidden * half, slope


def project_kernel(shards, table, gain, shift, bias, weight, *refs):
    blocks, (normed, projected, kept) = refs[:shards], refs[shards:]
    span = blocks[0].shape[0]
    for r in range(shards):
        normed[rows_of(table[r], span), :] = blocks[r][...]
    length = span * shards
    chunk = min(256, length)

    def some_rows(i, carry):
        rows = rows_of(i, chunk)
        xhat, _ = norm_stats(normed[rows, :].astype(F32))
        kept[rows, :] = xhat.astype(BF)
        normed[rows, :] = (xhat * gain[...] + shift[...]).astype(BF)
        projected[rows, :] = (dot_nn(normed[rows, :], weight[...]) + bias[...]).astype(BF)
        return carry

    lax.fori_loop(0, length // chunk, some_rows, 0)


def unproject_kernel(shards, batches, heads, table, grad, weight, xhat, norms, cots, head_sums, *refs):
    others, blocks, (sums, rows, vectors) = refs[:shards], refs[shards : 2 * shards], refs[2 * shards :]
    length = rows.shape[0]
    span, chunk = length // shards, min(256, length)
    sums[...] = jnp.zeros_like(sums)

    def some_rows(i, carry):
        at = rows_of(i, chunk)
        share = dot_nt(grad[at, :], weight[...])
        rows[at, :] = share.astype(BF)
        sums[0:1, :] += jnp.sum(share * xhat[at, :].astype(F32), axis=0, keepdims=True)
        sums[1:2, :] += jnp.sum(share, axis=0, keepdims=True)
        return carry

    lax.fori_loop(0, length // chunk, some_rows, 0)
    width = sums.shape[1]
    part = width // shards
    for s in range(shards):
        for i, source in enumerate([sums[0:1], sums[1:2], norms[0:1], norms[1:2], norms[2:3], cots[...]]):
            vectors[s, :, i * part : (i + 1) * part] = source[:, s * part : (s + 1) * part]
        vectors[s, :, 6 * part :] = jnp.zeros((1, width - 6 * part), F32)
    for s in range(shards):

        @pl.when(table[0] == s)
        def _(s=s):
            for first, shard, to, size in head_copies(s, shards, heads, width):
                pair, at = first
                vectors[shard, :, 6 * part + to : 6 * part + to + size] = head_sums[pair, :, at : at + size]

    last = others[0].shape[0] - 1
    for r in range(shards):
        blocks[r][:span, :] = rows[rows_of(table[r], span), :]
        blocks[r][span : span + last, :] = others[r][:last, :]
        blocks[r][span + last :, :] = vectors[table[r]].astype(BF)


def head_copies(shard, shards, heads, width):
    found, piece = [], 2 * width // shards
    for head in range(heads):
        number = shard * heads + head
        if (number + 1) * HEAD_DIM > width:
            continue
        for kind, base in ((0, 0), (2, width)):
            at, end = base + number * HEAD_DIM, base + (number + 1) * HEAD_DIM
            first = head % 2 * HEAD_COLS + kind * HEAD_DIM
            while at < end:
                size = min(end, (at // piece + 1) * piece) - at
                found.append(((head // 2, first), at // piece, at % piece, size))
                at, first = at + size, first + size
    return found


def mix_kernel(shards, table, tokens, weight, bias, gain, shift, heads, attended, mixed, normed, spread):
    cols, width = heads.shape[2], attended.shape[1]
    for s in range(shards):
        spread[:, s * cols : (s + 1) * cols] = heads[s]
    attended[...] = spread[:, :width]
    mixed[...] = tokens[...].astype(F32) + dot_nn(attended[...], weight[...]) + bias[...]
    xhat, _ = norm_stats(mixed[...])
    normed[...] = (xhat * gain[...] + shift[...]).astype(BF)


def unmix_kernel(shards, table, first, second, third, mixed, cotangent, weight, gain, *refs):
    grad_mixed, low, sums, pieces, spread = refs
    cols, (span, width) = pieces.shape[2], low.shape
    grad = first[...].astype(F32) + second[...].astype(F32) + third[...].astype(F32)
    xhat, inverse = norm_stats(mixed[...])
    full = cotangent[...].astype(F32) + norm_back(grad, xhat, inverse, gain[...])
    grad_mixed[...] = full
    low[...] = full.astype(BF)
    sums[0:1, :] = jnp.sum(grad * xhat, axis=0, keepdims=True)
    sums[1:2, :] = jnp.sum(grad, axis=0, keepdims=True)
    sums[2:3, :] = jnp.sum(full, axis=0, keepdims=True)
    spread[:, width:] = jnp.zeros_like(spread[:, width:])
    spread[:, :width] = dot_nt(low[...], weight[...]).astype(BF)
    for s in range(shards):
        pieces[s] = spread[:, s * cols : (s + 1) * cols]


def mlp_kernel(shards, group, table, fc, bias, out, *refs):
    blocks, cotangents, refs = refs[:shards], refs[shards : 2 * shards], refs[2 * shards :]
    act, low, sums, results = refs[:4]
    shares, refs = refs[4 : 4 + shards], refs[4 + shards :]
    fc_in, out_in, normed, cots, act_here, low_here, results_here, shares_here, came, left = refs
    span = blocks[0].shape[0]
    pairs = [(fc, fc_in), (out, out_in)]
    for r in range(shards):
        pairs += [(blocks[r], normed.at[r]), (cotangents[r], cots.at[r])]
    copies = [pltpu.make_async_copy(a, b, came.at[i]) for i, (a, b) in enumerate(pairs)]
    for i in [0, *range(2, 2 + 2 * group), 1, *range(2 + 2 * group, len(copies))]:
        copies[i].start()
    copies[0].wait()
    sums[...] = jnp.zeros_like(sums)
    sent = []

    def send(source, target):
        copy = pltpu.make_async_copy(source, target, left.at[len(sent)])
        copy.start()
        sent.append(copy)

    for first in range(0, shards, group):
        places = range(first, first + group)
        rows = pl.ds(first * span, group * span)
        some = pl.ds(first, group)
        for r in places:
            copies[2 + 2 * r].wait()
            copies[3 + 2 * r].wait()
        flat = lambda ref: ref[some].reshape(group * span, ref.shape[2])
        hidden = dot_nn(flat(normed), fc_in[...]) + bias[...]
        activated, slope = gelu_both(hidden)
        act_here[rows, :] = activated.astype(BF)
        if not first:
            copies[1].wait()
        grad = dot_nt(flat(cots), out_in[...]) * slope
        sums[...] += jnp.sum(grad, axis=0, keepdims=True)
        low_here[rows, :] = grad.astype(BF)
        share = dot_nt(low_here[rows, :], fc_in[...]).astype(BF)
        shares_here[some] = share.reshape(group, span, share.shape[1])
        for r in places:
            send(shares_here.at[r], shares[r])
        send(act_here.at[rows, :], act.at[rows, :])
        send(low_here.at[rows, :], low.at[rows, :])
        result = dot_nn(act_here[rows, :], out_in[...]).astype(BF)
        results_here[some] = result.reshape(group, span, result.shape[1])
        send(results_here.at[some], results.at[some])
    for copy in sent:
        copy.wait()


def mlp_part(blocks, cotangents, fc, bias, out, table):
    shards = len(blocks)
    span, width = blocks[0].shape
    rows, units = shards * span, fc.shape[1]
    if rows > MOST_ROWS:
        half = shards // 2
        halves = [mlp_part(blocks[i:][:half], cotangents[i:][:half], fc, bias, out, table) for i in (0, half)]
        first, second = halves
        results = jnp.concatenate([first[3], second[3]])
        return first[0] + second[0], first[1] + second[1], first[2] + second[2], results, first[4] + second[4]
    group = min(shards, max(1, 512 // span))
    rows_at = lambda cols: pl.BlockSpec((group * span, cols), lambda g, t: (g, 0))
    anywhere = pl.BlockSpec(memory_space=pl.ANY)
    stack = pltpu.VMEM((shards, span, width), BF)
    got = call(
        functools.partial(mlp_kernel, shards, group),
        table,
        [fc, bias, out, *blocks, *cotangents],
        [shape_of((rows, units), BF)] * 2
        + [shape_of((1, units), F32), shape_of((shards, span, width), BF)]
        + [shape_of((span, width), BF)] * shards,
        grid=(1,),
        in_specs=[anywhere, whole(1, units)] + [anywhere] * (1 + 2 * shards),
        out_specs=[anywhere, anywhere, whole(1, units)] + [anywhere] * (1 + shards),
        scratch=[
            pltpu.VMEM(fc.shape, BF),
            pltpu.VMEM(out.shape, BF),
            stack,
            stack,
            pltpu.VMEM((rows, units), BF),
            pltpu.VMEM((rows, units), BF),
            stack,
            stack,
            pltpu.SemaphoreType.DMA((2 + 2 * shards,)),
            pltpu.SemaphoreType.DMA((shards + 3 * (shards // group),)),
        ],
        us=18,
        name="mlp",
    )
    return got[:1], got[1:2], got[2], got[3], got[4:]


def take_rows(pieces):
    found = []
    while pieces and sum(v.shape[0] for v in found) < MOST_ROWS:
        found.append(pieces.pop(0))
    return found


def weight_kernel(shards, batches, row_blocks, count, table, *refs):
    lefts, rights, refs = refs[:count], refs[count:-batches], refs[-batches:]
    left = jnp.concatenate([v[...] for v in lefts])
    right = jnp.concatenate([v[...] for v in rights])
    product = dot_tn(left, right).astype(BF)
    cols = product.shape[1] // batches
    size = product.shape[0] // row_blocks
    for member in range(batches):

        @pl.when(table[shards] == member)
        def _(member=member):
            for apart in range(batches):
                first = (member ^ apart) * cols
                for s in range(row_blocks):
                    refs[apart][s] = product[s * size : (s + 1) * size, first : first + cols]


def weight_shares(lefts, rights, table, shards, batches, row_blocks, name, wait=()):
    rows, cols = lefts[0].shape[1], rights[0].shape[1]
    dims = (row_blocks, rows // row_blocks, cols // batches)
    if sum(v.shape[0] for v in lefts) > MOST_ROWS:
        cut_rows = lambda vs: [v[i : i + MOST_ROWS] for v in vs for i in range(0, v.shape[0], MOST_ROWS)]
        total, lefts, rights = None, cut_rows(lefts), cut_rows(rights)
        while lefts:
            some = [take_rows(lefts), take_rows(rights)]
            found = weight_shares(*some, table, shards, batches, row_blocks, name, wait)
            total = found if total is None else [add(a, b) for a, b in zip(total, found)]
        return total
    return call(
        functools.partial(weight_kernel, shards, batches, row_blocks, len(lefts)),
        table,
        [*lefts, *rights],
        [shape_of(dims, BF)] * batches,
        us=9,
        wait=wait,
        name=name,
    )


def pack_kernel(shards, batches, ranges, table, weight, *refs):
    out, rows = refs[-1], weight.shape[0]
    for extra in refs[:-1]:
        count = (out.shape[1] - rows) // extra.shape[0]
        size = extra.shape[1] // count
        for shard in range(shards):
            for i in range(extra.shape[0]):
                for j in range(count):
                    at = rows + i * count + j
                    out[shard, at : at + 1, :size] = extra[i : i + 1, j * size : (j + 1) * size]
    for member in range(batches):

        @pl.when(table[shards] == member)
        def _(member=member):
            for shard in range(shards):
                at = 0
                for first, size in ranges(shard, member):
                    if first is None:
                        out[shard, :rows, at : at + size] = jnp.zeros((rows, size), BF)
                    else:
                        out[shard, :rows, at : at + size] = weight[:, first : first + size]
                    at += size


def pack(weight, table, shards, batches, cols, ranges, extra=(), wait=()):
    rows = weight.shape[0] + sum(v.shape[0] * -(-v.shape[1] // cols) for v in extra)
    return call(
        functools.partial(pack_kernel, shards, batches, ranges),
        table,
        [weight, *extra],
        [shape_of((shards, rows, cols), BF)],
        us=3.5,
        wait=wait,
        name="pack",
    )[0]


def assemble_kernel(shards, batches, rows, pieces, table, *refs):
    out = refs[-1]
    blocks, _, cols = refs[0].shape
    for member in range(batches):

        @pl.when(table[shards] == member)
        def _(member=member):
            for apart in range(batches):
                at = (member ^ apart) * cols
                for i in range(pieces * blocks):
                    source = refs[apart * pieces + i // blocks][i % blocks, :rows, :]
                    out[i * rows : (i + 1) * rows, at : at + cols] = source


def assemble(parts, table, shards, rows, pieces=1, wait=()):
    blocks, _, cols = parts[0].shape
    batches = len(parts) // pieces
    return call(
        functools.partial(assemble_kernel, shards, batches, rows, pieces),
        table,
        parts,
        [shape_of((pieces * blocks * rows, batches * cols), BF)],
        us=5,
        wait=wait,
        name="assemble",
    )[0]


def join_kernel(table, source, out):
    out[...] = source[...]


def join(source, table, wait):
    shards, rows, cols = source.shape
    return call(
        join_kernel,
        table,
        [source],
        [shape_of(source.shape, BF)],
        grid=(shards,),
        in_specs=[pl.BlockSpec((1, rows, cols), lambda g, t: (g, 0, 0))],
        out_specs=[pl.BlockSpec((1, rows, cols), lambda g, t: (t[g], 0, 0))],
        us=4,
        wait=wait,
        name="join",
    )[0]


def proj_grad_kernel(shards, batches, table, *refs):
    lefts, rights, refs = refs[:batches], refs[batches : 2 * batches], refs[2 * batches :]
    blocks, quarter, product = refs[:-2], refs[-2], refs[-1]
    span, cols = rights[0].shape[0], quarter.shape[1]
    for member in range(batches):

        @pl.when(table[shards] == member)
        def _(member=member):
            for i in range(batches):
                quarter[i * span : (i + 1) * span, :] = rights[i][:, member * cols : (member + 1) * cols]

    left = jnp.concatenate([v[...] for v in lefts])
    result = dot_tn(left, quarter[...]).astype(BF)
    rows = result.shape[0] // shards
    piece = -(-rows // batches)
    product[...] = jnp.zeros_like(product)
    for s in range(shards):
        for i in range(batches):
            size = min(piece, rows - i * piece)
            first = s * rows + i * piece
            product[s, :size, i * cols : (i + 1) * cols] = result[first : first + size, :]
    for r in range(shards):
        blocks[r][...] = product[table[r]]


def proj_grad(lefts, rights, table, shards, span):
    batches, rows = len(lefts), lefts[0].shape[1]
    width = rights[0].shape[1]
    piece = -(-(rows // shards) // batches)
    dims = (piece + 1 + -(span + piece + 1) % 8, width)
    return call(
        functools.partial(proj_grad_kernel, shards, batches),
        table,
        [*lefts, *rights],
        [shape_of(dims, BF)] * shards,
        scratch=[
            pltpu.VMEM((batches * lefts[0].shape[0], width // batches), BF),
            pltpu.VMEM((shards, *dims), BF),
        ],
        us=6,
        name="proj_grad",
    )


def copy_kernel(shards, batches, copies, table, source, out):
    for member in range(batches):

        @pl.when(table[shards] == member)
        def _(member=member):
            for block, first, to_block, to, size in copies(member):
                piece = source[block, :, first : first + size].astype(out.dtype)
                out[to_block, :, to : to + size] = piece


def copy_columns(source, table, shards, batches, dims, kind, copies):
    return call(
        functools.partial(copy_kernel, shards, batches, copies),
        table,
        [source],
        [shape_of(dims, kind)],
        us=4,
        name="copy_columns",
    )[0]


def cut(value):
    rows = value.shape[-2]
    if rows % 8:
        return value
    groups = max(g for g in range(1, 33) if rows // 8 % g == 0)
    return value.reshape(*value.shape[:-2], rows // 8 // groups, groups, 8, value.shape[-1])


def permute(value, axis, pairs):
    return lax.ppermute(cut(value), axis, pairs).reshape(value.shape)


def gate_kernel(count, total, *refs):
    outs = refs[-total:]
    for i in range(count):
        outs[i][...] = (refs[i][...].astype(F32) + refs[total + i][...].astype(F32)).astype(BF)


def gate(values, *others, parts=()):
    values, others, parts = list(values), jax.tree.leaves(others), list(parts)
    if not values:
        return []
    count, total = len(parts), len(values)
    anywhere = pl.BlockSpec(memory_space=pl.ANY)
    blocks = [pl.BlockSpec(memory_space=pltpu.VMEM)] * count
    return pl.pallas_call(
        functools.partial(gate_kernel, count, total),
        in_specs=blocks + [anywhere] * (total - count) + blocks + [anywhere] * len(others),
        out_specs=blocks + [anywhere] * (total - count),
        out_shape=[shape_of(v.shape, v.dtype) for v in values],
        input_output_aliases={i: i for i in range(count, total)},
        name="gate",
    )(*values, *parts, *others)


def after(value, *others):
    return gate([value], *others)[0]


class Rounds:
    def __init__(self):
        self.chains, self.mark, self.waits = [], None, []

    def add(self, chain):
        self.chains.append([chain, None])

    def end(self, start, parts=()):
        pending, alive = [], []
        for chain, gated in self.chains:
            try:
                pending.append(list(chain.send(gated)))
                alive.append(chain)
            except StopIteration:
                pass
        values = list(start())
        out = gate(values + [v for p in pending for v in p], self.waits, parts=parts)
        self.waits = []
        at, self.chains = len(values), []
        for chain, p in zip(alive, pending):
            self.chains.append([chain, out[at : at + len(p)]])
            at += len(p)
        if out:
            self.mark = out[0]
        return out[: len(values)]

    def finish(self):
        while self.chains:
            self.end(lambda: [])


class Ring:
    def __init__(self, size, rounds):
        self.size, self.rounds = size, rounds
        self.order = list(range(0, size, 2)) + list(range(size - 1, 0, -2))

    def shift(self, value, by):
        pairs = [(self.order[i], self.order[(i + by) % self.size]) for i in range(self.size)]
        return permute(value, "seq", pairs)

    def both(self, right, left):
        return [self.shift(v, 1) for v in right] + [self.shift(v, -1) for v in left]

    def gather(self, value):
        got = [value] * self.size
        right = left = value
        for far in range(1, self.size // 2 + 1):
            left = left if far < self.size - far else []
            came = self.rounds.end(lambda: self.both(right, left))
            right, left = came[: len(value)], came[len(value) :]
            got[self.size - far] = right
            if left:
                got[far] = left
        return got

    def scatter_sum(self, parts):
        size = self.size
        right, left = [parts[size // 2]], []
        for far in range(size // 2 - 1, -1, -1):
            adds = [] if not far else [parts[far]] + [parts[size - far]] * len(left)
            right, *left = self.rounds.end(lambda: self.both(right, left), adds)
            right = [right]
            if far and not left:
                left = [parts[size - far]]
        return right[0], left[0], parts[0]


def add(a, b):
    return (a.astype(F32) + b.astype(F32)).astype(BF)


def swap_blocks(value, axis="seq"):
    return lax.all_to_all(cut(value), axis, 0, 0, tiled=True).reshape(value.shape)


def over_batch(value, batches, apart):
    return permute(value, "batch", [(b, b ^ apart) for b in range(batches)])


def batch_gather_steps(value, batches):
    parts, bit = {0: value}, batches // 2
    while bit:
        came = {apart ^ bit: over_batch(part, batches, bit) for apart, part in parts.items()}
        parts.update(zip(came, (yield list(came.values()))))
        bit //= 2
    return [parts[apart] for apart in range(batches)]


def per_device(
    shards,
    batches,
    tokens,
    ln1_gain,
    ln1_bias,
    qkv_weight,
    qv_bias,
    proj_weight,
    proj_bias,
    ln2_gain,
    ln2_bias,
    fc_weight,
    fc_bias,
    out_weight,
    out_bias,
    cotangent,
):
    _, span, width = tokens.shape
    head_count = width // HEAD_DIM
    heads = -(-head_count // shards)
    heads += heads % 2
    padded = heads * shards
    length = span * shards
    units = fc_bias.shape[0]
    part = width // shards
    me, member = lax.axis_index("seq"), lax.axis_index("batch")
    rounds = Rounds()
    ring = Ring(shards, rounds)
    place = jnp.where(me % 2 == 0, me // 2, shards - 1 - me // 2)
    place = (place + jnp.arange(shards, dtype=jnp.int32)) % shards
    order = jnp.where(place < shards // 2, 2 * place, 2 * shards - 2 * place - 1)
    table = jnp.concatenate([order, member[None]]).astype(jnp.int32)
    row = lambda v: v.reshape(1, -1).astype(F32)

    slice_cols = heads * HEAD_COLS
    quarter = slice_cols // batches
    fc_quarter = units // batches

    def head_ranges(shard, b):
        found = []
        for col in range(shard * slice_cols + b * quarter, shard * slice_cols + (b + 1) * quarter):
            head, kind, at = col // HEAD_COLS, col % HEAD_COLS // HEAD_DIM, col % HEAD_DIM
            first = kind * width + head * HEAD_DIM + at if head < head_count else None
            if found and first is not None and found[-1][0] is not None and first == sum(found[-1]):
                found[-1] = (found[-1][0], found[-1][1] + 1)
            elif found and first is None and found[-1][0] is None:
                found[-1] = (None, found[-1][1] + 1)
            else:
                found.append((first, 1))
        return found

    def fc_ranges(shard, b):
        return [(shard * units + b * fc_quarter, fc_quarter)]

    own_tokens, own_cot = tokens[0], cotangent[0]
    far = shards // 2
    out_cols = width // batches
    out_cols = width // batches
    proj_part = lax.dynamic_slice_in_dim(proj_weight, member * out_cols, out_cols, 1)
    small = jnp.stack(
        [ln1_gain, ln1_bias, qv_bias[:part], qv_bias[part:], proj_bias, ln2_gain, ln2_bias, out_bias]
    )
    packed = pack(qkv_weight, table, shards, batches, quarter, head_ranges, [small])
    held = {}

    def first_weights():
        (got,) = yield [swap_blocks(packed)]
        held["small"] = got[:, part:, : part // ((got.shape[1] - part) // 8)]
        parts = yield from batch_gather_steps(got, batches)
        held["qkv"] = assemble(parts, table, shards, part)
        rounds.waits.append(held["qkv"])

    far = shards // 2

    def fc_weights():
        yield []
        got = pack(fc_weight, table, shards, batches, fc_quarter, fc_ranges, wait=[rounds.mark])
        (got,) = yield [got]
        for _ in range(far - 2):
            yield []
        (got,) = yield [swap_blocks(after(got, rounds.mark))]
        while "normed_two" not in held:
            yield []
        got = after(got, rounds.mark)
        came = over_batch(got, batches, batches // 2)
        yield []
        parts = {0: got, batches // 2: (yield [came])[0]}
        bit = batches // 4
        while bit:
            came = {apart ^ bit: over_batch(p, batches, bit) for apart, p in parts.items()}
            parts.update(zip(came, (yield list(came.values()))))
            bit //= 2
        parts = [parts[apart] for apart in range(batches)]
        held["fc"] = (yield [assemble(parts, table, shards, part)])[0]

    def proj_weights():
        got = lax.all_gather(cut(proj_part), "seq", axis=0, tiled=True)
        for _ in range(far):
            yield []
        got = after(got.reshape(shards, part, out_cols), rounds.mark)
        got = [got[:far], got[far:]]
        came = [over_batch(v, batches, batches // 2) for v in got]
        came[0] = (yield came[:1])[0]
        came[1] = (yield came[1:])[0]
        parts = {0: got, batches // 2: came}
        bit = batches // 4
        while bit:
            parts.update(
                {apart ^ bit: [over_batch(v, batches, bit) for v in p] for apart, p in parts.items()}
            )
            bit //= 2
        parts = [v for apart in range(batches) for v in parts[apart]]
        held["w_proj"] = (yield [assemble(parts, table, shards, part, 2)])[0]

    rounds.add(first_weights())
    rounds.add(fc_weights())
    rounds.add(proj_weights())
    token_blocks = [block for (block,) in ring.gather([own_tokens])]
    while "qkv" not in held:
        rounds.end(lambda: [])
    w_qkv = held["qkv"]
    small = held["small"].reshape(shards, -1)
    gain_one = row(small[:, :part])
    shift_one = row(small[:, part : 2 * part])
    bias_qv = small[:, 2 * part : 4 * part].reshape(2 * width)
    b_proj = row(small[:, 4 * part : 5 * part])
    gain_two = row(small[:, 5 * part : 6 * part])
    shift_two = row(small[:, 6 * part : 7 * part])
    b_out = row(small[:, 7 * part : 8 * part])
    bias_row = jnp.concatenate([bias_qv[:width], jnp.zeros((width,), BF), bias_qv[width:]])
    bias_heads = jnp.pad(
        bias_row.reshape(3, head_count, HEAD_DIM), ((0, 0), (0, padded - head_count), (0, 0))
    )
    bias_heads = jnp.swapaxes(bias_heads, 0, 1).reshape(1, padded * HEAD_COLS)
    bias_slice = lax.dynamic_slice_in_dim(bias_heads, me * slice_cols, slice_cols, 1).astype(F32)
    cot_blocks = [own_cot] * shards

    def cotangents():
        right = left = after(own_cot, rounds.mark)
        for step in range(1, far + 1):
            came = yield ring.both([right], [left] if step < shards - step else [])
            right = cot_blocks[shards - step] = came[0]
            if step < shards - step:
                left = cot_blocks[step] = came[1]

    rounds.add(cotangents())

    def project():
        return call(
            functools.partial(project_kernel, shards),
            table,
            [gain_one, shift_one, bias_slice, w_qkv, *token_blocks],
            [
                shape_of((length, width), BF),
                shape_of((length, slice_cols), BF),
                shape_of((length, width), BF),
            ],
            us=11,
            name="project",
        )

    normed_one, projected, xhat_one = rounds.end(project)
    attended_heads, attended_full, log_total = rounds.end(lambda: attention_forward(projected, table, heads))
    (attended_heads,) = rounds.end(
        lambda: [
            swap_blocks(
                attended_heads.reshape(shards, span, heads * HEAD_DIM)
            )
        ]
    )
    while "w_proj" not in held:
        rounds.end(lambda: [])
    w_proj = held["w_proj"]
    attended, mixed, normed_two = call(
        functools.partial(mix_kernel, shards),
        table,
        [own_tokens, w_proj, b_proj, gain_two, shift_two, attended_heads],
        [shape_of((span, width), BF), shape_of((span, width), F32), shape_of((span, width), BF)],
        scratch=[pltpu.VMEM((span, padded * HEAD_DIM), BF)],
        us=6,
        name="mix",
    )

    held["normed_two"] = normed_two
    gathered = {}

    def batch_rows(value, name, flag):
        while flag not in held:
            yield []
        value = after(value, rounds.mark)
        gathered[name] = yield from batch_gather_steps(value, batches)

    rounds.add(batch_rows(attended, "attended", "mlp"))
    normed_blocks = [block for (block,) in ring.gather([normed_two])]
    while "fc" not in held:
        rounds.end(lambda: [])
    w_fc = held["fc"]
    activated, hidden_low, fc_sums, out_rows, g_two = mlp_part(
        normed_blocks, cot_blocks, w_fc, row(fc_bias), out_weight, table
    )

    shares = functools.partial(weight_shares, table=table, shards=shards, batches=batches)

    def near_sums(found):
        came = yield [over_batch(found[apart ^ 1], batches, 1) for apart in range(0, batches, 2)]
        return [add(found[2 * i], c) for i, c in enumerate(came)]

    def far_sum(kept):
        came = yield [over_batch(kept[1], batches, 2)]
        return add(kept[0], came[0])

    def fc_gradient():
        yield []
        yield []
        found = yield shares(
            normed_blocks, hidden_low, row_blocks=shards, name="fc_grad", wait=[rounds.mark]
        )
        kept = yield from near_sums(found)
        yield []
        yield []
        came = over_batch(after(kept[1], rounds.mark), batches, 2)
        share = add(kept[0], *(yield [came]))
        share = swap_blocks(share)
        yield []
        (share,) = yield [share]
        for _ in range(far - 1):
            yield []
        held["fc_grad"] = (yield [swap_blocks(after(share, rounds.mark), "batch")])[0]

    def out_gradient():
        yield []
        yield []
        yield []
        found = yield shares(activated, cot_blocks, row_blocks=1, name="out_grad", wait=[rounds.mark])
        yield []
        kept = yield from near_sums(found)
        while "unproject" not in held:
            yield []
        came = over_batch(after(kept[1], rounds.mark), batches, 2)
        yield []
        held["out_grad"] = add(kept[0], *(yield [came]))

    def out_result():
        yield []
        (total,) = yield [join(out_rows, table, [rounds.mark])]
        for _ in range(far - 2):
            yield []
        total = cut(after(total, rounds.mark))
        held["out"] = lax.psum_scatter(total, "seq", scatter_dimension=0, tiled=True)

    held["mlp"] = True
    rounds.add(out_result())
    rounds.add(fc_gradient())
    rounds.add(out_gradient())
    g_two = ring.scatter_sum(g_two)

    def unmix():
        return call(
            functools.partial(unmix_kernel, shards),
            table,
            [*g_two, mixed, own_cot, w_proj, gain_two],
            [
                shape_of((span, width), F32),
                shape_of((span, width), BF),
                shape_of((3, width), F32),
                shape_of((shards, span, heads * HEAD_DIM), BF),
            ],
            scratch=[pltpu.VMEM((span, padded * HEAD_DIM), BF)],
            us=7,
            name="unmix",
        )

    grad_mixed, mixed_low, norm_sums, grad_messages = rounds.end(unmix)

    rounds.add(batch_rows(mixed_low, "mixed_low", "mlp"))
    (grad_heads,) = rounds.end(lambda: [swap_blocks(grad_messages)])
    held["grad_heads"] = grad_heads
    grad_projected, column_sums = rounds.end(
        lambda: attention_backward(
            projected, grad_heads.reshape(length, -1), attended_full, log_total, table, heads, []
        )
    )
    held["qkv_found"] = shares([normed_one], [grad_projected], row_blocks=shards, name="qkv_grad")
    qkv_near = rounds.end(
        lambda: [over_batch(held["qkv_found"][apart ^ 1], batches, 1) for apart in range(0, batches, 2)]
    )
    proj_blocks = proj_grad(gathered["attended"], gathered["mixed_low"], table, shards, span)
    share_cols = 3 * width // batches

    def overlaps(source, target):
        found = []
        for shard in range(shards):
            at = 0
            for first, size in head_ranges(shard, source):
                if first is not None:
                    low = max(first, target * share_cols)
                    high = min(first + size, (target + 1) * share_cols)
                    if low < high:
                        found.append((shard, at + low - first, low - target * share_cols, high - low))
                at += size
        return found

    most = max(sum(o[3] for o in overlaps(q, b)) for q in range(batches) for b in range(batches))
    most = -(-most // 128) * 128

    def outgoing(b):
        copies = []
        for target in range(batches):
            at = 0
            for shard, first, _, size in overlaps(b, target):
                copies.append((shard, first, target, at, size))
                at += size
        return copies

    def incoming(b):
        copies = []
        for source in range(batches):
            at = 0
            for _, _, to, size in overlaps(source, b):
                copies.append((source, at, 0, to, size))
                at += size
        return copies

    def qkv_gradient():
        kept = [add(held["qkv_found"][2 * i], c) for i, c in enumerate(qkv_near)]
        share = yield from far_sum(kept)
        share = swap_blocks(share)
        yield []
        (share,) = yield [share]
        share = copy_columns(share, table, shards, batches, (batches, part, most), BF, outgoing)
        (share,) = yield [swap_blocks(share, "batch")]
        held["qkv_grad"] = copy_columns(share, table, shards, batches, (1, part, share_cols), F32, incoming)[0]

    rounds.add(qkv_gradient())

    cot_sums = jnp.sum(own_cot.astype(F32), axis=0, keepdims=True)

    def unproject():
        return call(
            functools.partial(unproject_kernel, shards, batches, heads),
            table,
            [grad_projected, w_qkv, xhat_one, norm_sums, cot_sums, column_sums, *proj_blocks],
            [shape_of((span + proj_blocks[0].shape[0], width), BF)] * shards,
            scratch=[
                pltpu.VMEM((2, width), F32),
                pltpu.VMEM((length, width), BF),
                pltpu.VMEM((shards, 1, width), F32),
            ],
            us=9,
            name="unproject",
        )

    g_one = rounds.end(unproject)
    held["unproject"] = True
    rounds.waits.append(held["out"])
    total = sum(term.astype(F32) for term in ring.scatter_sum(g_one))
    g_one, pieces = total[:span], -(-part // batches)
    proj_share = [total[span : span + pieces, b * out_cols : (b + 1) * out_cols] for b in range(batches)]
    proj_share = jnp.concatenate(proj_share)[:part]
    xhat, inverse = norm_stats(own_tokens.astype(F32))
    block_out = (mixed + b_out + held["out"].reshape(span, width).astype(F32)).astype(BF)
    input_grad = (grad_mixed + norm_back(g_one, xhat, inverse, gain_one)).astype(BF)

    def vector_gradients():
        sums = jnp.concatenate([total[-1:, : 8 * part], fc_sums], axis=1)
        came = yield [
            lax.ppermute(sums, "batch", [(b, b ^ apart) for b in range(batches)])
            for apart in range(1, batches)
        ]
        sums = sums + sum(came)
        held["sums"] = sums[0]

    rounds.add(vector_gradients())
    rounds.finish()

    runs = shards // batches

    def fc_copies(b):
        return [
            (q * runs + run, 0, 0, (run * batches + q) * fc_quarter, fc_quarter)
            for q in range(batches)
            for run in range(runs)
        ]

    fc_share = held["fc_grad"]
    fc_share = copy_columns(fc_share, table, shards, batches, (1, part, runs * units), F32, fc_copies)[0]
    sums = held["sums"]
    vectors = [sums[i * part : (i + 1) * part] for i in range(6)]
    return (
        block_out[None],
        input_grad[None],
        vectors[0],
        vectors[1],
        held["qkv_grad"],
        sums[6 * part : 8 * part],
        proj_share,
        vectors[4],
        vectors[2],
        vectors[3],
        fc_share,
        sums[8 * part : 8 * part + units],
        held["out_grad"][0].astype(F32),
        vectors[5],
    )


def solution(mesh):
    rows = P("batch", "seq", None)
    matrix, vector = P("seq", None), P("seq")
    shared = P("seq", "batch")
    return jax.shard_map(
        functools.partial(per_device, mesh.shape["seq"], mesh.shape["batch"]),
        mesh=mesh,
        in_specs=(
            rows, vector, vector, matrix, vector, matrix, vector,
            vector, vector, matrix, vector, matrix, vector, rows,
        ),
        out_specs=(
            rows, rows, vector, vector, shared, vector, shared,
            vector, vector, vector, shared, vector, shared, vector,
        ),
        check_vma=False,
    )
```
